128 devices in a mesh: along: 8 (over y, core), depth: 16 (over x, z).
Axes of the slice: x: 4, y: 4, z: 4, core: 2. Of those that a mesh axis runs over, the one named last changes fastest.
Arguments:
- right_side: float32 [3, 20, 8, 16, 1024], P(None, None, 'along', 'depth'), may hold values from -6 to 6
- shear_modulus: float32 [8, 16, 1024], P('along', 'depth'), may hold values from 0.5 to 2
- lame_lambda: float32 [8, 16, 1024], P('along', 'depth'), may hold values from 0.5 to 2
- stiff_shear: float32 [60, 60], replicated, may hold values from -0.1 to 1.8, as said below
- stiff_lame: float32 [60, 60], replicated, may hold values from -0.1 to 1.8, as said below
- face_interp: float32 [12, 4, 20], replicated, may hold values from -0.875 to 0.875
- neighbours: int32 [8, 16, 4096], P('along', 'depth'), may hold values from 0 to 4607, as said below
- fault_count: int32 [8, 16], P('along', 'depth'), may hold values from 0 to 2048, as said below
- fault_owner: int32 [8, 16, 2048], P('along', 'depth'), may hold values from 0 to 127, as said below
- fault_slot: int32 [8, 16, 2048], P('along', 'depth'), may hold values from 0 to 511, as said below
- fault_face: int32 [8, 16, 2048], P('along', 'depth'), may hold values from 0 to 4095, as said below
- normal_stress: float32 [12, 65536], P(None, ('along', 'depth')), may hold values from 1 to 10
- friction: float32 [12, 65536], P(None, ('along', 'depth')), may hold values from 0.3 to 1
- state_factor: float32 [12, 65536], P(None, ('along', 'depth')), may hold values from 0.5 to 8
- shear_load: float32 [2, 12, 65536], P(None, None, ('along', 'depth')), may hold values from -6 to 6
Outputs:
- displacement: float32 [3, 20, 8, 16, 1024], P(None, None, 'along', 'depth')
- residual: float32 [3, 20, 8, 16, 1024], P(None, None, 'along', 'depth')
- slip_rate: float32 [12, 65536], P(None, ('along', 'depth'))
The draws below stay inside these ranges and needn't reach their ends.
Inputs may be any that keep to these rules, and one draw needn't show every extreme that they name: `neighbours`: slots below 4096 other than 3072 + e for e < 512 are paired: each names its partner and its partner names it; slot 3072 + e for e < 512 names 4096 + e. `fault_count`: the counts of all partitions add up to 65536. `fault_owner`: owners are flat device indices along * 16 + depth; entries at or past a partition's count are zero. Every grid point of every owner is named by exactly one live fault face; among the live faces of one partition no owner is named more than 16 times, and in every draw some partition names every owner exactly 16 times. `fault_slot`: entries at or past a partition's count are zero. `fault_face`: the slots of one partition are distinct. `stiff_shear`: Symmetric. `stiff_lame`: Symmetric.
All inputs are finite; a program needn't handle non-finite values.
Results may differ from the reference program's by a relative error of at most 0.0003.
Values sent between devices are 32-bit elements; how exact they have to be, the bound alone decides.
A program may use at most 128 MiB of HBM per device.

```python
import math
import jax
import jax.numpy as jnp
from jax import lax

NODES = 20
QPTS = 12
ELEMS = 1024
FMAX = 2048
ITERS = 4
NEWTON = 6
SIDE = 128
PA = 8
PD = 16
FACE_OWN = 512
GRID = 65536


def stiffness(subkey):
    halves = jax.random.split(subkey)
    width = 3 * NODES
    scatter_part = jax.random.uniform(halves[0], (width, width), jnp.float32, -0.1, 0.1)
    symmetric = 0.5 * (scatter_part + scatter_part.T)
    diagonal = jax.random.uniform(halves[1], (width,), jnp.float32, 1.2, 1.8)
    identity = jnp.eye(width, dtype=jnp.float32)
    return symmetric * (1.0 - identity) + identity * diagonal[None, :]


def draw_stiff_shear(key, part):
    return stiffness(jax.random.fold_in(key, 1))


def draw_stiff_lame(key, part):
    return stiffness(jax.random.fold_in(key, 2))


def pair_faces(subkey):
    inner = jnp.concatenate([jnp.arange(3 * ELEMS), 3 * ELEMS + 4 * SIDE + jnp.arange(ELEMS - 4 * SIDE)]).astype(jnp.int32)
    mixed = jax.random.permutation(subkey, inner)
    first = mixed[0::2]
    second = mixed[1::2]
    table = jnp.zeros((4 * ELEMS,), jnp.int32).at[first].set(second).at[second].set(first)
    outer = jnp.arange(4 * SIDE).astype(jnp.int32)
    return table.at[3 * ELEMS + outer].set(4 * ELEMS + outer)


def draw_neighbours(key, part):
    subkeys = jax.random.split(jax.random.fold_in(key, 3), PA * PD)
    return jax.vmap(pair_faces)(subkeys).reshape(PA, PD, 4 * ELEMS)


def pick_faces(subkey):
    return jax.random.permutation(subkey, jnp.arange(4 * ELEMS).astype(jnp.int32))[:FMAX]


def draw_fault_face(key, part):
    subkeys = jax.random.split(jax.random.fold_in(key, 4), PA * PD)
    return jax.vmap(pick_faces)(subkeys).reshape(PA, PD, FMAX)


def fault_plan(key):
    subkeys = jax.random.split(jax.random.fold_in(key, 5), 5)
    devices = PA * PD
    total = devices * FACE_OWN
    index = jnp.arange(devices).astype(jnp.int32)
    busiest = jax.random.randint(subkeys[0], (), 0, devices).astype(jnp.int32)
    weights = jax.random.randint(subkeys[1], (devices,), 2, 6).astype(jnp.int32)
    weights = jnp.where(index == busiest, 0, weights)
    remain = total - FMAX
    base = remain * weights // jnp.sum(weights)
    short = remain - jnp.sum(base)
    shuffled = jax.random.permutation(subkeys[2], index)
    ranking = jnp.zeros((devices,), jnp.int32).at[shuffled].set(index)
    ranking = ranking - (ranking > ranking[busiest]).astype(jnp.int32)
    counts = base + ((ranking < short) & (index != busiest)).astype(jnp.int32)
    counts = jnp.where(index == busiest, FMAX, counts)
    starts = jnp.cumsum(counts) - counts
    order = jnp.arange(FMAX).astype(jnp.int32)
    global_index = starts[:, None] + order[None, :]
    live = order[None, :] < counts[:, None]
    owner_perm = jax.random.permutation(subkeys[3], index)
    slot_perm = jax.random.permutation(subkeys[4], jnp.arange(FACE_OWN).astype(jnp.int32))
    owners = jnp.where(live, owner_perm[global_index % devices], 0)
    slots = jnp.where(live, slot_perm[jnp.minimum(global_index // devices, FACE_OWN - 1)], 0)
    return (counts.reshape(PA, PD), owners.reshape(PA, PD, FMAX), slots.reshape(PA, PD, FMAX))


def draw_fault_count(key, part):
    return fault_plan(key)[0]


def draw_fault_owner(key, part):
    return fault_plan(key)[1]


def draw_fault_slot(key, part):
    return fault_plan(key)[2]


def levels(key, shape, cuts, low, largest):
    def one(dim, parts):
        heights = jax.random.uniform(jax.random.fold_in(jax.random.fold_in(key, 6), dim), (parts,), jnp.float32, low / len(cuts), largest / len(cuts))
        return jnp.repeat(jnp.exp(heights), shape[dim] // parts).reshape((-1,) + (1,) * (len(shape) - dim - 1))

    level = one(*cuts[0])
    for cut in cuts[1:]:
        level = level * one(*cut)
    return level


def scatter_about(own_key, shape, deviation, limit, cuts=(), kind=jnp.bfloat16):
    result = deviation * jax.random.normal(own_key, shape, jnp.float32)
    if cuts:
        result = result * levels(own_key, shape, cuts, -0.22, 0.18)
    return jnp.clip(result, -limit, limit).astype(kind)


def setup_inputs(seed: int = 0) -> dict:
    arg_keys = jax.random.split(jax.random.key(seed), 16)
    return {
        "right_side": scatter_about(arg_keys[0], (3, NODES, PA, PD, ELEMS), 1.0, 6.0, ((2, 8), (3, 16)), jnp.float32),
        "shear_modulus": jnp.clip(jnp.exp(math.log(2.0) - 1.3862944 * jax.random.uniform(arg_keys[1], (PA, PD, ELEMS), jnp.float32) ** levels(arg_keys[1], (PA, PD, ELEMS), ((0, 8), (1, 16)), -0.2, 0.2)), 0.5, 2.0),
        "lame_lambda": jnp.clip(jnp.exp(math.log(2.0) - 1.3862944 * jax.random.uniform(arg_keys[2], (PA, PD, ELEMS), jnp.float32) ** levels(arg_keys[2], (PA, PD, ELEMS), ((0, 8), (1, 16)), -0.2, 0.2)), 0.5, 2.0),
        "stiff_shear": draw_stiff_shear(jax.random.fold_in(arg_keys[15], 71), 0),
        "stiff_lame": draw_stiff_lame(jax.random.fold_in(arg_keys[15], 71), 0),
        "face_interp": scatter_about(arg_keys[5], (QPTS, 4, NODES), 0.06, 0.875, (), jnp.float32),
        "neighbours": draw_neighbours(jax.random.fold_in(arg_keys[15], 71), 0),
        "fault_count": draw_fault_count(jax.random.fold_in(arg_keys[15], 71), 0),
        "fault_owner": draw_fault_owner(jax.random.fold_in(arg_keys[15], 71), 0),
        "fault_slot": draw_fault_slot(jax.random.fold_in(arg_keys[15], 71), 0),
        "fault_face": draw_fault_face(jax.random.fold_in(arg_keys[15], 71), 0),
        "normal_stress": jnp.clip(jnp.exp(math.log(10.0) - 2.3025851 * jax.random.uniform(arg_keys[11], (QPTS, GRID), jnp.float32) ** levels(arg_keys[11], (QPTS, GRID), ((1, 128),), -0.2, 0.2)), 1.0, 10.0),
        "friction": jnp.clip(jnp.exp(math.log(1.0) - 1.2039728 * jax.random.uniform(arg_keys[12], (QPTS, GRID), jnp.float32) ** levels(arg_keys[12], (QPTS, GRID), ((1, 128),), -0.2, 0.2)), 0.3, 1.0),
        "state_factor": jnp.clip(jnp.exp(math.log(8.0) - 2.7725887 * jax.random.uniform(arg_keys[13], (QPTS, GRID), jnp.float32) ** levels(arg_keys[13], (QPTS, GRID), ((1, 128),), -0.2, 0.2)), 0.5, 8.0),
        "shear_load": scatter_about(arg_keys[14], (2, QPTS, GRID), 1.5, 6.0, ((2, 128),), jnp.float32),
    }


highest = lax.Precision.HIGHEST
damping = 0.5
time_step = 0.5
lower_edge = 0.25
upper_edge = 5.0

def inverse_sinh(value):
    size_abs = jnp.abs(value)
    sign_of = jnp.where(value < 0.0, -1.0, 1.0)
    return sign_of * jnp.log(size_abs + jnp.sqrt(size_abs * size_abs + 1.0))

def slip_law(traction, normal_stress, friction, state_factor, shear_load):
    effective = normal_stress * (1.0 + 0.5 * jnp.tanh(traction[2]))
    strike = shear_load[0] + traction[0]
    updip = shear_load[1] + traction[1]
    magnitude = jnp.sqrt(strike * strike + updip * updip)
    resist = friction * effective
    velocity = jnp.zeros_like(magnitude)
    for sweep in range(NEWTON):
        scaled = state_factor * velocity
        misfit = magnitude - damping * velocity - resist * inverse_sinh(scaled)
        slope = -damping - resist * state_factor / jnp.sqrt(1.0 + scaled * scaled)
        velocity = velocity - misfit / slope
    factor = time_step * velocity / jnp.maximum(magnitude, 1.0)
    return (velocity, jnp.stack([factor * strike, factor * updip]))

def shift_from(values, axis, offset):
    extent = values.shape[axis]
    blank = jnp.zeros_like(lax.slice_in_dim(values, 0, 1, axis=axis))
    if offset > 0:
        return jnp.concatenate([blank, lax.slice_in_dim(values, 0, extent - 1, axis=axis)], axis)
    return jnp.concatenate([lax.slice_in_dim(values, 1, extent, axis=axis), blank], axis)

def reference(right_side, shear_modulus, lame_lambda, stiff_shear, stiff_lame, face_interp, neighbours, fault_count, fault_owner, fault_slot, fault_face, normal_stress, friction, state_factor, shear_load):
    material = lame_lambda + 2.0 * shear_modulus
    slots = 4 * ELEMS
    own_material = jnp.concatenate([material] * 4, axis=-1)
    links = jnp.broadcast_to(neighbours[None, None], (3, QPTS, PA, PD, slots))

    def face_flux(field):
        traces = jnp.einsum('qfn,cnade->cqadfe', face_interp, field, precision=highest).reshape(3, QPTS, PA, PD, slots)
        rims = traces[..., 3 * ELEMS:3 * ELEMS + 4 * SIDE].reshape(3, QPTS, PA, PD, 4, SIDE)
        rim_material = material[..., :4 * SIDE].reshape(PA, PD, 4, SIDE)
        arrived = jnp.stack([shift_from(rims[..., 1, :], 2, 1), shift_from(rims[..., 0, :], 2, -1), shift_from(rims[..., 3, :], 3, 1), shift_from(rims[..., 2, :], 3, -1)], axis=4).reshape(3, QPTS, PA, PD, 4 * SIDE)
        arrived_material = jnp.stack([shift_from(rim_material[:, :, 1], 0, 1), shift_from(rim_material[:, :, 0], 0, -1), shift_from(rim_material[:, :, 3], 1, 1), shift_from(rim_material[:, :, 2], 1, -1)], axis=2).reshape(PA, PD, 4 * SIDE)
        table = jnp.concatenate([traces, arrived], axis=-1)
        material_table = jnp.concatenate([own_material, arrived_material], axis=-1)
        other = jnp.take_along_axis(table, links, axis=-1)
        other_material = jnp.take_along_axis(material_table, neighbours, axis=-1)
        return 0.5 * (own_material + other_material) * (traces - other)

    def operate(field):
        flux = face_flux(field)
        lifted = jnp.einsum('qfn,cqadfe->cnade', face_interp, flux.reshape(3, QPTS, PA, PD, 4, ELEMS), precision=highest)
        flat = field.reshape(3 * NODES, PA, PD, ELEMS)
        volume = shear_modulus * jnp.einsum('ij,jade->iade', stiff_shear, flat, precision=highest) + lame_lambda * jnp.einsum('ij,jade->iade', stiff_lame, flat, precision=highest)
        return volume.reshape(3, NODES, PA, PD, ELEMS) + lifted
    center = 0.5 * (upper_edge + lower_edge)
    spread = 0.5 * (upper_edge - lower_edge)
    ratio = center / spread
    rho = 1.0 / ratio
    solution = jnp.zeros_like(right_side)
    residual = right_side
    direction = residual / (center * material)
    for sweep in range(ITERS):
        solution = solution + direction
        residual = residual - operate(direction)
        rho_next = 1.0 / (2.0 * ratio - rho)
        direction = rho_next * rho * direction + 2.0 * rho_next / spread * residual / material
        rho = rho_next
    face_links = jnp.broadcast_to(fault_face[None, None], (3, QPTS, PA, PD, FMAX))
    traction = jnp.take_along_axis(face_flux(solution), face_links, axis=-1)
    devices = PA * PD
    grid_size = devices * FACE_OWN
    order = jnp.arange(FMAX).astype(jnp.int32)
    live = order[None, None, :] < fault_count[:, :, None]
    grid_index = jnp.where(live, fault_owner * FACE_OWN + fault_slot, grid_size)
    grid_traction = jnp.zeros((3, QPTS, grid_size), jnp.float32).at[:, :, grid_index.reshape(-1)].set(traction.reshape(3, QPTS, devices * FMAX), mode='drop')
    slip_rate, shear_slip = slip_law(grid_traction, normal_stress, friction, state_factor, shear_load)
    fetch = jnp.minimum(grid_index, grid_size - 1).reshape(-1)
    returned = shear_slip[:, :, fetch].reshape(2, QPTS, PA, PD, FMAX) * live.astype(jnp.float32)
    face_kind = fault_face // ELEMS
    element = fault_face % ELEMS
    interp = face_interp[:, face_kind, :]
    values = 0.5 * jnp.einsum('qadjn,cqadj->cnadj', interp, returned, precision=highest)
    along_index = jnp.broadcast_to(jnp.arange(PA).astype(jnp.int32)[:, None, None], (PA, PD, FMAX))
    depth_index = jnp.broadcast_to(jnp.arange(PD).astype(jnp.int32)[None, :, None], (PA, PD, FMAX))
    jump = jnp.zeros((2, NODES, PA, PD, ELEMS), jnp.float32).at[:, :, along_index, depth_index, element].add(values)
    displacement = solution + jnp.concatenate([jump, jnp.zeros((1, NODES, PA, PD, ELEMS), jnp.float32)], axis=0)
    return (displacement, residual, slip_rate)
```

```python
import functools

import jax
import jax.numpy as jnp
from jax import lax
from jax.experimental import pallas as pl
from jax.experimental.pallas import tpu as pltpu
from jax.sharding import PartitionSpec as P

ITERS = 4
NEWTON = 6
DAMPING = 0.5
TIME_STEP = 0.5
LOWER_EDGE = 0.25
UPPER_EDGE = 5.0
CENTER = 0.5 * (UPPER_EDGE + LOWER_EDGE)
SPREAD = 0.5 * (UPPER_EDGE - LOWER_EDGE)

MESH = pl.DeviceIdType.MESH
F32 = jnp.float32
BF16 = jnp.bfloat16
NT = (((1,), (1,)), ((), ()))

PA, PD = 8, 16
DEVS = PA * PD
ELEMS = 1024
ROWS = 40
BLOCK = 512
CHUNKS = 28
RANKS = 16


def coefficients():
    ratio = CENTER / SPREAD
    rho = 1.0 / ratio
    pairs = []
    for _ in range(ITERS):
        rho_next = 1.0 / (2.0 * ratio - rho)
        pairs.append((rho_next * rho, 2.0 * rho_next / SPREAD))
        rho = rho_next
    return pairs


def halves(value):
    high = value.astype(BF16)
    return high, (value - high.astype(F32)).astype(BF16)


def product(left, right):
    return jnp.dot(left, right, preferred_element_type=F32)


def onehot(digit, rows, columns):
    return (lax.broadcasted_iota(jnp.int32, (rows, columns), 0) == digit).astype(F32)


def choose(result, chunk, count, rows):
    width = result.shape[1]
    index = jnp.broadcast_to(chunk, (8, width))
    total = jnp.zeros((rows // 8, 8, width), F32)
    for s in range(count):
        part = result[s * rows : (s + 1) * rows].reshape(rows // 8, 8, width)
        total = jnp.where((index == s)[None], part, total)
    return total.reshape(rows, width)


def inverse_sinh(size, root):
    magnitude = jnp.log(jnp.abs(size) + root)
    return jnp.where(size < 0.0, -magnitude, magnitude)


def kernel(
    load, shear_ref, lame_ref, stiff_shear, stiff_lame, interp, links, count_ref, owner_ref, slot_ref, face_ref,
    normal_ref, friction_ref, state_ref, shear_load,
    disp_ref, residual_ref, rate_ref,
    weight, weights, lift_pair, field, stacked, trace, image, gathered, flux, flux_sum, alpha, table, hot_links,
    hot_owner, prefix, send_maps, face_maps, hot_send, hot_face, table_send, halo, pack, outbox, inbox, unpack,
    wide, hot_grid, pack_back, outbox_back, inbox_back, table_back,
    halo_send, halo_recv, go_send, go_recv, back_send, back_recv,
):
    along = lax.axis_index("along")
    depth = lax.axis_index("depth")
    me = along * PD + depth

    sides = (
        (0, 1, (along + 1, depth), along < PA - 1, along > 0),
        (1, 0, (along - 1, depth), along > 0, along < PA - 1),
        (2, 3, (along, depth + 1), depth < PD - 1, depth > 0),
        (3, 2, (along, depth - 1), depth > 0, depth < PD - 1),
    )

    for side, piece, target, sends, receives in sides:
        @pl.when(jnp.logical_not(receives))
        def _():
            halo[:, side] = jnp.zeros((ITERS, ROWS, 128), F32)

    weight[...] = jnp.zeros_like(weight)
    for f in range(4):
        for c in range(3):
            weight[f * ROWS + c * 12 : f * ROWS + c * 12 + 12, c * 20 : c * 20 + 20] = interp[:, f, :]
    weight[160:220, 0:60] = stiff_shear[...]
    weight[224:284, 0:60] = stiff_lame[...]
    whole = weight[:, 0:64]
    high = whole.astype(BF16).astype(F32)
    rest = whole - high
    lift_pair[0:128, 0:128] = jnp.transpose(weight[0:128, :])
    lift_pair[0:128, 128:256] = jnp.transpose(weight[128:256, :])
    weight[:, 64:128] = high
    weights[:, 0:64] = high
    weights[:, 64:128] = high
    weights[:, 128:192] = rest
    lifter, lifter_rest = halves(lift_pair[0:64, 0:160])
    matrix = weights[:, 0:192].astype(BF16)

    shear = shear_ref[...]
    lame = lame_ref[...]
    material = lame + 2.0 * shear
    inverse = 1.0 / material

    def lifted(ref):
        high, low = halves(ref[...])
        return product(lifter, high) + product(lifter_rest, high) + product(lifter, low)

    def build_links(b, carry):
        slots = links[b + b // 6]
        hot = onehot(jnp.bitwise_and(slots, 127), 128, BLOCK).astype(BF16)
        hot_links[b, 0:128, :] = hot
        hot_links[b, 128:256, :] = hot
        return carry

    lax.fori_loop(0, 7, build_links, 0)

    residual_ref[...] = load[...]
    field[60:64, :] = jnp.zeros((4, ELEMS), F32)
    field[0:60, :] = load[...] * (inverse * (1.0 / CENTER))
    disp_ref[...] = jnp.zeros_like(disp_ref)
    flux_sum[...] = jnp.zeros_like(flux_sum)

    def halo_copy(i, side, piece, target):
        return pltpu.make_async_remote_copy(
            src_ref=trace.at[120:160, piece * 128 : piece * 128 + 128],
            dst_ref=halo.at[i, side],
            send_sem=halo_send.at[i, side],
            recv_sem=halo_recv.at[i, side],
            device_id=target,
            device_id_type=MESH,
        )

    def step(i, first, scale_old, scale_new):
        now = field[...]
        high, low = halves(now)
        stacked[0:64, :] = high
        stacked[64:128, :] = low
        stacked[128:192, :] = high
        trace[...] = product(matrix[0:160], stacked[...])
        if first:
            for f in range(4):
                trace[f * ROWS + 36 : f * ROWS + 37, :] = material
        for side, piece, target, sends, receives in sides:
            @pl.when(sends)
            def _():
                halo_copy(i, side, piece, target).start()

        for p in range(CHUNKS // 2):
            parts = []
            for s in (2 * p, 2 * p + 1):
                t = s if s < 24 else s + 4
                f, j = t // 8, t % 8
                parts.append(trace[f * ROWS : (f + 1) * ROWS, j * 128 : (j + 1) * 128])
            high, low = halves(jnp.concatenate(parts, axis=0))
            table[p * 80 : p * 80 + 80, 0:128] = high
            table[p * 80 : p * 80 + 80, 128:256] = low

        def block(b, carry):
            place = b + b // 6
            chunk = lax.shift_right_logical(links[place], 7)
            chunk = jnp.where(chunk >= 24, chunk - 4, chunk)
            result = product(table[...], hot_links[b])
            f = place // 2
            half = place - 2 * f
            gathered[
                pl.ds(pl.multiple_of(f * ROWS, 8), ROWS), pl.ds(pl.multiple_of(half * BLOCK, BLOCK), BLOCK)
            ] = choose(result, chunk, CHUNKS, ROWS)
            return carry

        lax.fori_loop(0, 7, block, 0)

        volume = product(matrix[160:288], stacked[...])
        image[...] = shear * volume[0:64] + lame * volume[64:128]
        disp_ref[...] = disp_ref[...] + now[0:60]

        for side, piece, target, sends, receives in sides:
            @pl.when(receives)
            def _():
                halo_copy(i, side, piece, target).wait_recv()
            gathered[120:160, side * 128 : side * 128 + 128] = halo[i, side]

        if first:
            for f in range(4):
                alpha[f : f + 1, :] = 0.5 * (material + gathered[f * ROWS + 36 : f * ROWS + 37, :])
        for f in range(4):
            rows = slice(f * ROWS, (f + 1) * ROWS)
            value = alpha[f : f + 1, :] * (trace[rows, :] - gathered[rows, :])
            flux[rows, :] = value
            flux_sum[rows, :] = flux_sum[rows, :] + value
        left = residual_ref[...] - (image[...] + lifted(flux))[0:60]
        residual_ref[...] = left
        field[0:60, :] = scale_old * now[0:60] + scale_new * (left * inverse)
        for side, piece, target, sends, receives in sides:
            @pl.when(sends)
            def _():
                halo_copy(i, side, piece, target).wait_send()

    pairs = coefficients()
    step(0, True, *pairs[0])

    def later(i, carry):
        scale_old = jnp.where(i == 1, pairs[1][0], jnp.where(i == 2, pairs[2][0], pairs[3][0]))
        scale_new = jnp.where(i == 1, pairs[1][1], jnp.where(i == 2, pairs[2][1], pairs[3][1]))
        step(i, False, scale_old, scale_new)
        return carry

    lax.fori_loop(1, ITERS, later, 0)

    count = count_ref[...]
    lane = lax.broadcasted_iota(jnp.int32, (1, 128), 1)
    for t in range(RANKS):
        live = (lane + t * 128) < count
        owner = jnp.where(live, owner_ref[t], -1)
        hot_owner[t * 128 : (t + 1) * 128, :] = onehot(owner, 128, 128).astype(BF16)
    row = lax.broadcasted_iota(jnp.int32, (128, 256), 0)
    column = lax.broadcasted_iota(jnp.int32, (128, 256), 1)
    earlier = ((row < column) | (column >= 128)).astype(F32).astype(BF16)
    prefix[...] = product(hot_owner[...], earlier)
    base = jnp.zeros((128, 128), F32)
    sent = jnp.zeros((64, 128), F32)
    placed = jnp.zeros((64, 128), F32)
    for t in range(RANKS):
        rows = slice(t * 128, (t + 1) * 128)
        hot = hot_owner[rows, :]
        rank = jnp.sum(hot.astype(F32) * (prefix[rows, 0:128] + base), axis=0, keepdims=True)
        base = base + prefix[rows, 128:256]
        live = ((lane + t * 128) < count).astype(F32)
        rank_live = jnp.where(live > 0.0, rank, -1.0).astype(jnp.int32)
        face = face_ref[t]
        slot = slot_ref[t]
        face_high = lax.shift_right_logical(face, 7)
        face_low = jnp.bitwise_and(face, 127)
        ranks = onehot(rank_live, RANKS, 128)
        values = jnp.concatenate(
            [
                ranks * face_high.astype(F32),
                ranks * face_low.astype(F32),
                ranks * (lax.shift_right_logical(slot, 4) + 1).astype(F32),
                ranks * jnp.bitwise_and(slot, 15).astype(F32),
            ],
            axis=0,
        ).astype(BF16)
        sent = sent + lax.dot_general(values, hot, NT, preferred_element_type=F32)
        highs = onehot(face_high, 32, 128) * live
        values = jnp.concatenate([highs * (rank + 1.0), highs * owner_ref[t].astype(F32)], axis=0).astype(BF16)
        lows = onehot(face_low, 128, 128).astype(BF16)
        placed = placed + lax.dot_general(values, lows, NT, preferred_element_type=F32)
    send_maps[...] = sent
    face_maps[...] = placed

    for p in range(16):
        parts = []
        for s in (2 * p, 2 * p + 1):
            f, j = s // 8, s % 8
            parts.append(flux_sum[f * ROWS : (f + 1) * ROWS, j * 128 : (j + 1) * 128])
        high, low = halves(jnp.concatenate(parts, axis=0))
        table_send[p * 80 : p * 80 + 80, 0:128] = high
        table_send[p * 80 : p * 80 + 80, 128:256] = low
    for b in range(4):
        high = jnp.concatenate([send_maps[4 * b + j : 4 * b + j + 1, :] for j in range(4)], axis=1)
        low = jnp.concatenate([send_maps[16 + 4 * b + j : 17 + 4 * b + j, :] for j in range(4)], axis=1)
        hot = onehot(low.astype(jnp.int32), 128, BLOCK).astype(BF16)
        hot_send[0:128, :] = hot
        hot_send[128:256, :] = hot
        result = product(table_send[...], hot_send[...])
        chosen = choose(result, high.astype(jnp.int32), 32, ROWS)
        for j in range(4):
            rank = 4 * b + j
            pack[rank * ROWS : (rank + 1) * ROWS, :] = chosen[:, j * 128 : (j + 1) * 128]
            pack[rank * ROWS + 36 : rank * ROWS + 37, :] = (
                16.0 * send_maps[32 + rank : 33 + rank, :] + send_maps[48 + rank : 49 + rank, :] - 16.0
            )
    for j in range(5):
        outbox[pl.ds(j, 128, stride=8), :] = jnp.transpose(pack[j * 128 : (j + 1) * 128, :])

    def exchange(k, source, landing, size, send_sem, recv_sem):
        target = lax.rem(me + k, DEVS)
        return pltpu.make_async_remote_copy(
            src_ref=source.at[pl.ds(pl.multiple_of(target * 8, 8), size)],
            dst_ref=landing.at[pl.ds(pl.multiple_of(me * 8, 8), size)],
            send_sem=send_sem.at[k],
            recv_sem=recv_sem.at[k],
            device_id=(lax.div(target, PD), lax.rem(target, PD)),
            device_id_type=MESH,
        )

    def arrival(k, source, landing, size, send_sem, recv_sem):
        origin = lax.rem(me + DEVS - k, DEVS)
        return pltpu.make_async_remote_copy(
            src_ref=source.at[pl.ds(pl.multiple_of(origin * 8, 8), size)],
            dst_ref=landing.at[pl.ds(pl.multiple_of(origin * 8, 8), size)],
            send_sem=send_sem.at[k],
            recv_sem=recv_sem.at[k],
            device_id=(lax.div(origin, PD), lax.rem(origin, PD)),
            device_id_type=MESH,
        )

    def start_all(*what):
        def one(k, carry):
            exchange(k, *what).start()
            return carry

        lax.fori_loop(1, DEVS, one, 0)

    def receive_all(*what):
        def one(k, carry):
            arrival(k, *what).wait_recv()
            return carry

        lax.fori_loop(1, DEVS, one, 0)

    def sent_all(*what):
        def one(k, carry):
            exchange(k, *what).wait_send()
            return carry

        lax.fori_loop(1, DEVS, one, 0)

    go = (outbox, inbox, 5, go_send, go_recv)
    start_all(*go)
    mine = pl.ds(pl.multiple_of(me * 8, 8), 8)
    inbox[mine, :] = outbox[mine, :]

    def build_face(b, carry):
        low = jnp.concatenate([face_maps[pl.ds(32 + 4 * b + j, 1), :] for j in range(4)], axis=1)
        hot = onehot(low.astype(jnp.int32), 128, BLOCK).astype(BF16)
        hot_face[b, 0:128, :] = hot
        hot_face[b, 128:256, :] = hot
        return carry

    lax.fori_loop(0, 8, build_face, 0)

    receive_all(*go)
    for j in range(5):
        unpack[j * 128 : (j + 1) * 128, :] = jnp.transpose(inbox[pl.ds(j, 128, stride=8), :])
    for rank in range(RANKS):
        lanes = slice(rank * 128, (rank + 1) * 128)
        value = unpack[rank * ROWS : (rank + 1) * ROWS, :]
        high, low = halves(value)
        wide[0:40, lanes] = high.astype(F32)
        wide[40:80, lanes] = low.astype(F32)
        place = value[36:37, :].astype(jnp.int32)
        hot_grid[:, lanes] = onehot(place, BLOCK, 128).astype(BF16)
    both = lax.dot_general(wide[...].astype(BF16), hot_grid[...], NT, preferred_element_type=F32)
    traction = both[0:40] + both[40:80]

    state = state_ref[...]
    effective = normal_ref[...] * (1.0 + 0.5 * jnp.tanh(traction[24:36]))
    strike = shear_load[0] + traction[0:12]
    updip = shear_load[1] + traction[12:24]
    magnitude = jnp.sqrt(strike * strike + updip * updip)
    resist = friction_ref[...] * effective
    steep = resist * state
    velocity = magnitude / (DAMPING + steep)
    for _ in range(NEWTON - 1):
        scaled = state * velocity
        square = 1.0 + scaled * scaled
        inverse_root = lax.rsqrt(square)
        misfit = magnitude - DAMPING * velocity - resist * inverse_sinh(scaled, square * inverse_root)
        velocity = velocity + misfit / (DAMPING + steep * inverse_root)
    rate_ref[...] = velocity
    factor = TIME_STEP * velocity / jnp.maximum(magnitude, 1.0)
    slip = jnp.concatenate([factor * strike, factor * updip], axis=0)
    high = slip.astype(BF16).astype(F32)
    slip = jnp.concatenate([high, slip - high], axis=0).astype(BF16)
    out = product(slip, hot_grid[...])
    for rank in range(RANKS):
        lanes = slice(rank * 128, (rank + 1) * 128)
        pack_back[rank * 24 : (rank + 1) * 24, :] = out[0:24, lanes] + out[24:48, lanes]
    for j in range(3):
        outbox_back[pl.ds(j, 128, stride=8), :] = jnp.transpose(pack_back[j * 128 : (j + 1) * 128, :])
    back = (outbox_back, inbox_back, 3, back_send, back_recv)
    start_all(*back)
    inbox_back[mine, :] = outbox_back[mine, :]
    sent_all(*go)
    flux[...] = jnp.zeros_like(flux)
    receive_all(*back)

    for j in range(3):
        high, low = halves(jnp.transpose(inbox_back[pl.ds(j, 128, stride=8), :]))
        table_back[j * 128 : (j + 1) * 128, 0:128] = high
        table_back[j * 128 : (j + 1) * 128, 128:256] = low

    def place_back(b, carry):
        rank = jnp.concatenate([face_maps[pl.ds(4 * b + j, 1), :] for j in range(4)], axis=1)
        result = product(table_back[...], hot_face[b])
        f = b // 2
        half = b - 2 * f
        flux[
            pl.ds(pl.multiple_of(f * ROWS, 8), 24), pl.ds(pl.multiple_of(half * BLOCK, BLOCK), BLOCK)
        ] = choose(result, rank.astype(jnp.int32) - 1, RANKS, 24)
        return carry

    lax.fori_loop(0, 8, place_back, 0)
    disp_ref[...] = disp_ref[...] + 0.5 * lifted(flux)[0:60]
    sent_all(*back)


def on_device(
    right_side,
    shear_modulus,
    lame_lambda,
    stiff_shear,
    stiff_lame,
    face_interp,
    neighbours,
    fault_count,
    fault_owner,
    fault_slot,
    fault_face,
    normal_stress,
    friction,
    state_factor,
    shear_load,
):
    vmem = pl.BlockSpec(memory_space=pltpu.VMEM)
    scratch = [
        pltpu.VMEM((288, 128), F32),
        pltpu.VMEM((288, 256), F32),
        pltpu.VMEM((128, 256), F32),
        pltpu.VMEM((64, ELEMS), F32),
        pltpu.VMEM((192, ELEMS), BF16),
        pltpu.VMEM((160, ELEMS), F32),
        pltpu.VMEM((64, ELEMS), F32),
        pltpu.VMEM((160, ELEMS), F32),
        pltpu.VMEM((160, ELEMS), F32),
        pltpu.VMEM((160, ELEMS), F32),
        pltpu.VMEM((8, ELEMS), F32),
        pltpu.VMEM((CHUNKS * ROWS, 256), BF16),
        pltpu.VMEM((7, 256, BLOCK), BF16),
        pltpu.VMEM((2048, 128), BF16),
        pltpu.VMEM((2048, 256), F32),
        pltpu.VMEM((64, 128), F32),
        pltpu.VMEM((64, 128), F32),
        pltpu.VMEM((256, BLOCK), BF16),
        pltpu.VMEM((8, 256, BLOCK), BF16),
        pltpu.VMEM((32 * ROWS, 256), BF16),
        pltpu.VMEM((ITERS, 4, ROWS, 128), F32),
        pltpu.VMEM((640, 128), F32),
        pltpu.VMEM((1024, 128), F32),
        pltpu.VMEM((1024, 128), F32),
        pltpu.VMEM((640, 128), F32),
        pltpu.VMEM((80, 2048), F32),
        pltpu.VMEM((BLOCK, 2048), BF16),
        pltpu.VMEM((384, 128), F32),
        pltpu.VMEM((1024, 128), F32),
        pltpu.VMEM((1024, 128), F32),
        pltpu.VMEM((384, 256), BF16),
        pltpu.SemaphoreType.DMA((ITERS, 4)),
        pltpu.SemaphoreType.DMA((ITERS, 4)),
        pltpu.SemaphoreType.DMA((DEVS,)),
        pltpu.SemaphoreType.DMA((DEVS,)),
        pltpu.SemaphoreType.DMA((DEVS,)),
        pltpu.SemaphoreType.DMA((DEVS,)),
    ]
    displacement, residual, rate = pl.pallas_call(
        kernel,
        out_shape=(
            jax.ShapeDtypeStruct((60, ELEMS), F32),
            jax.ShapeDtypeStruct((60, ELEMS), F32),
            jax.ShapeDtypeStruct((12, 512), F32),
        ),
        in_specs=[vmem] * 15,
        out_specs=(vmem, vmem, vmem),
        scratch_shapes=scratch,
        compiler_params=pltpu.CompilerParams(has_side_effects=True, vmem_limit_bytes=48 * 2**20),
        name="window",
    )(
        right_side.reshape(60, ELEMS),
        shear_modulus.reshape(1, ELEMS),
        lame_lambda.reshape(1, ELEMS),
        stiff_shear,
        stiff_lame,
        face_interp,
        neighbours.reshape(8, 1, BLOCK),
        fault_count.reshape(1, 1),
        fault_owner.reshape(16, 1, 128),
        fault_slot.reshape(16, 1, 128),
        fault_face.reshape(16, 1, 128),
        normal_stress,
        friction,
        state_factor,
        shear_load,
    )
    return displacement.reshape(right_side.shape), residual.reshape(right_side.shape), rate


def solution(mesh):
    in_specs = (
        P(None, None, "along", "depth", None),
        P("along", "depth", None),
        P("along", "depth", None),
        P(),
        P(),
        P(),
        P("along", "depth", None),
        P("along", "depth"),
        P("along", "depth", None),
        P("along", "depth", None),
        P("along", "depth", None),
        P(None, ("along", "depth")),
        P(None, ("along", "depth")),
        P(None, ("along", "depth")),
        P(None, None, ("along", "depth")),
    )
    out_specs = (
        P(None, None, "along", "depth", None),
        P(None, None, "along", "depth", None),
        P(None, ("along", "depth")),
    )
    return jax.shard_map(
        on_device, mesh=mesh, in_specs=in_specs, out_specs=out_specs, check_vma=False
    )
```

```python
import functools

import jax
import jax.numpy as jnp
from jax import lax
from jax.experimental import pallas as pl
from jax.experimental.pallas import tpu as pltpu
from jax.sharding import PartitionSpec as P

ITERS = 4
NEWTON = 6
DAMPING = 0.5
TIME_STEP = 0.5
LOWER_EDGE = 0.25
UPPER_EDGE = 5.0
CENTER = 0.5 * (UPPER_EDGE + LOWER_EDGE)
SPREAD = 0.5 * (UPPER_EDGE - LOWER_EDGE)

MESH = pl.DeviceIdType.MESH
F32 = jnp.float32
BF16 = jnp.bfloat16
NT = (((1,), (1,)), ((), ()))

PA, PD = 8, 16
DEVS = PA * PD
ELEMS = 1024
ROWS = 40
BLOCK = 512
CHUNKS = 28
RANKS = 16


def coefficients():
    ratio = CENTER / SPREAD
    rho = 1.0 / ratio
    pairs = []
    for _ in range(ITERS):
        rho_next = 1.0 / (2.0 * ratio - rho)
        pairs.append((rho_next * rho, 2.0 * rho_next / SPREAD))
        rho = rho_next
    return pairs


def halves(value):
    high = value.astype(BF16)
    return high, (value - high.astype(F32)).astype(BF16)


def product(left, right):
    return jnp.dot(left, right, preferred_element_type=F32)


def onehot(digit, rows, columns):
    return (lax.broadcasted_iota(jnp.int32, (rows, columns), 0) == digit).astype(F32)


def choose(result, chunk, count, rows):
    width = result.shape[1]
    index = jnp.broadcast_to(chunk, (8, width))
    total = jnp.zeros((rows // 8, 8, width), F32)
    for s in range(count):
        part = result[s * rows : (s + 1) * rows].reshape(rows // 8, 8, width)
        total = jnp.where((index == s)[None], part, total)
    return total.reshape(rows, width)


def inverse_sinh(size, root):
    magnitude = jnp.log(jnp.abs(size) + root)
    return jnp.where(size < 0.0, -magnitude, magnitude)


def kernel(
    load, shear_ref, lame_ref, stiff_shear, stiff_lame, interp, links, count_ref, owner_ref, slot_ref, face_ref,
    normal_ref, friction_ref, state_ref, shear_load,
    disp_ref, residual_ref, rate_ref,
    weight, weights, lift_pair, solved, left_over, field, stacked, trace, image, gathered, flux, flux_sum, alpha,
    table, hot_links, hot_owner, prefix, send_maps, face_maps, hot_send, hot_face, table_send, halo, rims,
    ids_out, ids_one, ids_mid, ids_in, hot_grid, params_pack, params_out, params_one, params_mid, params_in, params,
    tractions, rate_pack, rate_out, rate_one, rate_mid, rate_in, wide, table_back,
    halo_send, halo_recv, ids_a, ids_b, ids_c, ids_d, par_a, par_b, par_c, par_d, rate_a, rate_b, rate_c, rate_d,
):
    along = lax.axis_index("along")
    depth = lax.axis_index("depth")

    barrier = pltpu.get_barrier_semaphore()
    for i in range(1, PA):
        pl.semaphore_signal(barrier, inc=1, device_id=(lax.rem(along + i, PA), depth), device_id_type=MESH)
    for i in range(1, PD):
        pl.semaphore_signal(barrier, inc=1, device_id=(along, lax.rem(depth + i, PD)), device_id_type=MESH)

    def row_copy(i, source, landing, size, sems, sending):
        peer = lax.rem(along + i, PA) if sending else lax.rem(along + PA - i, PA)
        place = along if sending else peer
        return pltpu.make_async_remote_copy(
            src_ref=source.at[pl.ds(pl.multiple_of(peer * size, 8), size)],
            dst_ref=landing.at[pl.ds(pl.multiple_of(place * size, 8), size)],
            send_sem=sems[0].at[i],
            recv_sem=sems[1].at[i],
            device_id=(peer, depth),
            device_id_type=MESH,
        )

    def column_copy(i, source, landing, size, sems, sending):
        peer = lax.rem(depth + i, PD) if sending else lax.rem(depth + PD - i, PD)
        place = depth if sending else peer
        return pltpu.make_async_remote_copy(
            src_ref=source.at[pl.ds(pl.multiple_of(peer * size, 8), size)],
            dst_ref=landing.at[pl.ds(pl.multiple_of(place * size, 8), size)],
            send_sem=sems[0].at[i],
            recv_sem=sems[1].at[i],
            device_id=(along, peer),
            device_id_type=MESH,
        )

    def go(kind, source, landing, size, sems):
        mine, peers = (along, PA) if kind is row_copy else (depth, PD)
        for i in range(1, peers):
            kind(i, source, landing, size, sems, True).start()
        own = pl.ds(pl.multiple_of(mine * size, 8), size)
        landing[own, :] = source[own, :]

    def arrive(kind, source, landing, size, sems):
        for i in range(1, PA if kind is row_copy else PD):
            kind(i, source, landing, size, sems, False).wait_recv()

    def drain(kind, source, landing, size, sems):
        for i in range(1, PA if kind is row_copy else PD):
            kind(i, source, landing, size, sems, True).wait_send()

    ids_first = (row_copy, ids_out, ids_one, 16, (ids_a, ids_b))
    ids_second = (column_copy, ids_mid, ids_in, 8, (ids_c, ids_d))
    params_first = (column_copy, params_out, params_one, 48, (par_a, par_b))
    params_second = (row_copy, params_mid, params_in, 96, (par_c, par_d))
    rate_first = (row_copy, rate_out, rate_one, 32, (rate_a, rate_b))
    rate_second = (column_copy, rate_mid, rate_in, 16, (rate_c, rate_d))

    count = count_ref[...]
    lane = lax.broadcasted_iota(jnp.int32, (1, 128), 1)
    for t in range(RANKS):
        live = (lane + t * 128) < count
        owner = jnp.where(live, owner_ref[t], -1)
        hot_owner[t * 128 : (t + 1) * 128, :] = onehot(owner, 128, 128).astype(BF16)
    row = lax.broadcasted_iota(jnp.int32, (128, 256), 0)
    column = lax.broadcasted_iota(jnp.int32, (128, 256), 1)
    earlier = ((row < column) | (column >= 128)).astype(F32).astype(BF16)
    prefix[...] = product(hot_owner[...], earlier)
    base = jnp.zeros((128, 128), F32)
    sent = jnp.zeros((64, 128), F32)
    placed = jnp.zeros((64, 128), F32)
    for t in range(RANKS):
        rows = slice(t * 128, (t + 1) * 128)
        hot = hot_owner[rows, :]
        rank = jnp.sum(hot.astype(F32) * (prefix[rows, 0:128] + base), axis=0, keepdims=True)
        base = base + prefix[rows, 128:256]
        live = ((lane + t * 128) < count).astype(F32)
        rank_live = jnp.where(live > 0.0, rank, -1.0).astype(jnp.int32)
        face = face_ref[t]
        slot = slot_ref[t]
        face_high = lax.shift_right_logical(face, 7)
        face_low = jnp.bitwise_and(face, 127)
        ranks = onehot(rank_live, RANKS, 128)
        values = jnp.concatenate(
            [
                ranks * face_high.astype(F32),
                ranks * face_low.astype(F32),
                ranks * (lax.shift_right_logical(slot, 4) + 1).astype(F32),
                ranks * jnp.bitwise_and(slot, 15).astype(F32),
            ],
            axis=0,
        ).astype(BF16)
        sent = sent + lax.dot_general(values, hot, NT, preferred_element_type=F32)
        highs = onehot(face_high, 32, 128) * live
        values = jnp.concatenate([highs * (rank + 1.0), highs * owner_ref[t].astype(F32)], axis=0).astype(BF16)
        lows = onehot(face_low, 128, 128).astype(BF16)
        placed = placed + lax.dot_general(values, lows, NT, preferred_element_type=F32)
    send_maps[...] = sent
    face_maps[...] = placed
    ids = 16.0 * sent[32:48] + sent[48:64] - 16.0
    ids_out[...] = jnp.transpose(jnp.concatenate([ids, jnp.zeros((112, 128), F32)], axis=0))

    pl.semaphore_wait(barrier, PA + PD - 2)
    go(*ids_first)

    sides = (
        (0, 1, (along + 1, depth), along < PA - 1, along > 0),
        (1, 0, (along - 1, depth), along > 0, along < PA - 1),
        (2, 3, (along, depth + 1), depth < PD - 1, depth > 0),
        (3, 2, (along, depth - 1), depth > 0, depth < PD - 1),
    )

    for side, piece, target, sends, receives in sides:
        @pl.when(jnp.logical_not(receives))
        def _():
            halo[:, side] = jnp.zeros((ITERS, ROWS, 128), F32)

    weight[...] = jnp.zeros_like(weight)
    for f in range(4):
        for c in range(3):
            weight[f * ROWS + c * 12 : f * ROWS + c * 12 + 12, c * 20 : c * 20 + 20] = interp[:, f, :]
    weight[160:220, 0:60] = stiff_shear[...]
    weight[224:284, 0:60] = stiff_lame[...]
    whole = weight[:, 0:64]
    high = whole.astype(BF16).astype(F32)
    rest = whole - high
    lift_pair[0:128, 0:128] = jnp.transpose(weight[0:128, :])
    lift_pair[0:128, 128:256] = jnp.transpose(weight[128:256, :])
    weights[:, 0:64] = high
    weights[:, 64:128] = high
    weights[:, 128:192] = rest
    lifter, lifter_rest = halves(lift_pair[0:64, 0:160])
    matrix = weights[:, 0:192].astype(BF16)

    shear = shear_ref[...]
    lame = lame_ref[...]
    material = lame + 2.0 * shear
    inverse = 1.0 / material

    def lifted(ref):
        high, low = halves(ref[...])
        return product(lifter, high) + product(lifter_rest, high) + product(lifter, low)

    def build_links(b, carry):
        slots = links[b + b // 6]
        hot = onehot(jnp.bitwise_and(slots, 127), 128, BLOCK).astype(BF16)
        hot_links[b, 0:128, :] = hot
        hot_links[b, 128:256, :] = hot
        return carry

    right = load[...].reshape(60, ELEMS)
    left_over[...] = right
    field[60:64, :] = jnp.zeros((4, ELEMS), F32)
    field[0:60, :] = right * (inverse * (1.0 / CENTER))
    solved[...] = jnp.zeros_like(solved)
    flux_sum[...] = jnp.zeros_like(flux_sum)

    def halo_copy(i, side, piece, target):
        return pltpu.make_async_remote_copy(
            src_ref=rims.at[i, piece],
            dst_ref=halo.at[i, side],
            send_sem=halo_send.at[i, side],
            recv_sem=halo_recv.at[i, side],
            device_id=target,
            device_id_type=MESH,
        )

    def step(i, scale_old, scale_new, between):
        first = i == 0
        now = field[...]
        high, low = halves(now)
        stacked[0:64, :] = high
        stacked[64:128, :] = low
        stacked[128:192, :] = high
        trace[...] = product(matrix[0:160], stacked[...])
        if first:
            for f in range(4):
                trace[f * ROWS + 36 : f * ROWS + 37, :] = material
        for side, piece, target, sends, receives in sides:
            rims[i, piece] = trace[120:160, piece * 128 : piece * 128 + 128]

            @pl.when(sends)
            def _():
                halo_copy(i, side, piece, target).start()

        if first:
            lax.fori_loop(0, 7, build_links, 0)

        for p in range(CHUNKS // 2):
            parts = []
            for s in (2 * p, 2 * p + 1):
                t = s if s < 24 else s + 4
                f, j = t // 8, t % 8
                parts.append(trace[f * ROWS : (f + 1) * ROWS, j * 128 : (j + 1) * 128])
            high, low = halves(jnp.concatenate(parts, axis=0))
            table[p * 80 : p * 80 + 80, 0:128] = high
            table[p * 80 : p * 80 + 80, 128:256] = low

        def block(b, carry):
            place = b + b // 6
            chunk = lax.shift_right_logical(links[place], 7)
            chunk = jnp.where(chunk >= 24, chunk - 4, chunk)
            result = product(table[...], hot_links[b])
            f = place // 2
            half = place - 2 * f
            gathered[
                pl.ds(pl.multiple_of(f * ROWS, 8), ROWS), pl.ds(pl.multiple_of(half * BLOCK, BLOCK), BLOCK)
            ] = choose(result, chunk, CHUNKS, ROWS)
            return carry

        lax.fori_loop(0, 7, block, 0)

        volume = product(matrix[160:288], stacked[...])
        image[...] = shear * volume[0:64] + lame * volume[64:128]
        solved[...] = solved[...] + now[0:60]
        between()

        for side, piece, target, sends, receives in sides:
            @pl.when(receives)
            def _():
                halo_copy(i, side, piece, target).wait_recv()
            gathered[120:160, side * 128 : side * 128 + 128] = halo[i, side]

        if first:
            for f in range(4):
                alpha[f : f + 1, :] = 0.5 * (material + gathered[f * ROWS + 36 : f * ROWS + 37, :])
        for f in range(4):
            rows = slice(f * ROWS, (f + 1) * ROWS)
            value = alpha[f : f + 1, :] * (trace[rows, :] - gathered[rows, :])
            flux[rows, :] = value
            flux_sum[rows, :] = flux_sum[rows, :] + value
        left = left_over[...] - (image[...] + lifted(flux))[0:60]
        left_over[...] = left
        if i < ITERS - 1:
            field[0:60, :] = scale_old * now[0:60] + scale_new * (left * inverse)

    def nothing():
        pass

    def ids_middle():
        arrive(*ids_first)
        for a in range(PA):
            ids_mid[pl.ds(a, PD, stride=PA), :] = ids_one[a * PD : (a + 1) * PD, :]
        go(*ids_second)

    def answer():
        arrive(*ids_second)
        asked = jnp.transpose(ids_in[...])[0:RANKS].astype(jnp.int32)
        for rank in range(RANKS):
            hot_grid[:, rank * 128 : (rank + 1) * 128] = onehot(asked[rank : rank + 1], BLOCK, 128).astype(BF16)
        owned = jnp.concatenate(
            [normal_ref[...] * friction_ref[...], state_ref[...], shear_load[0], shear_load[1]], axis=0
        )
        high = owned.astype(BF16).astype(F32)
        both = product(jnp.concatenate([high, owned - high], axis=0).astype(BF16), hot_grid[...])
        for rank in range(RANKS):
            lanes = slice(rank * 128, (rank + 1) * 128)
            params_pack[rank * 48 : (rank + 1) * 48, :] = both[0:48, lanes] + both[48:96, lanes]
        for j in range(6):
            params_out[pl.ds(j, 128, stride=6), :] = jnp.transpose(params_pack[j * 128 : (j + 1) * 128, :])
        go(*params_first)

    def params_middle():
        arrive(*params_first)
        for d in range(PD):
            for j in range(6):
                params_mid[pl.ds(d * 6 + j, PA, stride=96), :] = params_one[pl.ds(d * 48 + j, PA, stride=6), :]
        go(*params_second)

    pairs = coefficients()
    step(0, *pairs[0], nothing)
    ids_middle()
    step(1, *pairs[1], nothing)
    answer()
    step(2, *pairs[2], nothing)
    step(3, *pairs[3], params_middle)
    residual_ref[...] = left_over[...].reshape(60, 1, ELEMS)

    for p in range(16):
        parts = []
        for s in (2 * p, 2 * p + 1):
            f, j = s // 8, s % 8
            parts.append(flux_sum[f * ROWS : (f + 1) * ROWS, j * 128 : (j + 1) * 128])
        high, low = halves(jnp.concatenate(parts, axis=0))
        table_send[p * 80 : p * 80 + 80, 0:128] = high
        table_send[p * 80 : p * 80 + 80, 128:256] = low
    for b in range(4):
        high = jnp.concatenate([send_maps[4 * b + j : 4 * b + j + 1, :] for j in range(4)], axis=1)
        low = jnp.concatenate([send_maps[16 + 4 * b + j : 17 + 4 * b + j, :] for j in range(4)], axis=1)
        hot = onehot(low.astype(jnp.int32), 128, BLOCK).astype(BF16)
        hot_send[0:128, :] = hot
        hot_send[128:256, :] = hot
        result = product(table_send[...], hot_send[...])
        tractions[b] = choose(result, high.astype(jnp.int32), 32, ROWS)

    def build_face(b, carry):
        low = jnp.concatenate([face_maps[pl.ds(32 + 4 * b + j, 1), :] for j in range(4)], axis=1)
        hot = onehot(low.astype(jnp.int32), 128, BLOCK).astype(BF16)
        hot_face[b, 0:128, :] = hot
        hot_face[b, 128:256, :] = hot
        return carry

    lax.fori_loop(0, 8, build_face, 0)
    rate_pack[...] = jnp.zeros_like(rate_pack)

    arrive(*params_second)
    for j in range(6):
        params[j * 128 : (j + 1) * 128, :] = jnp.transpose(params_in[pl.ds(j, 128, stride=6), :])
    for b in range(4):
        first = [params[(4 * b + j) * 48 : (4 * b + j + 1) * 48, :] for j in range(4)]
        owned = jnp.concatenate(first, axis=1)
        traction = tractions[b]
        state = owned[12:24]
        strike = owned[24:36] + traction[0:12]
        updip = owned[36:48] + traction[12:24]
        magnitude = jnp.sqrt(strike * strike + updip * updip)
        resist = owned[0:12] * (1.0 + 0.5 * jnp.tanh(traction[24:36]))
        steep = resist * state
        velocity = magnitude / (DAMPING + steep)
        for _ in range(NEWTON - 1):
            scaled = state * velocity
            square = 1.0 + scaled * scaled
            inverse_root = lax.rsqrt(square)
            misfit = magnitude - DAMPING * velocity - resist * inverse_sinh(scaled, square * inverse_root)
            velocity = velocity + misfit / (DAMPING + steep * inverse_root)
        factor = TIME_STEP * velocity / jnp.maximum(magnitude, 1.0)
        slip = jnp.concatenate([factor * strike, factor * updip], axis=0)
        for j in range(4):
            rank = 4 * b + j
            rate_pack[rank * 16 : rank * 16 + 12, :] = velocity[:, j * 128 : (j + 1) * 128]
        for j in (0, 2):
            parts = [slip[:, j * 128 : (j + 1) * 128], slip[:, (j + 1) * 128 : (j + 2) * 128]]
            high, low = halves(jnp.concatenate(parts, axis=0))
            at = (4 * b + j) * 24
            table_back[at : at + 48, 0:128] = high
            table_back[at : at + 48, 128:256] = low
    for j in range(2):
        rate_out[pl.ds(j, 128, stride=2), :] = jnp.transpose(rate_pack[j * 128 : (j + 1) * 128, :])
    go(*rate_first)

    flux[...] = jnp.zeros_like(flux)

    def place_back(b, carry):
        rank = jnp.concatenate([face_maps[pl.ds(4 * b + j, 1), :] for j in range(4)], axis=1)
        result = product(table_back[...], hot_face[b])
        f = b // 2
        half = b - 2 * f
        flux[
            pl.ds(pl.multiple_of(f * ROWS, 8), 24), pl.ds(pl.multiple_of(half * BLOCK, BLOCK), BLOCK)
        ] = choose(result, rank.astype(jnp.int32) - 1, RANKS, 24)
        return carry

    lax.fori_loop(0, 8, place_back, 0)

    arrive(*rate_first)
    for a in range(PA):
        for j in range(2):
            rate_mid[pl.ds(a * 2 + j, PD, stride=16), :] = rate_one[pl.ds(a * 32 + j, PD, stride=2), :]
    go(*rate_second)
    disp_ref[...] = (solved[...] + 0.5 * lifted(flux)[0:60]).reshape(60, 1, ELEMS)
    for each in (ids_first, ids_second, params_first, params_second, rate_first):
        drain(*each)
    for i in range(ITERS):
        for side, piece, target, sends, receives in sides:
            @pl.when(sends)
            def _():
                halo_copy(i, side, piece, target).wait_send()

    arrive(*rate_second)
    for j in range(2):
        value = jnp.transpose(rate_in[pl.ds(j, 128, stride=2), :])
        high = value.astype(BF16).astype(F32)
        low = value - high
        for r in range(8):
            lanes = slice((8 * j + r) * 128, (8 * j + r + 1) * 128)
            wide[0:16, lanes] = high[r * 16 : (r + 1) * 16]
            wide[16:32, lanes] = low[r * 16 : (r + 1) * 16]
    both = lax.dot_general(wide[...].astype(BF16), hot_grid[...], NT, preferred_element_type=F32)
    rate_ref[...] = both[0:12] + both[16:28]
    drain(*rate_second)


def on_device(
    right_side,
    shear_modulus,
    lame_lambda,
    stiff_shear,
    stiff_lame,
    face_interp,
    neighbours,
    fault_count,
    fault_owner,
    fault_slot,
    fault_face,
    normal_stress,
    friction,
    state_factor,
    shear_load,
):
    vmem = pl.BlockSpec(memory_space=pltpu.VMEM)
    scratch = [
        pltpu.VMEM((288, 128), F32),
        pltpu.VMEM((288, 256), F32),
        pltpu.VMEM((128, 256), F32),
        pltpu.VMEM((60, ELEMS), F32),
        pltpu.VMEM((60, ELEMS), F32),
        pltpu.VMEM((64, ELEMS), F32),
        pltpu.VMEM((192, ELEMS), BF16),
        pltpu.VMEM((160, ELEMS), F32),
        pltpu.VMEM((64, ELEMS), F32),
        pltpu.VMEM((160, ELEMS), F32),
        pltpu.VMEM((160, ELEMS), F32),
        pltpu.VMEM((160, ELEMS), F32),
        pltpu.VMEM((8, ELEMS), F32),
        pltpu.VMEM((CHUNKS * ROWS, 256), BF16),
        pltpu.VMEM((7, 256, BLOCK), BF16),
        pltpu.VMEM((2048, 128), BF16),
        pltpu.VMEM((2048, 256), F32),
        pltpu.VMEM((64, 128), F32),
        pltpu.VMEM((64, 128), F32),
        pltpu.VMEM((256, BLOCK), BF16),
        pltpu.VMEM((8, 256, BLOCK), BF16),
        pltpu.VMEM((32 * ROWS, 256), BF16),
        pltpu.VMEM((ITERS, 4, ROWS, 128), F32),
        pltpu.VMEM((ITERS, 4, ROWS, 128), F32),
        pltpu.VMEM((128, 128), F32),
        pltpu.VMEM((128, 128), F32),
        pltpu.VMEM((128, 128), F32),
        pltpu.VMEM((128, 128), F32),
        pltpu.VMEM((BLOCK, 2048), BF16),
        pltpu.VMEM((768, 128), F32),
        pltpu.VMEM((768, 128), F32),
        pltpu.VMEM((768, 128), F32),
        pltpu.VMEM((768, 128), F32),
        pltpu.VMEM((768, 128), F32),
        pltpu.VMEM((768, 128), F32),
        pltpu.VMEM((4, ROWS, BLOCK), F32),
        pltpu.VMEM((256, 128), F32),
        pltpu.VMEM((256, 128), F32),
        pltpu.VMEM((256, 128), F32),
        pltpu.VMEM((256, 128), F32),
        pltpu.VMEM((256, 128), F32),
        pltpu.VMEM((32, 2048), F32),
        pltpu.VMEM((384, 256), BF16),
        pltpu.SemaphoreType.DMA((ITERS, 4)),
        pltpu.SemaphoreType.DMA((ITERS, 4)),
    ] + [pltpu.SemaphoreType.DMA((PD,))] * 12
    displacement, residual, rate = pl.pallas_call(
        kernel,
        out_shape=(
            jax.ShapeDtypeStruct((60, 1, ELEMS), F32),
            jax.ShapeDtypeStruct((60, 1, ELEMS), F32),
            jax.ShapeDtypeStruct((12, 512), F32),
        ),
        in_specs=[vmem] * 15,
        out_specs=(vmem, vmem, vmem),
        scratch_shapes=scratch,
        compiler_params=pltpu.CompilerParams(collective_id=0, has_side_effects=True, vmem_limit_bytes=48 * 2**20),
        name="window",
    )(
        right_side.reshape(60, 1, ELEMS),
        shear_modulus.reshape(1, ELEMS),
        lame_lambda.reshape(1, ELEMS),
        stiff_shear,
        stiff_lame,
        face_interp,
        neighbours.reshape(8, 1, BLOCK),
        fault_count.reshape(1, 1),
        fault_owner.reshape(16, 1, 128),
        fault_slot.reshape(16, 1, 128),
        fault_face.reshape(16, 1, 128),
        normal_stress,
        friction,
        state_factor,
        shear_load,
    )
    return displacement.reshape(right_side.shape), residual.reshape(right_side.shape), rate


def solution(mesh):
    in_specs = (
        P(None, None, "along", "depth", None),
        P("along", "depth", None),
        P("along", "depth", None),
        P(),
        P(),
        P(),
        P("along", "depth", None),
        P("along", "depth"),
        P("along", "depth", None),
        P("along", "depth", None),
        P("along", "depth", None),
        P(None, ("along", "depth")),
        P(None, ("along", "depth")),
        P(None, ("along", "depth")),
        P(None, None, ("along", "depth")),
    )
    out_specs = (
        P(None, None, "along", "depth", None),
        P(None, None, "along", "depth", None),
        P(None, ("along", "depth")),
    )
    return jax.shard_map(
        on_device, mesh=mesh, in_specs=in_specs, out_specs=out_specs, check_vma=False
    )
```

```python
import functools

import jax
import jax.numpy as jnp
from jax import lax
from jax.experimental import pallas as pl
from jax.experimental.pallas import tpu as pltpu
from jax.sharding import PartitionSpec as P

ITERS = 4
NEWTON = 6
DAMPING = 0.5
TIME_STEP = 0.5
LOWER_EDGE = 0.25
UPPER_EDGE = 5.0
CENTER = 0.5 * (UPPER_EDGE + LOWER_EDGE)
SPREAD = 0.5 * (UPPER_EDGE - LOWER_EDGE)

MESH = pl.DeviceIdType.MESH
F32 = jnp.float32
BF16 = jnp.bfloat16
NT = (((1,), (1,)), ((), ()))

PA, PD = 8, 16
DEVS = PA * PD
ELEMS = 1024
ROWS = 40
BLOCK = 512
CHUNKS = 28
RANKS = 16


def coefficients():
    ratio = CENTER / SPREAD
    rho = 1.0 / ratio
    pairs = []
    for _ in range(ITERS):
        rho_next = 1.0 / (2.0 * ratio - rho)
        pairs.append((rho_next * rho, 2.0 * rho_next / SPREAD))
        rho = rho_next
    return pairs


def halves(value):
    high = value.astype(BF16)
    return high, (value - high.astype(F32)).astype(BF16)


def product(left, right):
    return jnp.dot(left, right, preferred_element_type=F32)


def onehot(digit, rows, columns):
    return (lax.broadcasted_iota(jnp.int32, (rows, columns), 0) == digit).astype(F32)


def choose(result, chunk, count, rows):
    width = result.shape[1]
    index = jnp.broadcast_to(chunk, (8, width))
    total = jnp.zeros((rows // 8, 8, width), F32)
    for s in range(count):
        part = result[s * rows : (s + 1) * rows].reshape(rows // 8, 8, width)
        total = jnp.where((index == s)[None], part, total)
    return total.reshape(rows, width)


def inverse_sinh(size, root):
    magnitude = jnp.log(jnp.abs(size) + root)
    return jnp.where(size < 0.0, -magnitude, magnitude)


def kernel(
    count_ref, load_hbm, shear_hbm, lame_hbm, stiff_shear_hbm, stiff_lame_hbm, interp_hbm, links_hbm, owner_hbm,
    slot_hbm, face_hbm, normal_hbm, friction_hbm, state_hbm, shear_load_hbm,
    disp_ref, residual_ref, rate_ref,
    load, shear_ref, lame_ref, stiff_shear, stiff_lame, interp, links, owner_ref, slot_ref, face_ref,
    normal_ref, friction_ref, state_ref, shear_load, fetch_sem,
    weight, weights, lift_pair, solved, left_over, field, stacked, trace, image, gathered, flux, flux_sum, alpha,
    table, hot_links, hot_owner, prefix, send_maps, face_maps, hot_send, hot_face, table_send, halo, rims,
    ids_out, ids_one, ids_mid, ids_in, hot_grid, params_pack, params_out, params_one, params_mid, params_in, params,
    tractions, rate_pack, rate_out, rate_one, rate_mid, rate_in, wide, table_back,
    halo_send, halo_recv, ids_a, ids_b, ids_c, ids_d, par_a, par_b, par_c, par_d, rate_a, rate_b, rate_c, rate_d,
):
    along = lax.axis_index("along")
    depth = lax.axis_index("depth")

    operands = (
        (owner_hbm, owner_ref), (slot_hbm, slot_ref), (face_hbm, face_ref), (load_hbm, load), (shear_hbm, shear_ref),
        (lame_hbm, lame_ref), (stiff_shear_hbm, stiff_shear), (stiff_lame_hbm, stiff_lame), (interp_hbm, interp),
        (links_hbm, links), (normal_hbm, normal_ref), (friction_hbm, friction_ref), (state_hbm, state_ref),
        (shear_load_hbm, shear_load),
    )
    fetches = [
        pltpu.make_async_copy(source, target, fetch_sem.at[i]) for i, (source, target) in enumerate(operands)
    ]
    for fetch in fetches:
        fetch.start()

    barrier = pltpu.get_barrier_semaphore()
    for i in range(1, PA):
        pl.semaphore_signal(barrier, inc=1, device_id=(lax.rem(along + i, PA), depth), device_id_type=MESH)
    for i in range(1, PD):
        pl.semaphore_signal(barrier, inc=1, device_id=(along, lax.rem(depth + i, PD)), device_id_type=MESH)

    def row_copy(i, source, landing, size, sems, sending):
        peer = lax.rem(along + i, PA) if sending else lax.rem(along + PA - i, PA)
        place = along if sending else peer
        return pltpu.make_async_remote_copy(
            src_ref=source.at[pl.ds(pl.multiple_of(peer * size, 8), size)],
            dst_ref=landing.at[pl.ds(pl.multiple_of(place * size, 8), size)],
            send_sem=sems[0].at[i],
            recv_sem=sems[1].at[i],
            device_id=(peer, depth),
            device_id_type=MESH,
        )

    def column_copy(i, source, landing, size, sems, sending):
        peer = lax.rem(depth + i, PD) if sending else lax.rem(depth + PD - i, PD)
        place = depth if sending else peer
        return pltpu.make_async_remote_copy(
            src_ref=source.at[pl.ds(pl.multiple_of(peer * size, 8), size)],
            dst_ref=landing.at[pl.ds(pl.multiple_of(place * size, 8), size)],
            send_sem=sems[0].at[i],
            recv_sem=sems[1].at[i],
            device_id=(along, peer),
            device_id_type=MESH,
        )

    def go(kind, source, landing, size, sems):
        mine, peers = (along, PA) if kind is row_copy else (depth, PD)
        for i in range(1, peers):
            kind(i, source, landing, size, sems, True).start()
        own = pl.ds(pl.multiple_of(mine * size, 8), size)
        landing[own, :] = source[own, :]

    def arrive(kind, source, landing, size, sems):
        for i in range(1, PA if kind is row_copy else PD):
            kind(i, source, landing, size, sems, False).wait_recv()

    def drain(kind, source, landing, size, sems):
        for i in range(1, PA if kind is row_copy else PD):
            kind(i, source, landing, size, sems, True).wait_send()

    ids_first = (row_copy, ids_out, ids_one, 16, (ids_a, ids_b))
    ids_second = (column_copy, ids_mid, ids_in, 8, (ids_c, ids_d))
    params_first = (column_copy, params_out, params_one, 48, (par_a, par_b))
    params_second = (row_copy, params_mid, params_in, 96, (par_c, par_d))
    rate_first = (row_copy, rate_out, rate_one, 32, (rate_a, rate_b))
    rate_second = (column_copy, rate_mid, rate_in, 16, (rate_c, rate_d))

    for fetch in fetches[0:3]:
        fetch.wait()
    count = count_ref[...]
    lane = lax.broadcasted_iota(jnp.int32, (1, 128), 1)
    for t in range(RANKS):
        live = (lane + t * 128) < count
        owner = jnp.where(live, owner_ref[t], -1)
        hot_owner[t * 128 : (t + 1) * 128, :] = onehot(owner, 128, 128).astype(BF16)
    row = lax.broadcasted_iota(jnp.int32, (128, 256), 0)
    column = lax.broadcasted_iota(jnp.int32, (128, 256), 1)
    earlier = ((row < column) | (column >= 128)).astype(F32).astype(BF16)
    prefix[...] = product(hot_owner[...], earlier)
    base = jnp.zeros((128, 128), F32)
    sent = jnp.zeros((64, 128), F32)
    placed = jnp.zeros((64, 128), F32)
    for t in range(RANKS):
        rows = slice(t * 128, (t + 1) * 128)
        hot = hot_owner[rows, :]
        rank = jnp.sum(hot.astype(F32) * (prefix[rows, 0:128] + base), axis=0, keepdims=True)
        base = base + prefix[rows, 128:256]
        live = ((lane + t * 128) < count).astype(F32)
        rank_live = jnp.where(live > 0.0, rank, -1.0).astype(jnp.int32)
        face = face_ref[t]
        slot = slot_ref[t]
        face_high = lax.shift_right_logical(face, 7)
        face_low = jnp.bitwise_and(face, 127)
        ranks = onehot(rank_live, RANKS, 128)
        values = jnp.concatenate(
            [
                ranks * face_high.astype(F32),
                ranks * face_low.astype(F32),
                ranks * (lax.shift_right_logical(slot, 4) + 1).astype(F32),
                ranks * jnp.bitwise_and(slot, 15).astype(F32),
            ],
            axis=0,
        ).astype(BF16)
        sent = sent + lax.dot_general(values, hot, NT, preferred_element_type=F32)
        highs = onehot(face_high, 32, 128) * live
        values = jnp.concatenate([highs * (rank + 1.0), highs * owner_ref[t].astype(F32)], axis=0).astype(BF16)
        lows = onehot(face_low, 128, 128).astype(BF16)
        placed = placed + lax.dot_general(values, lows, NT, preferred_element_type=F32)
    send_maps[...] = sent
    face_maps[...] = placed
    ids = 16.0 * sent[32:48] + sent[48:64] - 16.0
    ids_out[...] = jnp.transpose(jnp.concatenate([ids, jnp.zeros((112, 128), F32)], axis=0))

    pl.semaphore_wait(barrier, PA + PD - 2)
    go(*ids_first)

    sides = (
        (0, 1, (along + 1, depth), along < PA - 1, along > 0),
        (1, 0, (along - 1, depth), along > 0, along < PA - 1),
        (2, 3, (along, depth + 1), depth < PD - 1, depth > 0),
        (3, 2, (along, depth - 1), depth > 0, depth < PD - 1),
    )

    for side, piece, target, sends, receives in sides:
        @pl.when(jnp.logical_not(receives))
        def _():
            halo[:, side] = jnp.zeros((ITERS, ROWS, 128), F32)

    for fetch in fetches[3:]:
        fetch.wait()
    weight[...] = jnp.zeros_like(weight)
    for f in range(4):
        for c in range(3):
            weight[f * ROWS + c * 12 : f * ROWS + c * 12 + 12, c * 20 : c * 20 + 20] = interp[:, f, :]
    weight[160:220, 0:60] = stiff_shear[...]
    weight[224:284, 0:60] = stiff_lame[...]
    whole = weight[:, 0:64]
    high = whole.astype(BF16).astype(F32)
    rest = whole - high
    lift_pair[0:128, 0:128] = jnp.transpose(weight[0:128, :])
    lift_pair[0:128, 128:256] = jnp.transpose(weight[128:256, :])
    weights[:, 0:64] = high
    weights[:, 64:128] = high
    weights[:, 128:192] = rest
    lifter, lifter_rest = halves(lift_pair[0:64, 0:160])
    matrix = weights[:, 0:192].astype(BF16)

    shear = shear_ref[...]
    lame = lame_ref[...]
    material = lame + 2.0 * shear
    inverse = 1.0 / material

    def lifted(ref):
        high, low = halves(ref[...])
        return product(lifter, high) + product(lifter_rest, high) + product(lifter, low)

    def build_links(b, carry):
        slots = links[b + b // 6]
        hot = onehot(jnp.bitwise_and(slots, 127), 128, BLOCK).astype(BF16)
        hot_links[b, 0:128, :] = hot
        hot_links[b, 128:256, :] = hot
        return carry

    right = load[...].reshape(60, ELEMS)
    left_over[...] = right
    field[60:64, :] = jnp.zeros((4, ELEMS), F32)
    field[0:60, :] = right * (inverse * (1.0 / CENTER))
    solved[...] = jnp.zeros_like(solved)
    flux_sum[...] = jnp.zeros_like(flux_sum)

    def halo_copy(i, side, piece, target):
        return pltpu.make_async_remote_copy(
            src_ref=rims.at[i, piece],
            dst_ref=halo.at[i, side],
            send_sem=halo_send.at[i, side],
            recv_sem=halo_recv.at[i, side],
            device_id=target,
            device_id_type=MESH,
        )

    def step(i, scale_old, scale_new, between):
        first = i == 0
        now = field[...]
        high, low = halves(now)
        stacked[0:64, :] = high
        stacked[64:128, :] = low
        stacked[128:192, :] = high
        trace[...] = product(matrix[0:160], stacked[...])
        if first:
            for f in range(4):
                trace[f * ROWS + 36 : f * ROWS + 37, :] = material
        for side, piece, target, sends, receives in sides:
            rims[i, piece] = trace[120:160, piece * 128 : piece * 128 + 128]

            @pl.when(sends)
            def _():
                halo_copy(i, side, piece, target).start()

        if first:
            lax.fori_loop(0, 7, build_links, 0)

        for p in range(CHUNKS // 2):
            parts = []
            for s in (2 * p, 2 * p + 1):
                t = s if s < 24 else s + 4
                f, j = t // 8, t % 8
                parts.append(trace[f * ROWS : (f + 1) * ROWS, j * 128 : (j + 1) * 128])
            high, low = halves(jnp.concatenate(parts, axis=0))
            table[p * 80 : p * 80 + 80, 0:128] = high
            table[p * 80 : p * 80 + 80, 128:256] = low

        def block(b, carry):
            place = b + b // 6
            chunk = lax.shift_right_logical(links[place], 7)
            chunk = jnp.where(chunk >= 24, chunk - 4, chunk)
            result = product(table[...], hot_links[b])
            f = place // 2
            half = place - 2 * f
            gathered[
                pl.ds(pl.multiple_of(f * ROWS, 8), ROWS), pl.ds(pl.multiple_of(half * BLOCK, BLOCK), BLOCK)
            ] = choose(result, chunk, CHUNKS, ROWS)
            return carry

        lax.fori_loop(0, 7, block, 0)

        volume = product(matrix[160:288], stacked[...])
        image[...] = shear * volume[0:64] + lame * volume[64:128]
        solved[...] = solved[...] + now[0:60]
        between()

        for side, piece, target, sends, receives in sides:
            @pl.when(receives)
            def _():
                halo_copy(i, side, piece, target).wait_recv()
            gathered[120:160, side * 128 : side * 128 + 128] = halo[i, side]

        if first:
            for f in range(4):
                alpha[f : f + 1, :] = 0.5 * (material + gathered[f * ROWS + 36 : f * ROWS + 37, :])
        for f in range(4):
            rows = slice(f * ROWS, (f + 1) * ROWS)
            value = alpha[f : f + 1, :] * (trace[rows, :] - gathered[rows, :])
            flux[rows, :] = value
            flux_sum[rows, :] = flux_sum[rows, :] + value
        left = left_over[...] - (image[...] + lifted(flux))[0:60]
        left_over[...] = left
        if i < ITERS - 1:
            field[0:60, :] = scale_old * now[0:60] + scale_new * (left * inverse)

    def nothing():
        pass

    def ids_middle():
        arrive(*ids_first)
        for a in range(PA):
            ids_mid[pl.ds(a, PD, stride=PA), :] = ids_one[a * PD : (a + 1) * PD, :]
        go(*ids_second)

    def answer():
        arrive(*ids_second)
        asked = jnp.transpose(ids_in[...])[0:RANKS].astype(jnp.int32)
        for rank in range(RANKS):
            hot_grid[:, rank * 128 : (rank + 1) * 128] = onehot(asked[rank : rank + 1], BLOCK, 128).astype(BF16)
        owned = jnp.concatenate(
            [normal_ref[...] * friction_ref[...], state_ref[...], shear_load[:, 0, :], shear_load[:, 1, :]], axis=0
        )
        high = owned.astype(BF16).astype(F32)
        both = product(jnp.concatenate([high, owned - high], axis=0).astype(BF16), hot_grid[...])
        for rank in range(RANKS):
            lanes = slice(rank * 128, (rank + 1) * 128)
            params_pack[rank * 48 : (rank + 1) * 48, :] = both[0:48, lanes] + both[48:96, lanes]
        for j in range(6):
            params_out[pl.ds(j, 128, stride=6), :] = jnp.transpose(params_pack[j * 128 : (j + 1) * 128, :])
        go(*params_first)

    def params_middle():
        arrive(*params_first)
        for d in range(PD):
            for j in range(6):
                params_mid[pl.ds(d * 6 + j, PA, stride=96), :] = params_one[pl.ds(d * 48 + j, PA, stride=6), :]
        go(*params_second)

    pairs = coefficients()
    step(0, *pairs[0], ids_middle)
    step(1, *pairs[1], answer)
    step(2, *pairs[2], nothing)
    step(3, *pairs[3], params_middle)
    residual_ref[...] = left_over[...].reshape(60, 1, ELEMS)

    for p in range(16):
        parts = []
        for s in (2 * p, 2 * p + 1):
            f, j = s // 8, s % 8
            parts.append(flux_sum[f * ROWS : (f + 1) * ROWS, j * 128 : (j + 1) * 128])
        high, low = halves(jnp.concatenate(parts, axis=0))
        table_send[p * 80 : p * 80 + 80, 0:128] = high
        table_send[p * 80 : p * 80 + 80, 128:256] = low
    for b in range(4):
        high = jnp.concatenate([send_maps[4 * b + j : 4 * b + j + 1, :] for j in range(4)], axis=1)
        low = jnp.concatenate([send_maps[16 + 4 * b + j : 17 + 4 * b + j, :] for j in range(4)], axis=1)
        hot = onehot(low.astype(jnp.int32), 128, BLOCK).astype(BF16)
        hot_send[0:128, :] = hot
        hot_send[128:256, :] = hot
        result = product(table_send[...], hot_send[...])
        tractions[b] = choose(result, high.astype(jnp.int32), 32, ROWS)

    def build_face(b, carry):
        low = jnp.concatenate([face_maps[pl.ds(32 + 4 * b + j, 1), :] for j in range(4)], axis=1)
        hot = onehot(low.astype(jnp.int32), 128, BLOCK).astype(BF16)
        hot_face[b, 0:128, :] = hot
        hot_face[b, 128:256, :] = hot
        return carry

    lax.fori_loop(0, 8, build_face, 0)
    rate_pack[...] = jnp.zeros_like(rate_pack)

    arrive(*params_second)
    for j in range(6):
        params[j * 128 : (j + 1) * 128, :] = jnp.transpose(params_in[pl.ds(j, 128, stride=6), :])
    for b in range(4):
        first = [params[(4 * b + j) * 48 : (4 * b + j + 1) * 48, :] for j in range(4)]
        owned = jnp.concatenate(first, axis=1)
        traction = tractions[b]
        state = owned[12:24]
        strike = owned[24:36] + traction[0:12]
        updip = owned[36:48] + traction[12:24]
        magnitude = jnp.sqrt(strike * strike + updip * updip)
        resist = owned[0:12] * (1.0 + 0.5 * jnp.tanh(traction[24:36]))
        steep = resist * state
        velocity = magnitude / (DAMPING + steep)
        for _ in range(NEWTON - 1):
            scaled = state * velocity
            square = 1.0 + scaled * scaled
            inverse_root = lax.rsqrt(square)
            misfit = magnitude - DAMPING * velocity - resist * inverse_sinh(scaled, square * inverse_root)
            velocity = velocity + misfit / (DAMPING + steep * inverse_root)
        factor = TIME_STEP * velocity / jnp.maximum(magnitude, 1.0)
        slip = jnp.concatenate([factor * strike, factor * updip], axis=0)
        for j in range(4):
            rank = 4 * b + j
            rate_pack[rank * 16 : rank * 16 + 12, :] = velocity[:, j * 128 : (j + 1) * 128]
        for j in (0, 2):
            parts = [slip[:, j * 128 : (j + 1) * 128], slip[:, (j + 1) * 128 : (j + 2) * 128]]
            high, low = halves(jnp.concatenate(parts, axis=0))
            at = (4 * b + j) * 24
            table_back[at : at + 48, 0:128] = high
            table_back[at : at + 48, 128:256] = low
    for j in range(2):
        rate_out[pl.ds(j, 128, stride=2), :] = jnp.transpose(rate_pack[j * 128 : (j + 1) * 128, :])
    go(*rate_first)

    flux[...] = jnp.zeros_like(flux)

    def place_back(b, carry):
        rank = jnp.concatenate([face_maps[pl.ds(4 * b + j, 1), :] for j in range(4)], axis=1)
        result = product(table_back[...], hot_face[b])
        f = b // 2
        half = b - 2 * f
        flux[
            pl.ds(pl.multiple_of(f * ROWS, 8), 24), pl.ds(pl.multiple_of(half * BLOCK, BLOCK), BLOCK)
        ] = choose(result, rank.astype(jnp.int32) - 1, RANKS, 24)
        return carry

    lax.fori_loop(0, 8, place_back, 0)

    arrive(*rate_first)
    for a in range(PA):
        for j in range(2):
            rate_mid[pl.ds(a * 2 + j, PD, stride=16), :] = rate_one[pl.ds(a * 32 + j, PD, stride=2), :]
    go(*rate_second)
    disp_ref[...] = (solved[...] + 0.5 * lifted(flux)[0:60]).reshape(60, 1, ELEMS)
    for each in (ids_first, ids_second, params_first, params_second, rate_first):
        drain(*each)
    for i in range(ITERS):
        for side, piece, target, sends, receives in sides:
            @pl.when(sends)
            def _():
                halo_copy(i, side, piece, target).wait_send()

    arrive(*rate_second)
    for j in range(2):
        value = jnp.transpose(rate_in[pl.ds(j, 128, stride=2), :])
        high = value.astype(BF16).astype(F32)
        low = value - high
        for r in range(8):
            lanes = slice((8 * j + r) * 128, (8 * j + r + 1) * 128)
            wide[0:16, lanes] = high[r * 16 : (r + 1) * 16]
            wide[16:32, lanes] = low[r * 16 : (r + 1) * 16]
    both = lax.dot_general(wide[...].astype(BF16), hot_grid[...], NT, preferred_element_type=F32)
    rate_ref[...] = both[0:12] + both[16:28]
    drain(*rate_second)


def on_device(
    right_side,
    shear_modulus,
    lame_lambda,
    stiff_shear,
    stiff_lame,
    face_interp,
    neighbours,
    fault_count,
    fault_owner,
    fault_slot,
    fault_face,
    normal_stress,
    friction,
    state_factor,
    shear_load,
):
    vmem = pl.BlockSpec(memory_space=pltpu.VMEM)
    hbm = pl.BlockSpec(memory_space=pltpu.HBM)
    scratch = [
        pltpu.VMEM((60, 1, ELEMS), F32),
        pltpu.VMEM((1, ELEMS), F32),
        pltpu.VMEM((1, ELEMS), F32),
        pltpu.VMEM((60, 60), F32),
        pltpu.VMEM((60, 60), F32),
        pltpu.VMEM((12, 4, 20), F32),
        pltpu.VMEM((8, 1, BLOCK), jnp.int32),
        pltpu.VMEM((16, 1, 128), jnp.int32),
        pltpu.VMEM((16, 1, 128), jnp.int32),
        pltpu.VMEM((16, 1, 128), jnp.int32),
        pltpu.VMEM((12, 512), F32),
        pltpu.VMEM((12, 512), F32),
        pltpu.VMEM((12, 512), F32),
        pltpu.VMEM((12, 2, 512), F32),
        pltpu.SemaphoreType.DMA((14,)),
        pltpu.VMEM((288, 128), F32),
        pltpu.VMEM((288, 256), F32),
        pltpu.VMEM((128, 256), F32),
        pltpu.VMEM((60, ELEMS), F32),
        pltpu.VMEM((60, ELEMS), F32),
        pltpu.VMEM((64, ELEMS), F32),
        pltpu.VMEM((192, ELEMS), BF16),
        pltpu.VMEM((160, ELEMS), F32),
        pltpu.VMEM((64, ELEMS), F32),
        pltpu.VMEM((160, ELEMS), F32),
        pltpu.VMEM((160, ELEMS), F32),
        pltpu.VMEM((160, ELEMS), F32),
        pltpu.VMEM((8, ELEMS), F32),
        pltpu.VMEM((CHUNKS * ROWS, 256), BF16),
        pltpu.VMEM((7, 256, BLOCK), BF16),
        pltpu.VMEM((2048, 128), BF16),
        pltpu.VMEM((2048, 256), F32),
        pltpu.VMEM((64, 128), F32),
        pltpu.VMEM((64, 128), F32),
        pltpu.VMEM((256, BLOCK), BF16),
        pltpu.VMEM((8, 256, BLOCK), BF16),
        pltpu.VMEM((32 * ROWS, 256), BF16),
        pltpu.VMEM((ITERS, 4, ROWS, 128), F32),
        pltpu.VMEM((ITERS, 4, ROWS, 128), F32),
        pltpu.VMEM((128, 128), F32),
        pltpu.VMEM((128, 128), F32),
        pltpu.VMEM((128, 128), F32),
        pltpu.VMEM((128, 128), F32),
        pltpu.VMEM((BLOCK, 2048), BF16),
        pltpu.VMEM((768, 128), F32),
        pltpu.VMEM((768, 128), F32),
        pltpu.VMEM((768, 128), F32),
        pltpu.VMEM((768, 128), F32),
        pltpu.VMEM((768, 128), F32),
        pltpu.VMEM((768, 128), F32),
        pltpu.VMEM((4, ROWS, BLOCK), F32),
        pltpu.VMEM((256, 128), F32),
        pltpu.VMEM((256, 128), F32),
        pltpu.VMEM((256, 128), F32),
        pltpu.VMEM((256, 128), F32),
        pltpu.VMEM((256, 128), F32),
        pltpu.VMEM((32, 2048), F32),
        pltpu.VMEM((384, 256), BF16),
        pltpu.SemaphoreType.DMA((ITERS, 4)),
        pltpu.SemaphoreType.DMA((ITERS, 4)),
    ] + [pltpu.SemaphoreType.DMA((PD,))] * 12
    displacement, residual, rate = pl.pallas_call(
        kernel,
        out_shape=(
            jax.ShapeDtypeStruct((60, 1, ELEMS), F32),
            jax.ShapeDtypeStruct((60, 1, ELEMS), F32),
            jax.ShapeDtypeStruct((12, 512), F32),
        ),
        in_specs=[vmem] + [hbm] * 14,
        out_specs=(vmem, vmem, vmem),
        scratch_shapes=scratch,
        compiler_params=pltpu.CompilerParams(collective_id=0, has_side_effects=True, vmem_limit_bytes=64000 * 1024),
        name="window",
    )(
        fault_count.reshape(1, 1),
        right_side.reshape(60, 1, ELEMS),
        shear_modulus.reshape(1, ELEMS),
        lame_lambda.reshape(1, ELEMS),
        stiff_shear,
        stiff_lame,
        face_interp,
        neighbours.reshape(8, 1, BLOCK),
        fault_owner.reshape(16, 1, 128),
        fault_slot.reshape(16, 1, 128),
        fault_face.reshape(16, 1, 128),
        normal_stress,
        friction,
        state_factor,
        shear_load.transpose(1, 0, 2),
    )
    return displacement.reshape(right_side.shape), residual.reshape(right_side.shape), rate


def solution(mesh):
    in_specs = (
        P(None, None, "along", "depth", None),
        P("along", "depth", None),
        P("along", "depth", None),
        P(),
        P(),
        P(),
        P("along", "depth", None),
        P("along", "depth"),
        P("along", "depth", None),
        P("along", "depth", None),
        P("along", "depth", None),
        P(None, ("along", "depth")),
        P(None, ("along", "depth")),
        P(None, ("along", "depth")),
        P(None, None, ("along", "depth")),
    )
    out_specs = (
        P(None, None, "along", "depth", None),
        P(None, None, "along", "depth", None),
        P(None, ("along", "depth")),
    )
    return jax.shard_map(
        on_device, mesh=mesh, in_specs=in_specs, out_specs=out_specs, check_vma=False
    )
```

```python
import functools

import jax
import jax.numpy as jnp
from jax import lax
from jax.experimental import pallas as pl
from jax.experimental.pallas import tpu as pltpu
from jax.sharding import PartitionSpec as P

ITERS = 4
NEWTON = 6
DAMPING = 0.5
TIME_STEP = 0.5
LOWER_EDGE = 0.25
UPPER_EDGE = 5.0
CENTER = 0.5 * (UPPER_EDGE + LOWER_EDGE)
SPREAD = 0.5 * (UPPER_EDGE - LOWER_EDGE)

MESH = pl.DeviceIdType.MESH
F32 = jnp.float32
BF16 = jnp.bfloat16
NT = (((1,), (1,)), ((), ()))

PA, PD = 8, 16
DEVS = PA * PD
ELEMS = 1024
ROWS = 40
BLOCK = 512
CHUNKS = 28
RANKS = 16


def coefficients():
    ratio = CENTER / SPREAD
    rho = 1.0 / ratio
    pairs = []
    for _ in range(ITERS):
        rho_next = 1.0 / (2.0 * ratio - rho)
        pairs.append((rho_next * rho, 2.0 * rho_next / SPREAD))
        rho = rho_next
    return pairs


def halves(value):
    high = value.astype(BF16)
    return high, (value - high.astype(F32)).astype(BF16)


def product(left, right):
    return jnp.dot(left, right, preferred_element_type=F32)


def onehot(digit, rows, columns):
    return (lax.broadcasted_iota(jnp.int32, (rows, columns), 0) == digit).astype(F32)


def choose(result, chunk, count, rows):
    width = result.shape[1]
    index = jnp.broadcast_to(chunk, (8, width))
    total = jnp.zeros((rows // 8, 8, width), F32)
    for s in range(count):
        part = result[s * rows : (s + 1) * rows].reshape(rows // 8, 8, width)
        total = jnp.where((index == s)[None], part, total)
    return total.reshape(rows, width)


def inverse_sinh(size, root):
    magnitude = jnp.log(jnp.abs(size) + root)
    return jnp.where(size < 0.0, -magnitude, magnitude)


def kernel(
    count_ref, load_hbm, shear_hbm, lame_hbm, stiff_shear_hbm, stiff_lame_hbm, interp_hbm, links_hbm, owner_hbm,
    slot_hbm, face_hbm, normal_hbm, friction_hbm, state_hbm, shear_load_hbm,
    disp_hbm, residual_hbm, rate_hbm,
    disp_ref, residual_ref, rate_ref, result_sem,
    load, shear_ref, lame_ref, stiff_shear, stiff_lame, interp, links, owner_ref, slot_ref, face_ref,
    normal_ref, friction_ref, state_ref, shear_load, fetch_sem,
    weight, weights, lift_pair, solved, left_over, field, stacked, trace, image, gathered, flux, flux_sum, alpha,
    table, hot_links, hot_owner, prefix, send_maps, face_maps, hot_send, hot_face, table_send, halo, rims,
    ids_out, ids_one, ids_mid, ids_in, hot_grid, params_pack, down_out, down_one, down_mid, down_in, over_out,
    over_one, over_mid, over_in, params,
    tractions, rate_pack, rate_out, rate_one, rate_mid, rate_in, wide, table_back,
    halo_send, halo_recv, ids_a, ids_b, ids_c, ids_d, par_a, par_b, par_c, par_d, par_e, par_f, par_g, par_h,
    rate_a, rate_b, rate_c, rate_d,
):
    along = lax.axis_index("along")
    depth = lax.axis_index("depth")

    operands = (
        (owner_hbm, owner_ref), (slot_hbm, slot_ref), (face_hbm, face_ref), (load_hbm, load), (shear_hbm, shear_ref),
        (lame_hbm, lame_ref), (stiff_shear_hbm, stiff_shear), (stiff_lame_hbm, stiff_lame), (interp_hbm, interp),
        (links_hbm, links), (normal_hbm, normal_ref), (friction_hbm, friction_ref), (state_hbm, state_ref),
        (shear_load_hbm, shear_load),
    )
    fetches = [
        pltpu.make_async_copy(source, target, fetch_sem.at[i]) for i, (source, target) in enumerate(operands)
    ]
    for fetch in fetches:
        fetch.start()

    results = [
        pltpu.make_async_copy(source, target, result_sem.at[i])
        for i, (source, target) in enumerate(
            ((residual_ref, residual_hbm), (disp_ref, disp_hbm), (rate_ref, rate_hbm))
        )
    ]

    barrier = pltpu.get_barrier_semaphore()
    for i in range(1, PA):
        pl.semaphore_signal(barrier, inc=1, device_id=(lax.rem(along + i, PA), depth), device_id_type=MESH)
    for i in range(1, PD):
        pl.semaphore_signal(barrier, inc=1, device_id=(along, lax.rem(depth + i, PD)), device_id_type=MESH)

    def row_copy(i, source, landing, size, sems, sending):
        peer = lax.rem(along + i, PA) if sending else lax.rem(along + PA - i, PA)
        place = along if sending else peer
        return pltpu.make_async_remote_copy(
            src_ref=source.at[pl.ds(pl.multiple_of(peer * size, 8), size)],
            dst_ref=landing.at[pl.ds(pl.multiple_of(place * size, 8), size)],
            send_sem=sems[0].at[i],
            recv_sem=sems[1].at[i],
            device_id=(peer, depth),
            device_id_type=MESH,
        )

    def column_copy(i, source, landing, size, sems, sending):
        peer = lax.rem(depth + i, PD) if sending else lax.rem(depth + PD - i, PD)
        place = depth if sending else peer
        return pltpu.make_async_remote_copy(
            src_ref=source.at[pl.ds(pl.multiple_of(peer * size, 8), size)],
            dst_ref=landing.at[pl.ds(pl.multiple_of(place * size, 8), size)],
            send_sem=sems[0].at[i],
            recv_sem=sems[1].at[i],
            device_id=(along, peer),
            device_id_type=MESH,
        )

    def go(kind, source, landing, size, sems):
        mine, peers = (along, PA) if kind is row_copy else (depth, PD)
        for i in range(1, peers):
            kind(i, source, landing, size, sems, True).start()
        own = pl.ds(pl.multiple_of(mine * size, 8), size)
        landing[own, :] = source[own, :]

    def arrive(kind, source, landing, size, sems):
        for i in range(1, PA if kind is row_copy else PD):
            kind(i, source, landing, size, sems, False).wait_recv()

    def drain(kind, source, landing, size, sems):
        for i in range(1, PA if kind is row_copy else PD):
            kind(i, source, landing, size, sems, True).wait_send()

    ids_first = (row_copy, ids_out, ids_one, 16, (ids_a, ids_b))
    ids_second = (column_copy, ids_mid, ids_in, 8, (ids_c, ids_d))
    down_first = (column_copy, down_out, down_one, 24, (par_a, par_b))
    down_second = (row_copy, down_mid, down_in, 48, (par_c, par_d))
    over_first = (row_copy, over_out, over_one, 48, (par_e, par_f))
    over_second = (column_copy, over_mid, over_in, 24, (par_g, par_h))
    rate_first = (row_copy, rate_out, rate_one, 32, (rate_a, rate_b))
    rate_second = (column_copy, rate_mid, rate_in, 16, (rate_c, rate_d))

    for fetch in fetches[0:3]:
        fetch.wait()
    count = count_ref[...]
    lane = lax.broadcasted_iota(jnp.int32, (1, 128), 1)
    for t in range(RANKS):
        live = (lane + t * 128) < count
        owner = jnp.where(live, owner_ref[t], -1)
        hot_owner[t * 128 : (t + 1) * 128, :] = onehot(owner, 128, 128).astype(BF16)
    row = lax.broadcasted_iota(jnp.int32, (128, 256), 0)
    column = lax.broadcasted_iota(jnp.int32, (128, 256), 1)
    earlier = ((row < column) | (column >= 128)).astype(F32).astype(BF16)
    prefix[...] = product(hot_owner[...], earlier)
    base = jnp.zeros((128, 128), F32)
    sent = jnp.zeros((64, 128), F32)
    placed = jnp.zeros((64, 128), F32)
    for t in range(RANKS):
        rows = slice(t * 128, (t + 1) * 128)
        hot = hot_owner[rows, :]
        rank = jnp.sum(hot.astype(F32) * (prefix[rows, 0:128] + base), axis=0, keepdims=True)
        base = base + prefix[rows, 128:256]
        live = ((lane + t * 128) < count).astype(F32)
        rank_live = jnp.where(live > 0.0, rank, -1.0).astype(jnp.int32)
        face = face_ref[t]
        slot = slot_ref[t]
        face_high = lax.shift_right_logical(face, 7)
        face_low = jnp.bitwise_and(face, 127)
        ranks = onehot(rank_live, RANKS, 128)
        values = jnp.concatenate(
            [
                ranks * face_high.astype(F32),
                ranks * face_low.astype(F32),
                ranks * (lax.shift_right_logical(slot, 4) + 1).astype(F32),
                ranks * jnp.bitwise_and(slot, 15).astype(F32),
            ],
            axis=0,
        ).astype(BF16)
        sent = sent + lax.dot_general(values, hot, NT, preferred_element_type=F32)
        highs = onehot(face_high, 32, 128) * live
        values = jnp.concatenate([highs * (rank + 1.0), highs * owner_ref[t].astype(F32)], axis=0).astype(BF16)
        lows = onehot(face_low, 128, 128).astype(BF16)
        placed = placed + lax.dot_general(values, lows, NT, preferred_element_type=F32)
    send_maps[...] = sent
    face_maps[...] = placed
    ids = 16.0 * sent[32:48] + sent[48:64] - 16.0
    ids_out[...] = jnp.transpose(jnp.concatenate([ids, jnp.zeros((112, 128), F32)], axis=0))

    pl.semaphore_wait(barrier, PA + PD - 2)
    go(*ids_first)

    sides = (
        (0, 1, (along + 1, depth), along < PA - 1, along > 0),
        (1, 0, (along - 1, depth), along > 0, along < PA - 1),
        (2, 3, (along, depth + 1), depth < PD - 1, depth > 0),
        (3, 2, (along, depth - 1), depth > 0, depth < PD - 1),
    )

    for side, piece, target, sends, receives in sides:
        @pl.when(jnp.logical_not(receives))
        def _():
            halo[:, side] = jnp.zeros((ITERS, ROWS, 128), F32)

    for fetch in fetches[3:]:
        fetch.wait()
    weight[...] = jnp.zeros_like(weight)
    for f in range(4):
        for c in range(3):
            weight[f * ROWS + c * 12 : f * ROWS + c * 12 + 12, c * 20 : c * 20 + 20] = interp[:, f, :]
    weight[160:220, 0:60] = stiff_shear[...]
    weight[224:284, 0:60] = stiff_lame[...]
    whole = weight[:, 0:64]
    high = whole.astype(BF16).astype(F32)
    rest = whole - high
    lift_pair[0:128, 0:128] = jnp.transpose(weight[0:128, :])
    lift_pair[0:128, 128:256] = jnp.transpose(weight[128:256, :])
    weights[:, 0:64] = high
    weights[:, 64:128] = high
    weights[:, 128:192] = rest
    lifter, lifter_rest = halves(lift_pair[0:64, 0:160])
    matrix = weights[:, 0:192].astype(BF16)

    shear = shear_ref[...]
    lame = lame_ref[...]
    material = lame + 2.0 * shear
    inverse = 1.0 / material

    def lifted(ref):
        high, low = halves(ref[...])
        return product(lifter, high) + product(lifter_rest, high) + product(lifter, low)

    def build_links(b, carry):
        slots = links[b + b // 6]
        hot = onehot(jnp.bitwise_and(slots, 127), 128, BLOCK).astype(BF16)
        hot_links[b, 0:128, :] = hot
        hot_links[b, 128:256, :] = hot
        return carry

    right = load[...].reshape(60, ELEMS)
    left_over[...] = right
    field[60:64, :] = jnp.zeros((4, ELEMS), F32)
    field[0:60, :] = right * (inverse * (1.0 / CENTER))
    solved[...] = jnp.zeros_like(solved)
    flux_sum[...] = jnp.zeros_like(flux_sum)

    def halo_copy(i, side, piece, target):
        return pltpu.make_async_remote_copy(
            src_ref=rims.at[i, piece],
            dst_ref=halo.at[i, side],
            send_sem=halo_send.at[i, side],
            recv_sem=halo_recv.at[i, side],
            device_id=target,
            device_id_type=MESH,
        )

    def step(i, scale_old, scale_new, before, between):
        first = i == 0
        now = field[...]
        high, low = halves(now)
        stacked[0:64, :] = high
        stacked[64:128, :] = low
        stacked[128:192, :] = high
        trace[...] = product(matrix[0:160], stacked[...])
        if first:
            for f in range(4):
                trace[f * ROWS + 36 : f * ROWS + 37, :] = material
        for side, piece, target, sends, receives in sides:
            rims[i, piece] = trace[120:160, piece * 128 : piece * 128 + 128]

            @pl.when(sends)
            def _():
                halo_copy(i, side, piece, target).start()

        before()
        if first:
            lax.fori_loop(0, 7, build_links, 0)

        for p in range(CHUNKS // 2):
            parts = []
            for s in (2 * p, 2 * p + 1):
                t = s if s < 24 else s + 4
                f, j = t // 8, t % 8
                parts.append(trace[f * ROWS : (f + 1) * ROWS, j * 128 : (j + 1) * 128])
            high, low = halves(jnp.concatenate(parts, axis=0))
            table[p * 80 : p * 80 + 80, 0:128] = high
            table[p * 80 : p * 80 + 80, 128:256] = low

        def block(b, carry):
            place = b + b // 6
            chunk = lax.shift_right_logical(links[place], 7)
            chunk = jnp.where(chunk >= 24, chunk - 4, chunk)
            result = product(table[...], hot_links[b])
            f = place // 2
            half = place - 2 * f
            gathered[
                pl.ds(pl.multiple_of(f * ROWS, 8), ROWS), pl.ds(pl.multiple_of(half * BLOCK, BLOCK), BLOCK)
            ] = choose(result, chunk, CHUNKS, ROWS)
            return carry

        lax.fori_loop(0, 7, block, 0)

        volume = product(matrix[160:288], stacked[...])
        image[...] = shear * volume[0:64] + lame * volume[64:128]
        solved[...] = solved[...] + now[0:60]
        between()

        for side, piece, target, sends, receives in sides:
            @pl.when(receives)
            def _():
                halo_copy(i, side, piece, target).wait_recv()
            gathered[120:160, side * 128 : side * 128 + 128] = halo[i, side]

        if first:
            for f in range(4):
                alpha[f : f + 1, :] = 0.5 * (material + gathered[f * ROWS + 36 : f * ROWS + 37, :])
        for f in range(4):
            rows = slice(f * ROWS, (f + 1) * ROWS)
            value = alpha[f : f + 1, :] * (trace[rows, :] - gathered[rows, :])
            flux[rows, :] = value
            flux_sum[rows, :] = flux_sum[rows, :] + value
        left = left_over[...] - (image[...] + lifted(flux))[0:60]
        left_over[...] = left
        if i < ITERS - 1:
            field[0:60, :] = scale_old * now[0:60] + scale_new * (left * inverse)

    def nothing():
        pass

    def ids_middle():
        arrive(*ids_first)
        for a in range(PA):
            ids_mid[pl.ds(a, PD, stride=PA), :] = ids_one[a * PD : (a + 1) * PD, :]
        go(*ids_second)

    def answer():
        arrive(*ids_second)
        asked = jnp.transpose(ids_in[...])[0:RANKS].astype(jnp.int32)
        for rank in range(RANKS):
            hot_grid[:, rank * 128 : (rank + 1) * 128] = onehot(asked[rank : rank + 1], BLOCK, 128).astype(BF16)
        owned = jnp.concatenate(
            [normal_ref[...] * friction_ref[...], state_ref[...], shear_load[:, 0, :], shear_load[:, 1, :]], axis=0
        )
        high = owned.astype(BF16).astype(F32)
        both = product(jnp.concatenate([high, owned - high], axis=0).astype(BF16), hot_grid[...])
        for rank in range(RANKS):
            lanes = slice(rank * 128, (rank + 1) * 128)
            params_pack[rank * 48 : (rank + 1) * 48, :] = both[0:48, lanes] + both[48:96, lanes]
        for j in range(3):
            down_out[pl.ds(j, 128, stride=3), :] = jnp.transpose(params_pack[j * 128 : (j + 1) * 128, :])
        go(*down_first)
        for j in range(3):
            turned = jnp.transpose(params_pack[(3 + j) * 128 : (4 + j) * 128, :])
            for d in range(PD):
                over_out[pl.ds(d * 3 + j, PA, stride=48), :] = turned[d * PA : (d + 1) * PA]
        go(*over_first)

    def params_middle():
        arrive(*down_first)
        for d in range(PD):
            for j in range(3):
                down_mid[pl.ds(d * 3 + j, PA, stride=48), :] = down_one[pl.ds(d * 24 + j, PA, stride=3), :]
        go(*down_second)
        arrive(*over_first)
        for a in range(PA):
            for j in range(3):
                over_mid[pl.ds(a * 3 + j, PD, stride=24), :] = over_one[pl.ds(a * 48 + j, PD, stride=3), :]
        go(*over_second)

    pairs = coefficients()
    step(0, *pairs[0], nothing, ids_middle)
    step(1, *pairs[1], nothing, answer)
    step(2, *pairs[2], nothing, nothing)
    step(3, *pairs[3], params_middle, nothing)
    residual_ref[...] = left_over[...].reshape(60, 1, ELEMS)
    results[0].start()

    for p in range(16):
        parts = []
        for s in (2 * p, 2 * p + 1):
            f, j = s // 8, s % 8
            parts.append(flux_sum[f * ROWS : (f + 1) * ROWS, j * 128 : (j + 1) * 128])
        high, low = halves(jnp.concatenate(parts, axis=0))
        table_send[p * 80 : p * 80 + 80, 0:128] = high
        table_send[p * 80 : p * 80 + 80, 128:256] = low
    for b in range(4):
        high = jnp.concatenate([send_maps[4 * b + j : 4 * b + j + 1, :] for j in range(4)], axis=1)
        low = jnp.concatenate([send_maps[16 + 4 * b + j : 17 + 4 * b + j, :] for j in range(4)], axis=1)
        hot = onehot(low.astype(jnp.int32), 128, BLOCK).astype(BF16)
        hot_send[0:128, :] = hot
        hot_send[128:256, :] = hot
        result = product(table_send[...], hot_send[...])
        tractions[b] = choose(result, high.astype(jnp.int32), 32, ROWS)

    def build_face(b, carry):
        low = jnp.concatenate([face_maps[pl.ds(32 + 4 * b + j, 1), :] for j in range(4)], axis=1)
        hot = onehot(low.astype(jnp.int32), 128, BLOCK).astype(BF16)
        hot_face[b, 0:128, :] = hot
        hot_face[b, 128:256, :] = hot
        return carry

    lax.fori_loop(0, 8, build_face, 0)
    rate_pack[...] = jnp.zeros_like(rate_pack)

    arrive(*down_second)
    for j in range(3):
        params[j * 128 : (j + 1) * 128, :] = jnp.transpose(down_in[pl.ds(j, 128, stride=3), :])
    arrive(*over_second)
    for j in range(3):
        parts = [over_in[pl.ds(a * 3 + j, PD, stride=24), :] for a in range(PA)]
        params[(3 + j) * 128 : (4 + j) * 128, :] = jnp.transpose(jnp.concatenate(parts, axis=0))
    for b in range(4):
        first = [params[(4 * b + j) * 48 : (4 * b + j + 1) * 48, :] for j in range(4)]
        owned = jnp.concatenate(first, axis=1)
        traction = tractions[b]
        state = owned[12:24]
        strike = owned[24:36] + traction[0:12]
        updip = owned[36:48] + traction[12:24]
        magnitude = jnp.sqrt(strike * strike + updip * updip)
        resist = owned[0:12] * (1.0 + 0.5 * jnp.tanh(traction[24:36]))
        steep = resist * state
        velocity = magnitude / (DAMPING + steep)
        for _ in range(NEWTON - 1):
            scaled = state * velocity
            square = 1.0 + scaled * scaled
            inverse_root = lax.rsqrt(square)
            misfit = magnitude - DAMPING * velocity - resist * inverse_sinh(scaled, square * inverse_root)
            velocity = velocity + misfit / (DAMPING + steep * inverse_root)
        factor = TIME_STEP * velocity / jnp.maximum(magnitude, 1.0)
        slip = jnp.concatenate([factor * strike, factor * updip], axis=0)
        for j in range(4):
            rank = 4 * b + j
            rate_pack[rank * 16 : rank * 16 + 12, :] = velocity[:, j * 128 : (j + 1) * 128]
        for j in (0, 2):
            parts = [slip[:, j * 128 : (j + 1) * 128], slip[:, (j + 1) * 128 : (j + 2) * 128]]
            high, low = halves(jnp.concatenate(parts, axis=0))
            at = (4 * b + j) * 24
            table_back[at : at + 48, 0:128] = high
            table_back[at : at + 48, 128:256] = low
    for j in range(2):
        rate_out[pl.ds(j, 128, stride=2), :] = jnp.transpose(rate_pack[j * 128 : (j + 1) * 128, :])
    go(*rate_first)

    flux[...] = jnp.zeros_like(flux)

    def place_back(b, carry):
        rank = jnp.concatenate([face_maps[pl.ds(4 * b + j, 1), :] for j in range(4)], axis=1)
        result = product(table_back[...], hot_face[b])
        f = b // 2
        half = b - 2 * f
        flux[
            pl.ds(pl.multiple_of(f * ROWS, 8), 24), pl.ds(pl.multiple_of(half * BLOCK, BLOCK), BLOCK)
        ] = choose(result, rank.astype(jnp.int32) - 1, RANKS, 24)
        return carry

    lax.fori_loop(0, 8, place_back, 0)

    arrive(*rate_first)
    for a in range(PA):
        for j in range(2):
            rate_mid[pl.ds(a * 2 + j, PD, stride=16), :] = rate_one[pl.ds(a * 32 + j, PD, stride=2), :]
    go(*rate_second)
    disp_ref[...] = (solved[...] + 0.5 * lifted(flux)[0:60]).reshape(60, 1, ELEMS)
    results[1].start()
    for each in (ids_first, ids_second, down_first, down_second, over_first, over_second, rate_first):
        drain(*each)
    for i in range(ITERS):
        for side, piece, target, sends, receives in sides:
            @pl.when(sends)
            def _():
                halo_copy(i, side, piece, target).wait_send()

    arrive(*rate_second)
    for j in range(2):
        value = jnp.transpose(rate_in[pl.ds(j, 128, stride=2), :])
        high = value.astype(BF16).astype(F32)
        low = value - high
        for r in range(8):
            lanes = slice((8 * j + r) * 128, (8 * j + r + 1) * 128)
            wide[0:16, lanes] = high[r * 16 : (r + 1) * 16]
            wide[16:32, lanes] = low[r * 16 : (r + 1) * 16]
    both = lax.dot_general(wide[...].astype(BF16), hot_grid[...], NT, preferred_element_type=F32)
    rate_ref[...] = both[0:12] + both[16:28]
    results[2].start()
    drain(*rate_second)
    for result in results:
        result.wait()


def hand_over(disp_ref, residual_ref, rate_ref, disp_out, residual_out, rate_out, disp, residual, rate, sems):
    ways = ((disp_ref, disp, disp_out), (residual_ref, residual, residual_out), (rate_ref, rate, rate_out))
    inward = [pltpu.make_async_copy(way[0], way[1], sems.at[0, i]) for i, way in enumerate(ways)]
    outward = [pltpu.make_async_copy(way[1], way[2], sems.at[1, i]) for i, way in enumerate(ways)]
    for copy in inward:
        copy.start()
    for first, second in zip(inward, outward):
        first.wait()
        second.start()
    for copy in outward:
        copy.wait()


def on_device(
    right_side,
    shear_modulus,
    lame_lambda,
    stiff_shear,
    stiff_lame,
    face_interp,
    neighbours,
    fault_count,
    fault_owner,
    fault_slot,
    fault_face,
    normal_stress,
    friction,
    state_factor,
    shear_load,
):
    vmem = pl.BlockSpec(memory_space=pltpu.VMEM)
    hbm = pl.BlockSpec(memory_space=pltpu.HBM)
    scratch = [
        pltpu.VMEM((60, 1, ELEMS), F32),
        pltpu.VMEM((60, 1, ELEMS), F32),
        pltpu.VMEM((12, 512), F32),
        pltpu.SemaphoreType.DMA((3,)),
        pltpu.VMEM((60, 1, ELEMS), F32),
        pltpu.VMEM((1, ELEMS), F32),
        pltpu.VMEM((1, ELEMS), F32),
        pltpu.VMEM((60, 60), F32),
        pltpu.VMEM((60, 60), F32),
        pltpu.VMEM((12, 4, 20), F32),
        pltpu.VMEM((8, 1, BLOCK), jnp.int32),
        pltpu.VMEM((16, 1, 128), jnp.int32),
        pltpu.VMEM((16, 1, 128), jnp.int32),
        pltpu.VMEM((16, 1, 128), jnp.int32),
        pltpu.VMEM((12, 512), F32),
        pltpu.VMEM((12, 512), F32),
        pltpu.VMEM((12, 512), F32),
        pltpu.VMEM((12, 2, 512), F32),
        pltpu.SemaphoreType.DMA((14,)),
        pltpu.VMEM((288, 128), F32),
        pltpu.VMEM((288, 256), F32),
        pltpu.VMEM((128, 256), F32),
        pltpu.VMEM((60, ELEMS), F32),
        pltpu.VMEM((60, ELEMS), F32),
        pltpu.VMEM((64, ELEMS), F32),
        pltpu.VMEM((192, ELEMS), BF16),
        pltpu.VMEM((160, ELEMS), F32),
        pltpu.VMEM((64, ELEMS), F32),
        pltpu.VMEM((160, ELEMS), F32),
        pltpu.VMEM((160, ELEMS), F32),
        pltpu.VMEM((160, ELEMS), F32),
        pltpu.VMEM((8, ELEMS), F32),
        pltpu.VMEM((CHUNKS * ROWS, 256), BF16),
        pltpu.VMEM((7, 256, BLOCK), BF16),
        pltpu.VMEM((2048, 128), BF16),
        pltpu.VMEM((2048, 256), F32),
        pltpu.VMEM((64, 128), F32),
        pltpu.VMEM((64, 128), F32),
        pltpu.VMEM((256, BLOCK), BF16),
        pltpu.VMEM((8, 256, BLOCK), BF16),
        pltpu.VMEM((32 * ROWS, 256), BF16),
        pltpu.VMEM((ITERS, 4, ROWS, 128), F32),
        pltpu.VMEM((ITERS, 4, ROWS, 128), F32),
        pltpu.VMEM((128, 128), F32),
        pltpu.VMEM((128, 128), F32),
        pltpu.VMEM((128, 128), F32),
        pltpu.VMEM((128, 128), F32),
        pltpu.VMEM((BLOCK, 2048), BF16),
        pltpu.VMEM((768, 128), F32),
        pltpu.VMEM((384, 128), F32),
        pltpu.VMEM((384, 128), F32),
        pltpu.VMEM((384, 128), F32),
        pltpu.VMEM((384, 128), F32),
        pltpu.VMEM((384, 128), F32),
        pltpu.VMEM((384, 128), F32),
        pltpu.VMEM((384, 128), F32),
        pltpu.VMEM((384, 128), F32),
        pltpu.VMEM((768, 128), F32),
        pltpu.VMEM((4, ROWS, BLOCK), F32),
        pltpu.VMEM((256, 128), F32),
        pltpu.VMEM((256, 128), F32),
        pltpu.VMEM((256, 128), F32),
        pltpu.VMEM((256, 128), F32),
        pltpu.VMEM((256, 128), F32),
        pltpu.VMEM((32, 2048), F32),
        pltpu.VMEM((384, 256), BF16),
        pltpu.SemaphoreType.DMA((ITERS, 4)),
        pltpu.SemaphoreType.DMA((ITERS, 4)),
    ] + [pltpu.SemaphoreType.DMA((PD,))] * 16
    displacement, residual, rate = pl.pallas_call(
        kernel,
        out_shape=(
            jax.ShapeDtypeStruct((60, 1, ELEMS), F32),
            jax.ShapeDtypeStruct((60, 1, ELEMS), F32),
            jax.ShapeDtypeStruct((12, 512), F32),
        ),
        in_specs=[vmem] + [hbm] * 14,
        out_specs=(hbm, hbm, hbm),
        scratch_shapes=scratch,
        compiler_params=pltpu.CompilerParams(collective_id=0, has_side_effects=True, vmem_limit_bytes=64000 * 1024),
        name="window",
    )(
        fault_count.reshape(1, 1),
        right_side.reshape(60, 1, ELEMS),
        shear_modulus.reshape(1, ELEMS),
        lame_lambda.reshape(1, ELEMS),
        stiff_shear,
        stiff_lame,
        face_interp,
        neighbours.reshape(8, 1, BLOCK),
        fault_owner.reshape(16, 1, 128),
        fault_slot.reshape(16, 1, 128),
        fault_face.reshape(16, 1, 128),
        normal_stress,
        friction,
        state_factor,
        shear_load.transpose(1, 0, 2),
    )
    displacement, residual, rate = pl.pallas_call(
        hand_over,
        out_shape=(
            jax.ShapeDtypeStruct((480, 128), F32),
            jax.ShapeDtypeStruct((480, 128), F32),
            jax.ShapeDtypeStruct((12, 512), F32),
        ),
        in_specs=[hbm] * 3,
        out_specs=(hbm, hbm, hbm),
        scratch_shapes=[
            pltpu.VMEM((480, 128), F32),
            pltpu.VMEM((480, 128), F32),
            pltpu.VMEM((12, 512), F32),
            pltpu.SemaphoreType.DMA((2, 3)),
        ],
        compiler_params=pltpu.CompilerParams(vmem_limit_bytes=64000 * 1024),
        name="hand_over",
    )(displacement.reshape(480, 128), residual.reshape(480, 128), rate)
    return displacement.reshape(right_side.shape), residual.reshape(right_side.shape), rate


def solution(mesh):
    in_specs = (
        P(None, None, "along", "depth", None),
        P("along", "depth", None),
        P("along", "depth", None),
        P(),
        P(),
        P(),
        P("along", "depth", None),
        P("along", "depth"),
        P("along", "depth", None),
        P("along", "depth", None),
        P("along", "depth", None),
        P(None, ("along", "depth")),
        P(None, ("along", "depth")),
        P(None, ("along", "depth")),
        P(None, None, ("along", "depth")),
    )
    out_specs = (
        P(None, None, "along", "depth", None),
        P(None, None, "along", "depth", None),
        P(None, ("along", "depth")),
    )
    return jax.shard_map(
        on_device, mesh=mesh, in_specs=in_specs, out_specs=out_specs, check_vma=False
    )
```

```python
import functools

import jax
import jax.numpy as jnp
from jax import lax
from jax.experimental import pallas as pl
from jax.experimental.pallas import tpu as pltpu
from jax.sharding import PartitionSpec as P

ITERS = 4
NEWTON = 6
DAMPING = 0.5
TIME_STEP = 0.5
LOWER_EDGE = 0.25
UPPER_EDGE = 5.0
CENTER = 0.5 * (UPPER_EDGE + LOWER_EDGE)
SPREAD = 0.5 * (UPPER_EDGE - LOWER_EDGE)

MESH = pl.DeviceIdType.MESH
F32 = jnp.float32
BF16 = jnp.bfloat16
NT = (((1,), (1,)), ((), ()))

PA, PD = 8, 16
DEVS = PA * PD
ELEMS = 1024
ROWS = 40
BLOCK = 512
CHUNKS = 28
SPLIT = 18
RANKS = 16


def coefficients():
    ratio = CENTER / SPREAD
    rho = 1.0 / ratio
    pairs = []
    for _ in range(ITERS):
        rho_next = 1.0 / (2.0 * ratio - rho)
        pairs.append((rho_next * rho, 2.0 * rho_next / SPREAD))
        rho = rho_next
    return pairs


def halves(value):
    high = value.astype(BF16)
    return high, (value - high.astype(F32)).astype(BF16)


def product(left, right):
    return jnp.dot(left, right, preferred_element_type=F32)


def onehot(digit, rows, columns):
    return (lax.broadcasted_iota(jnp.int32, (rows, columns), 0) == digit).astype(F32)


def choose(result, chunk, count, rows):
    width = result.shape[1]
    index = jnp.broadcast_to(chunk, (8, width))
    total = jnp.zeros((rows // 8, 8, width), F32)
    for s in range(count):
        part = result[s * rows : (s + 1) * rows].reshape(rows // 8, 8, width)
        total = jnp.where((index == s)[None], part, total)
    return total.reshape(rows, width)


def inverse_sinh(size, root):
    magnitude = jnp.log(jnp.abs(size) + root)
    return jnp.where(size < 0.0, -magnitude, magnitude)


def kernel(
    count_ref, load_hbm, shear_hbm, lame_hbm, stiff_shear_hbm, stiff_lame_hbm, interp_hbm, links_hbm, owner_hbm,
    slot_hbm, face_hbm, normal_hbm, friction_hbm, state_hbm, shear_load_hbm,
    disp_hbm, residual_hbm, rate_hbm,
    disp_ref, residual_ref, rate_ref, result_sem,
    load, shear_ref, lame_ref, stiff_shear, stiff_lame, interp, links, owner_ref, slot_ref, face_ref,
    normal_ref, friction_ref, state_ref, shear_load, fetch_sem,
    weight, weights, lift_pair, solved, left_over, field, stacked, trace, image, gathered, flux, flux_sum, alpha,
    table, hot_links, hot_owner, prefix, send_maps, face_maps, hot_send, hot_face, table_send, halo, rims,
    ids_out, ids_one, ids_mid, ids_in, hot_grid, params_pack, down_out, down_one, down_mid, down_in, over_out,
    over_one, over_mid, over_in, params,
    tractions, rate_pack, rate_out, rate_one, rate_mid, rate_in, wide, table_back,
    halo_send, halo_recv, ids_a, ids_b, ids_c, ids_d, par_a, par_b, par_c, par_d, par_e, par_f, par_g, par_h,
    rate_a, rate_b, rate_c, rate_d,
):
    along = lax.axis_index("along")
    depth = lax.axis_index("depth")

    operands = (
        (owner_hbm, owner_ref), (slot_hbm, slot_ref), (face_hbm, face_ref), (load_hbm, load), (shear_hbm, shear_ref),
        (lame_hbm, lame_ref), (stiff_shear_hbm, stiff_shear), (stiff_lame_hbm, stiff_lame), (interp_hbm, interp),
        (links_hbm, links), (normal_hbm, normal_ref), (friction_hbm, friction_ref), (state_hbm, state_ref),
        (shear_load_hbm, shear_load),
    )
    fetches = [
        pltpu.make_async_copy(source, target, fetch_sem.at[i]) for i, (source, target) in enumerate(operands)
    ]
    for fetch in fetches[0:3]:
        fetch.start()

    results = [
        pltpu.make_async_copy(source, target, result_sem.at[i])
        for i, (source, target) in enumerate(
            ((residual_ref, residual_hbm), (disp_ref, disp_hbm), (rate_ref, rate_hbm))
        )
    ]

    barrier = pltpu.get_barrier_semaphore()
    for i in range(1, PA):
        pl.semaphore_signal(barrier, inc=1, device_id=(lax.rem(along + i, PA), depth), device_id_type=MESH)
    for i in range(1, PD):
        pl.semaphore_signal(barrier, inc=1, device_id=(along, lax.rem(depth + i, PD)), device_id_type=MESH)

    for fetch in fetches[3:]:
        fetch.start()

    def row_copy(i, source, landing, size, sems, sending):
        peer = lax.rem(along + i, PA) if sending else lax.rem(along + PA - i, PA)
        place = along if sending else peer
        return pltpu.make_async_remote_copy(
            src_ref=source.at[pl.ds(pl.multiple_of(peer * size, 8), size)],
            dst_ref=landing.at[pl.ds(pl.multiple_of(place * size, 8), size)],
            send_sem=sems[0].at[i],
            recv_sem=sems[1].at[i],
            device_id=(peer, depth),
            device_id_type=MESH,
        )

    def column_copy(i, source, landing, size, sems, sending):
        peer = lax.rem(depth + i, PD) if sending else lax.rem(depth + PD - i, PD)
        place = depth if sending else peer
        return pltpu.make_async_remote_copy(
            src_ref=source.at[pl.ds(pl.multiple_of(peer * size, 8), size)],
            dst_ref=landing.at[pl.ds(pl.multiple_of(place * size, 8), size)],
            send_sem=sems[0].at[i],
            recv_sem=sems[1].at[i],
            device_id=(along, peer),
            device_id_type=MESH,
        )

    def go(kind, source, landing, size, sems):
        mine, peers = (along, PA) if kind is row_copy else (depth, PD)
        for i in range(1, peers):
            kind(i, source, landing, size, sems, True).start()
        own = pl.ds(pl.multiple_of(mine * size, 8), size)
        landing[own, :] = source[own, :]

    def arrive(kind, source, landing, size, sems):
        for i in range(1, PA if kind is row_copy else PD):
            kind(i, source, landing, size, sems, False).wait_recv()

    def drain(kind, source, landing, size, sems):
        for i in range(1, PA if kind is row_copy else PD):
            kind(i, source, landing, size, sems, True).wait_send()

    ids_first = (row_copy, ids_out, ids_one, 16, (ids_a, ids_b))
    ids_second = (column_copy, ids_mid, ids_in, 8, (ids_c, ids_d))
    down_first = (column_copy, down_out, down_one, 24, (par_a, par_b))
    down_second = (row_copy, down_mid, down_in, 48, (par_c, par_d))
    over_first = (row_copy, over_out, over_one, 48, (par_e, par_f))
    over_second = (column_copy, over_mid, over_in, 24, (par_g, par_h))
    rate_first = (row_copy, rate_out, rate_one, 32, (rate_a, rate_b))
    rate_second = (column_copy, rate_mid, rate_in, 16, (rate_c, rate_d))

    for fetch in fetches[0:3]:
        fetch.wait()
    count = count_ref[...]
    lane = lax.broadcasted_iota(jnp.int32, (1, 128), 1)
    for t in range(RANKS):
        live = (lane + t * 128) < count
        owner = jnp.where(live, owner_ref[t], -1)
        hot_owner[t * 128 : (t + 1) * 128, :] = onehot(owner, 128, 128).astype(BF16)
    row = lax.broadcasted_iota(jnp.int32, (128, 256), 0)
    column = lax.broadcasted_iota(jnp.int32, (128, 256), 1)
    earlier = ((row < column) | (column >= 128)).astype(F32).astype(BF16)
    prefix[...] = product(hot_owner[...], earlier)
    base = jnp.zeros((128, 128), F32)
    sent = jnp.zeros((64, 128), F32)
    ranked = []
    for t in range(RANKS):
        rows = slice(t * 128, (t + 1) * 128)
        hot = hot_owner[rows, :]
        rank = jnp.sum(hot.astype(F32) * (prefix[rows, 0:128] + base), axis=0, keepdims=True)
        base = base + prefix[rows, 128:256]
        live = ((lane + t * 128) < count).astype(F32)
        rank_live = jnp.where(live > 0.0, rank, -1.0).astype(jnp.int32)
        face = face_ref[t]
        slot = slot_ref[t]
        face_high = lax.shift_right_logical(face, 7)
        face_low = jnp.bitwise_and(face, 127)
        ranks = onehot(rank_live, RANKS, 128)
        values = jnp.concatenate(
            [
                ranks * face_high.astype(F32),
                ranks * face_low.astype(F32),
                ranks * (lax.shift_right_logical(slot, 4) + 1).astype(F32),
                ranks * jnp.bitwise_and(slot, 15).astype(F32),
            ],
            axis=0,
        ).astype(BF16)
        sent = sent + lax.dot_general(values, hot, NT, preferred_element_type=F32)
        ranked.append((rank, live))
    send_maps[...] = sent
    ids = 16.0 * sent[32:48] + sent[48:64] - 16.0
    ids_out[...] = jnp.transpose(jnp.concatenate([ids, jnp.zeros((112, 128), F32)], axis=0))

    pl.semaphore_wait(barrier, PA + PD - 2)
    go(*ids_first)

    placed = jnp.zeros((64, 128), F32)
    for t in range(RANKS):
        rank, live = ranked[t]
        face = face_ref[t]
        highs = onehot(lax.shift_right_logical(face, 7), 32, 128) * live
        values = jnp.concatenate([highs * (rank + 1.0), highs * owner_ref[t].astype(F32)], axis=0).astype(BF16)
        lows = onehot(jnp.bitwise_and(face, 127), 128, 128).astype(BF16)
        placed = placed + lax.dot_general(values, lows, NT, preferred_element_type=F32)
    face_maps[...] = placed

    sides = (
        (0, 1, (along + 1, depth), along < PA - 1, along > 0),
        (1, 0, (along - 1, depth), along > 0, along < PA - 1),
        (2, 3, (along, depth + 1), depth < PD - 1, depth > 0),
        (3, 2, (along, depth - 1), depth > 0, depth < PD - 1),
    )

    for side, piece, target, sends, receives in sides:
        @pl.when(jnp.logical_not(receives))
        def _():
            halo[:, side] = jnp.zeros((ITERS, ROWS, 128), F32)

    for fetch in fetches[3:]:
        fetch.wait()
    weight[...] = jnp.zeros_like(weight)
    for f in range(4):
        for c in range(3):
            weight[f * ROWS + c * 12 : f * ROWS + c * 12 + 12, c * 20 : c * 20 + 20] = interp[:, f, :]
    weight[160:220, 0:60] = stiff_shear[...]
    weight[224:284, 0:60] = stiff_lame[...]
    whole = weight[:, 0:64]
    high = whole.astype(BF16).astype(F32)
    rest = whole - high
    lift_pair[0:128, 0:128] = jnp.transpose(weight[0:128, :])
    lift_pair[0:128, 128:256] = jnp.transpose(weight[128:256, :])
    weights[:, 0:64] = high
    weights[:, 64:128] = high
    weights[:, 128:192] = rest
    lifter, lifter_rest = halves(lift_pair[0:64, 0:160])
    matrix = weights[:, 0:192].astype(BF16)
    rim_matrix = weights[120:160, 0:192].astype(BF16)
    rim_lifter, rim_rest = halves(lift_pair[0:64, 120:160])

    shear = shear_ref[...]
    lame = lame_ref[...]
    material = lame + 2.0 * shear
    inverse = 1.0 / material

    def lifted(ref):
        high, low = halves(ref[...])
        return product(lifter, high) + product(lifter_rest, high) + product(lifter, low)

    def build_links(b, carry):
        slots = links[b + b // 6]
        hot = onehot(jnp.bitwise_and(slots, 127), 128, BLOCK).astype(BF16)
        hot_links[b, 0:128, :] = hot
        hot_links[b, 128:256, :] = hot
        return carry

    right = load[...].reshape(60, ELEMS)
    left_over[...] = right
    field[60:64, :] = jnp.zeros((4, ELEMS), F32)
    field[0:60, :] = right * (inverse * (1.0 / CENTER))
    solved[...] = jnp.zeros_like(solved)
    flux_sum[...] = jnp.zeros_like(flux_sum)

    def halo_copy(i, side, piece, target):
        return pltpu.make_async_remote_copy(
            src_ref=rims.at[i, piece],
            dst_ref=halo.at[i, side],
            send_sem=halo_send.at[i, side],
            recv_sem=halo_recv.at[i, side],
            device_id=target,
            device_id_type=MESH,
        )

    def step(i, scale_old, scale_new, split, middle, between):
        first = i == 0
        now = field[...]
        high, low = halves(now)
        stacked[0:64, :] = high
        stacked[64:128, :] = low
        stacked[128:192, :] = high
        rim = product(rim_matrix, stacked[:, 0:BLOCK])
        for side, piece, target, sends, receives in sides:
            rims[i, piece] = rim[:, piece * 128 : piece * 128 + 128]
            if first:
                rims[i, piece, 36:37, :] = material[:, piece * 128 : piece * 128 + 128]

            @pl.when(sends)
            def _():
                halo_copy(i, side, piece, target).start()

        trace[...] = product(matrix[0:160], stacked[...])
        if first:
            for f in range(4):
                trace[f * ROWS + 36 : f * ROWS + 37, :] = material
        if first:
            lax.fori_loop(0, 7, build_links, 0)

        for p in range(SPLIT // 2):
            parts = []
            for s in (2 * p, 2 * p + 1):
                t = s if s < 24 else s + 4
                f, j = t // 8, t % 8
                parts.append(trace[f * ROWS : (f + 1) * ROWS, j * 128 : (j + 1) * 128])
            high, low = halves(jnp.concatenate(parts, axis=0))
            table[p * 80 : p * 80 + 80, 0:128] = high
            table[p * 80 : p * 80 + 80, 128:256] = low

        def block(b, carry):
            place = b + b // 6
            chunk = lax.shift_right_logical(links[place], 7)
            chunk = jnp.where(chunk >= 24, chunk - 4, chunk)
            result = product(table[0 : SPLIT * ROWS, :], hot_links[b])
            lanes = jnp.bitwise_and(links[place], 127)
            total = choose(result, chunk, SPLIT, ROWS)
            columns = []
            for q in range(4):
                part = slice(q * 128, (q + 1) * 128)
                low = jnp.broadcast_to(lanes[:, part], (8, 128))
                index = jnp.broadcast_to(chunk[:, part], (8, 128))
                groups = [total[8 * g : 8 * g + 8, part] for g in range(ROWS // 8)]
                for s in range(SPLIT, CHUNKS):
                    t = s if s < 24 else s + 4
                    mine = index == s
                    for g in range(ROWS // 8):
                        source = trace[t // 8 * ROWS + 8 * g : t // 8 * ROWS + 8 * g + 8, t % 8 * 128 : t % 8 * 128 + 128]
                        groups[g] = jnp.where(mine, jnp.take_along_axis(source, low, axis=1), groups[g])
                columns.append(jnp.concatenate(groups, axis=0))
            f = place // 2
            half = place - 2 * f
            gathered[
                pl.ds(pl.multiple_of(f * ROWS, 8), ROWS), pl.ds(pl.multiple_of(half * BLOCK, BLOCK), BLOCK)
            ] = jnp.concatenate(columns, axis=1)
            return carry

        lax.fori_loop(0, split, block, 0)
        middle()
        if split < 7:
            lax.fori_loop(split, 7, block, 0)

        volume = product(matrix[160:288], stacked[...])
        image[...] = shear * volume[0:64] + lame * volume[64:128]
        solved[...] = solved[...] + now[0:60]

        inner = slice(BLOCK, ELEMS)
        outer = slice(0, BLOCK)
        if first:
            for f in range(3):
                alpha[f : f + 1, :] = 0.5 * (material + gathered[f * ROWS + 36 : f * ROWS + 37, :])
            alpha[3:4, inner] = 0.5 * (material[:, inner] + gathered[156:157, inner])
        for f in range(4):
            rows = slice(f * ROWS, (f + 1) * ROWS)
            columns = slice(0, ELEMS) if f < 3 else inner
            value = alpha[f : f + 1, columns] * (trace[rows, columns] - gathered[rows, columns])
            flux[rows, columns] = value
            flux_sum[rows, columns] = flux_sum[rows, columns] + value
        flux[120:160, outer] = jnp.zeros((ROWS, BLOCK), F32)
        left = left_over[...] - (image[...] + lifted(flux))[0:60]
        left_over[...] = left
        if i < ITERS - 1:
            field[0:60, :] = scale_old * now[0:60] + scale_new * (left * inverse)
        between()

        for side, piece, target, sends, receives in sides:
            @pl.when(receives)
            def _():
                halo_copy(i, side, piece, target).wait_recv()
        arrived = jnp.concatenate([halo[i, side] for side in range(4)], axis=1)
        if first:
            alpha[3:4, outer] = 0.5 * (material[:, outer] + arrived[36:37])
        value = alpha[3:4, outer] * (trace[120:160, outer] - arrived)
        flux_sum[120:160, outer] = flux_sum[120:160, outer] + value
        high, low = halves(value)
        late = (product(rim_lifter, high) + product(rim_rest, high) + product(rim_lifter, low))[0:60]
        left_over[:, outer] = left_over[:, outer] - late
        if i < ITERS - 1:
            field[0:60, outer] = field[0:60, outer] - scale_new * (late * inverse[:, outer])

    def nothing():
        pass

    def ids_middle():
        arrive(*ids_first)
        for a in range(PA):
            ids_mid[pl.ds(a, PD, stride=PA), :] = ids_one[a * PD : (a + 1) * PD, :]
        go(*ids_second)

    def answer():
        arrive(*ids_second)
        asked = jnp.transpose(ids_in[...])[0:RANKS].astype(jnp.int32)
        for rank in range(RANKS):
            hot_grid[:, rank * 128 : (rank + 1) * 128] = onehot(asked[rank : rank + 1], BLOCK, 128).astype(BF16)
        owned = jnp.concatenate(
            [normal_ref[...] * friction_ref[...], state_ref[...], shear_load[:, 0, :], shear_load[:, 1, :]], axis=0
        )
        high = owned.astype(BF16).astype(F32)
        both = product(jnp.concatenate([high, owned - high], axis=0).astype(BF16), hot_grid[...])
        for rank in range(RANKS):
            lanes = slice(rank * 128, (rank + 1) * 128)
            params_pack[rank * 48 : (rank + 1) * 48, :] = both[0:48, lanes] + both[48:96, lanes]
        for j in range(3):
            down_out[pl.ds(j, 128, stride=3), :] = jnp.transpose(params_pack[j * 128 : (j + 1) * 128, :])
        go(*down_first)
        for j in range(3):
            turned = jnp.transpose(params_pack[(3 + j) * 128 : (4 + j) * 128, :])
            for d in range(PD):
                over_out[pl.ds(d * 3 + j, PA, stride=48), :] = turned[d * PA : (d + 1) * PA]
        go(*over_first)

    def params_middle():
        arrive(*down_first)
        for d in range(PD):
            for j in range(3):
                down_mid[pl.ds(d * 3 + j, PA, stride=48), :] = down_one[pl.ds(d * 24 + j, PA, stride=3), :]
        go(*down_second)
        arrive(*over_first)
        for a in range(PA):
            for j in range(3):
                over_mid[pl.ds(a * 3 + j, PD, stride=24), :] = over_one[pl.ds(a * 48 + j, PD, stride=3), :]
        go(*over_second)

    pairs = coefficients()
    step(0, *pairs[0], 4, ids_middle, nothing)
    step(1, *pairs[1], 7, nothing, answer)
    step(2, *pairs[2], 7, nothing, nothing)
    step(3, *pairs[3], 0, params_middle, nothing)
    residual_ref[...] = left_over[...].reshape(60, 1, ELEMS)
    results[0].start()

    for p in range(16):
        parts = []
        for s in (2 * p, 2 * p + 1):
            f, j = s // 8, s % 8
            parts.append(flux_sum[f * ROWS : (f + 1) * ROWS, j * 128 : (j + 1) * 128])
        high, low = halves(jnp.concatenate(parts, axis=0))
        table_send[p * 80 : p * 80 + 80, 0:128] = high
        table_send[p * 80 : p * 80 + 80, 128:256] = low
    for b in range(4):
        high = jnp.concatenate([send_maps[4 * b + j : 4 * b + j + 1, :] for j in range(4)], axis=1)
        low = jnp.concatenate([send_maps[16 + 4 * b + j : 17 + 4 * b + j, :] for j in range(4)], axis=1)
        hot = onehot(low.astype(jnp.int32), 128, BLOCK).astype(BF16)
        hot_send[0:128, :] = hot
        hot_send[128:256, :] = hot
        result = product(table_send[...], hot_send[...])
        tractions[b] = choose(result, high.astype(jnp.int32), 32, ROWS)

    def build_face(b, carry):
        low = jnp.concatenate([face_maps[pl.ds(32 + 4 * b + j, 1), :] for j in range(4)], axis=1)
        hot = onehot(low.astype(jnp.int32), 128, BLOCK).astype(BF16)
        hot_face[b, 0:128, :] = hot
        hot_face[b, 128:256, :] = hot
        return carry

    lax.fori_loop(0, 8, build_face, 0)
    rate_pack[...] = jnp.zeros_like(rate_pack)

    def solve(b):
        owned = jnp.concatenate([params[(4 * b + j) * 48 : (4 * b + j + 1) * 48, :] for j in range(4)], axis=1)
        traction = tractions[b]
        state = owned[12:24]
        strike = owned[24:36] + traction[0:12]
        updip = owned[36:48] + traction[12:24]
        magnitude = jnp.sqrt(strike * strike + updip * updip)
        resist = owned[0:12] * (1.0 + 0.5 * jnp.tanh(traction[24:36]))
        steep = resist * state
        velocity = magnitude / (DAMPING + steep)
        for _ in range(NEWTON - 1):
            scaled = state * velocity
            square = 1.0 + scaled * scaled
            inverse_root = lax.rsqrt(square)
            misfit = magnitude - DAMPING * velocity - resist * inverse_sinh(scaled, square * inverse_root)
            velocity = velocity + misfit / (DAMPING + steep * inverse_root)
        for j in range(4):
            rank = 4 * b + j
            rate_pack[rank * 16 : rank * 16 + 12, :] = velocity[:, j * 128 : (j + 1) * 128]
        return velocity, magnitude, strike, updip

    arrive(*down_second)
    for j in range(3):
        params[j * 128 : (j + 1) * 128, :] = jnp.transpose(down_in[pl.ds(j, 128, stride=3), :])
    arrive(*over_second)
    for j in range(3):
        parts = [over_in[pl.ds(a * 3 + j, PD, stride=24), :] for a in range(PA)]
        params[(3 + j) * 128 : (4 + j) * 128, :] = jnp.transpose(jnp.concatenate(parts, axis=0))
    motion = [solve(b) for b in range(4)]
    for j in range(2):
        rate_out[pl.ds(j, 128, stride=2), :] = jnp.transpose(rate_pack[j * 128 : (j + 1) * 128, :])
    go(*rate_first)

    for b, (velocity, magnitude, strike, updip) in enumerate(motion):
        factor = TIME_STEP * velocity / jnp.maximum(magnitude, 1.0)
        slip = jnp.concatenate([factor * strike, factor * updip], axis=0)
        for j in (0, 2):
            parts = [slip[:, j * 128 : (j + 1) * 128], slip[:, (j + 1) * 128 : (j + 2) * 128]]
            high, low = halves(jnp.concatenate(parts, axis=0))
            at = (4 * b + j) * 24
            table_back[at : at + 48, 0:128] = high
            table_back[at : at + 48, 128:256] = low

    flux[...] = jnp.zeros_like(flux)

    def place_back(b, carry):
        rank = jnp.concatenate([face_maps[pl.ds(4 * b + j, 1), :] for j in range(4)], axis=1)
        result = product(table_back[...], hot_face[b])
        f = b // 2
        half = b - 2 * f
        flux[
            pl.ds(pl.multiple_of(f * ROWS, 8), 24), pl.ds(pl.multiple_of(half * BLOCK, BLOCK), BLOCK)
        ] = choose(result, rank.astype(jnp.int32) - 1, RANKS, 24)
        return carry

    lax.fori_loop(0, 8, place_back, 0)

    arrive(*rate_first)
    for a in range(PA):
        for j in range(2):
            rate_mid[pl.ds(a * 2 + j, PD, stride=16), :] = rate_one[pl.ds(a * 32 + j, PD, stride=2), :]
    go(*rate_second)
    disp_ref[...] = (solved[...] + 0.5 * lifted(flux)[0:60]).reshape(60, 1, ELEMS)
    results[1].start()
    for each in (ids_first, ids_second, down_first, down_second, over_first, over_second, rate_first):
        drain(*each)
    for i in range(ITERS):
        for side, piece, target, sends, receives in sides:
            @pl.when(sends)
            def _():
                halo_copy(i, side, piece, target).wait_send()

    arrive(*rate_second)
    for j in range(2):
        value = jnp.transpose(rate_in[pl.ds(j, 128, stride=2), :])
        high = value.astype(BF16).astype(F32)
        low = value - high
        for r in range(8):
            lanes = slice((8 * j + r) * 128, (8 * j + r + 1) * 128)
            wide[0:16, lanes] = high[r * 16 : (r + 1) * 16]
            wide[16:32, lanes] = low[r * 16 : (r + 1) * 16]
    both = lax.dot_general(wide[...].astype(BF16), hot_grid[...], NT, preferred_element_type=F32)
    rate_ref[...] = both[0:12] + both[16:28]
    results[2].start()
    drain(*rate_second)
    for result in results:
        result.wait()


def hand_over(disp_ref, residual_ref, rate_ref, disp_out, residual_out, rate_out, disp, residual, rate, sems):
    ways = ((disp_ref, disp, disp_out), (residual_ref, residual, residual_out), (rate_ref, rate, rate_out))
    inward = [pltpu.make_async_copy(way[0], way[1], sems.at[0, i]) for i, way in enumerate(ways)]
    outward = [pltpu.make_async_copy(way[1], way[2], sems.at[1, i]) for i, way in enumerate(ways)]
    for copy in inward:
        copy.start()
    for first, second in zip(inward, outward):
        first.wait()
        second.start()
    for copy in outward:
        copy.wait()


def on_device(
    right_side,
    shear_modulus,
    lame_lambda,
    stiff_shear,
    stiff_lame,
    face_interp,
    neighbours,
    fault_count,
    fault_owner,
    fault_slot,
    fault_face,
    normal_stress,
    friction,
    state_factor,
    shear_load,
):
    vmem = pl.BlockSpec(memory_space=pltpu.VMEM)
    hbm = pl.BlockSpec(memory_space=pltpu.HBM)
    scratch = [
        pltpu.VMEM((60, 1, ELEMS), F32),
        pltpu.VMEM((60, 1, ELEMS), F32),
        pltpu.VMEM((12, 512), F32),
        pltpu.SemaphoreType.DMA((3,)),
        pltpu.VMEM((60, 1, ELEMS), F32),
        pltpu.VMEM((1, ELEMS), F32),
        pltpu.VMEM((1, ELEMS), F32),
        pltpu.VMEM((60, 60), F32),
        pltpu.VMEM((60, 60), F32),
        pltpu.VMEM((12, 4, 20), F32),
        pltpu.VMEM((8, 1, BLOCK), jnp.int32),
        pltpu.VMEM((16, 1, 128), jnp.int32),
        pltpu.VMEM((16, 1, 128), jnp.int32),
        pltpu.VMEM((16, 1, 128), jnp.int32),
        pltpu.VMEM((12, 512), F32),
        pltpu.VMEM((12, 512), F32),
        pltpu.VMEM((12, 512), F32),
        pltpu.VMEM((12, 2, 512), F32),
        pltpu.SemaphoreType.DMA((14,)),
        pltpu.VMEM((288, 128), F32),
        pltpu.VMEM((288, 256), F32),
        pltpu.VMEM((128, 256), F32),
        pltpu.VMEM((60, ELEMS), F32),
        pltpu.VMEM((60, ELEMS), F32),
        pltpu.VMEM((64, ELEMS), F32),
        pltpu.VMEM((192, ELEMS), BF16),
        pltpu.VMEM((160, ELEMS), F32),
        pltpu.VMEM((64, ELEMS), F32),
        pltpu.VMEM((160, ELEMS), F32),
        pltpu.VMEM((160, ELEMS), F32),
        pltpu.VMEM((160, ELEMS), F32),
        pltpu.VMEM((8, ELEMS), F32),
        pltpu.VMEM((CHUNKS * ROWS, 256), BF16),
        pltpu.VMEM((7, 256, BLOCK), BF16),
        pltpu.VMEM((2048, 128), BF16),
        pltpu.VMEM((2048, 256), F32),
        pltpu.VMEM((64, 128), F32),
        pltpu.VMEM((64, 128), F32),
        pltpu.VMEM((256, BLOCK), BF16),
        pltpu.VMEM((8, 256, BLOCK), BF16),
        pltpu.VMEM((32 * ROWS, 256), BF16),
        pltpu.VMEM((ITERS, 4, ROWS, 128), F32),
        pltpu.VMEM((ITERS, 4, ROWS, 128), F32),
        pltpu.VMEM((128, 128), F32),
        pltpu.VMEM((128, 128), F32),
        pltpu.VMEM((128, 128), F32),
        pltpu.VMEM((128, 128), F32),
        pltpu.VMEM((BLOCK, 2048), BF16),
        pltpu.VMEM((768, 128), F32),
        pltpu.VMEM((384, 128), F32),
        pltpu.VMEM((384, 128), F32),
        pltpu.VMEM((384, 128), F32),
        pltpu.VMEM((384, 128), F32),
        pltpu.VMEM((384, 128), F32),
        pltpu.VMEM((384, 128), F32),
        pltpu.VMEM((384, 128), F32),
        pltpu.VMEM((384, 128), F32),
        pltpu.VMEM((768, 128), F32),
        pltpu.VMEM((4, ROWS, BLOCK), F32),
        pltpu.VMEM((256, 128), F32),
        pltpu.VMEM((256, 128), F32),
        pltpu.VMEM((256, 128), F32),
        pltpu.VMEM((256, 128), F32),
        pltpu.VMEM((256, 128), F32),
        pltpu.VMEM((32, 2048), F32),
        pltpu.VMEM((384, 256), BF16),
        pltpu.SemaphoreType.DMA((ITERS, 4)),
        pltpu.SemaphoreType.DMA((ITERS, 4)),
    ] + [pltpu.SemaphoreType.DMA((PD,))] * 16
    displacement, residual, rate = pl.pallas_call(
        kernel,
        out_shape=(
            jax.ShapeDtypeStruct((60, 1, ELEMS), F32),
            jax.ShapeDtypeStruct((60, 1, ELEMS), F32),
            jax.ShapeDtypeStruct((12, 512), F32),
        ),
        in_specs=[vmem] + [hbm] * 14,
        out_specs=(hbm, hbm, hbm),
        scratch_shapes=scratch,
        compiler_params=pltpu.CompilerParams(collective_id=0, has_side_effects=True, vmem_limit_bytes=64000 * 1024),
        name="window",
    )(
        fault_count.reshape(1, 1),
        right_side.reshape(60, 1, ELEMS),
        shear_modulus.reshape(1, ELEMS),
        lame_lambda.reshape(1, ELEMS),
        stiff_shear,
        stiff_lame,
        face_interp,
        neighbours.reshape(8, 1, BLOCK),
        fault_owner.reshape(16, 1, 128),
        fault_slot.reshape(16, 1, 128),
        fault_face.reshape(16, 1, 128),
        normal_stress,
        friction,
        state_factor,
        shear_load.transpose(1, 0, 2),
    )
    displacement, residual, rate = pl.pallas_call(
        hand_over,
        out_shape=(
            jax.ShapeDtypeStruct((480, 128), F32),
            jax.ShapeDtypeStruct((480, 128), F32),
            jax.ShapeDtypeStruct((12, 512), F32),
        ),
        in_specs=[hbm] * 3,
        out_specs=(hbm, hbm, hbm),
        scratch_shapes=[
            pltpu.VMEM((480, 128), F32),
            pltpu.VMEM((480, 128), F32),
            pltpu.VMEM((12, 512), F32),
            pltpu.SemaphoreType.DMA((2, 3)),
        ],
        compiler_params=pltpu.CompilerParams(vmem_limit_bytes=64000 * 1024),
        name="hand_over",
    )(displacement.reshape(480, 128), residual.reshape(480, 128), rate)
    return displacement.reshape(right_side.shape), residual.reshape(right_side.shape), rate


def solution(mesh):
    in_specs = (
        P(None, None, "along", "depth", None),
        P("along", "depth", None),
        P("along", "depth", None),
        P(),
        P(),
        P(),
        P("along", "depth", None),
        P("along", "depth"),
        P("along", "depth", None),
        P("along", "depth", None),
        P("along", "depth", None),
        P(None, ("along", "depth")),
        P(None, ("along", "depth")),
        P(None, ("along", "depth")),
        P(None, None, ("along", "depth")),
    )
    out_specs = (
        P(None, None, "along", "depth", None),
        P(None, None, "along", "depth", None),
        P(None, ("along", "depth")),
    )
    return jax.shard_map(
        on_device, mesh=mesh, in_specs=in_specs, out_specs=out_specs, check_vma=False
    )
```

```python
import functools

import jax
import jax.numpy as jnp
from jax import lax
from jax.experimental import pallas as pl
from jax.experimental.pallas import tpu as pltpu
from jax.sharding import PartitionSpec as P

ITERS = 4
NEWTON = 6
DAMPING = 0.5
TIME_STEP = 0.5
LOWER_EDGE = 0.25
UPPER_EDGE = 5.0
CENTER = 0.5 * (UPPER_EDGE + LOWER_EDGE)
SPREAD = 0.5 * (UPPER_EDGE - LOWER_EDGE)

MESH = pl.DeviceIdType.MESH
F32 = jnp.float32
BF16 = jnp.bfloat16
NT = (((1,), (1,)), ((), ()))

PA, PD = 8, 16
DEVS = PA * PD
ELEMS = 1024
ROWS = 40
BLOCK = 512
CHUNKS = 28
SPLIT = 18
SEND_SPLIT = 20
FAR_ROW = (4, 3, 5, 2, 6, 1, 7)
FAR_COLUMN = (6, 10, 7, 9, 2, 14, 5, 11, 8, 3, 13, 1, 15, 4, 12)
RANKS = 16


def coefficients():
    ratio = CENTER / SPREAD
    rho = 1.0 / ratio
    pairs = []
    for _ in range(ITERS):
        rho_next = 1.0 / (2.0 * ratio - rho)
        pairs.append((rho_next * rho, 2.0 * rho_next / SPREAD))
        rho = rho_next
    return pairs


def halves(value):
    high = value.astype(BF16)
    return high, (value - high.astype(F32)).astype(BF16)


def product(left, right):
    return jnp.dot(left, right, preferred_element_type=F32)


def onehot(digit, rows, columns):
    return (lax.broadcasted_iota(jnp.int32, (rows, columns), 0) == digit).astype(F32)


def choose(result, chunk, count, rows):
    width = result.shape[1]
    index = jnp.broadcast_to(chunk, (8, width))
    total = jnp.zeros((rows // 8, 8, width), F32)
    for s in range(count):
        part = result[s * rows : (s + 1) * rows].reshape(rows // 8, 8, width)
        total = jnp.where((index == s)[None], part, total)
    return total.reshape(rows, width)


def lane_gather(total, rows_ref, chunk, lanes, chunks, rows):
    columns = []
    for q in range(4):
        part = slice(q * 128, (q + 1) * 128)
        low = jnp.broadcast_to(lanes[:, part], (8, 128))
        index = jnp.broadcast_to(chunk[:, part], (8, 128))
        groups = [total[8 * g : 8 * g + 8, part] for g in range(rows // 8)]
        for s in chunks:
            t = s if len(chunks) + chunks[0] == 32 or s < 24 else s + 4
            mine = index == s
            for g in range(rows // 8):
                at = t // 8 * ROWS + 8 * g
                source = rows_ref[at : at + 8, t % 8 * 128 : t % 8 * 128 + 128]
                groups[g] = jnp.where(mine, jnp.take_along_axis(source, low, axis=1), groups[g])
        columns.append(jnp.concatenate(groups, axis=0))
    return jnp.concatenate(columns, axis=1)


def inverse_sinh(size, root):
    magnitude = jnp.log(jnp.abs(size) + root)
    return jnp.where(size < 0.0, -magnitude, magnitude)


def kernel(
    count_ref, load_hbm, shear_hbm, lame_hbm, stiff_shear_hbm, stiff_lame_hbm, interp_hbm, links_hbm, owner_hbm,
    slot_hbm, face_hbm, normal_hbm, friction_hbm, state_hbm, shear_load_hbm,
    disp_hbm, residual_hbm, rate_hbm,
    disp_ref, residual_ref, rate_ref, result_sem,
    load, shear_ref, lame_ref, stiff_shear, stiff_lame, interp, links, owner_ref, slot_ref, face_ref,
    normal_ref, friction_ref, state_ref, shear_load, fetch_sem,
    weight, weights, lift_pair, solved, left_over, field, stacked, trace, image, gathered, flux, flux_sum, alpha,
    table, hot_links, hot_owner, prefix, send_maps, face_maps, hot_send, hot_face, table_send, halo, rims,
    ids_out, ids_one, ids_mid, ids_in, hot_grid, params_pack, down_out, down_one, down_mid, down_in, over_out,
    over_one, over_mid, over_in, params,
    tractions, rate_pack, rate_out, rate_one, rate_mid, rate_in, wide, table_back,
    halo_send, halo_recv, ids_a, ids_b, ids_c, ids_d, par_a, par_b, par_c, par_d, par_e, par_f, par_g, par_h,
    rate_a, rate_b, rate_c, rate_d,
):
    along = lax.axis_index("along")
    depth = lax.axis_index("depth")

    operands = (
        (owner_hbm, owner_ref), (slot_hbm, slot_ref), (face_hbm, face_ref), (load_hbm, load), (shear_hbm, shear_ref),
        (lame_hbm, lame_ref), (stiff_shear_hbm, stiff_shear), (stiff_lame_hbm, stiff_lame), (interp_hbm, interp),
        (links_hbm, links), (normal_hbm, normal_ref), (friction_hbm, friction_ref), (state_hbm, state_ref),
        (shear_load_hbm, shear_load),
    )
    fetches = [
        pltpu.make_async_copy(source, target, fetch_sem.at[i]) for i, (source, target) in enumerate(operands)
    ]
    for fetch in fetches[0:3]:
        fetch.start()

    results = [
        pltpu.make_async_copy(source, target, result_sem.at[i])
        for i, (source, target) in enumerate(
            ((residual_ref, residual_hbm), (disp_ref, disp_hbm), (rate_ref, rate_hbm))
        )
    ]

    barrier = pltpu.get_barrier_semaphore()
    for i in range(1, PA):
        pl.semaphore_signal(barrier, inc=1, device_id=(lax.rem(along + i, PA), depth), device_id_type=MESH)
    for i in range(1, PD):
        pl.semaphore_signal(barrier, inc=1, device_id=(along, lax.rem(depth + i, PD)), device_id_type=MESH)

    for fetch in fetches[3:]:
        fetch.start()

    def row_copy(i, source, landing, size, sems, sending):
        peer = lax.rem(along + i, PA) if sending else lax.rem(along + PA - i, PA)
        place = along if sending else peer
        return pltpu.make_async_remote_copy(
            src_ref=source.at[pl.ds(pl.multiple_of(peer * size, 8), size)],
            dst_ref=landing.at[pl.ds(pl.multiple_of(place * size, 8), size)],
            send_sem=sems[0].at[i],
            recv_sem=sems[1].at[i],
            device_id=(peer, depth),
            device_id_type=MESH,
        )

    def column_copy(i, source, landing, size, sems, sending):
        peer = lax.rem(depth + i, PD) if sending else lax.rem(depth + PD - i, PD)
        place = depth if sending else peer
        return pltpu.make_async_remote_copy(
            src_ref=source.at[pl.ds(pl.multiple_of(peer * size, 8), size)],
            dst_ref=landing.at[pl.ds(pl.multiple_of(place * size, 8), size)],
            send_sem=sems[0].at[i],
            recv_sem=sems[1].at[i],
            device_id=(along, peer),
            device_id_type=MESH,
        )

    def go(kind, source, landing, size, sems):
        mine, order = (along, FAR_ROW) if kind is row_copy else (depth, FAR_COLUMN)
        for i in order:
            kind(i, source, landing, size, sems, True).start()
        own = pl.ds(pl.multiple_of(mine * size, 8), size)
        landing[own, :] = source[own, :]

    def arrive(kind, source, landing, size, sems):
        for i in range(1, PA if kind is row_copy else PD):
            kind(i, source, landing, size, sems, False).wait_recv()

    def drain(kind, source, landing, size, sems):
        for i in range(1, PA if kind is row_copy else PD):
            kind(i, source, landing, size, sems, True).wait_send()

    ids_first = (row_copy, ids_out, ids_one, 16, (ids_a, ids_b))
    ids_second = (column_copy, ids_mid, ids_in, 8, (ids_c, ids_d))
    down_first = (column_copy, down_out, down_one, 24, (par_a, par_b))
    down_second = (row_copy, down_mid, down_in, 48, (par_c, par_d))
    over_first = (row_copy, over_out, over_one, 48, (par_e, par_f))
    over_second = (column_copy, over_mid, over_in, 24, (par_g, par_h))
    rate_first = (row_copy, rate_out, rate_one, 32, (rate_a, rate_b))
    rate_second = (column_copy, rate_mid, rate_in, 16, (rate_c, rate_d))

    for fetch in fetches[0:3]:
        fetch.wait()
    count = count_ref[...]
    lane = lax.broadcasted_iota(jnp.int32, (1, 128), 1)
    for t in range(RANKS):
        live = (lane + t * 128) < count
        owner = jnp.where(live, owner_ref[t], -1)
        hot_owner[t * 128 : (t + 1) * 128, :] = onehot(owner, 128, 128).astype(BF16)
    row = lax.broadcasted_iota(jnp.int32, (128, 256), 0)
    column = lax.broadcasted_iota(jnp.int32, (128, 256), 1)
    earlier = ((row < column) | (column >= 128)).astype(F32).astype(BF16)
    prefix[...] = product(hot_owner[...], earlier)
    base = jnp.zeros((128, 128), F32)
    sent = jnp.zeros((64, 128), F32)
    ranked = []
    for t in range(RANKS):
        rows = slice(t * 128, (t + 1) * 128)
        hot = hot_owner[rows, :]
        rank = jnp.sum(hot.astype(F32) * (prefix[rows, 0:128] + base), axis=0, keepdims=True)
        base = base + prefix[rows, 128:256]
        live = ((lane + t * 128) < count).astype(F32)
        rank_live = jnp.where(live > 0.0, rank, -1.0).astype(jnp.int32)
        face = face_ref[t]
        slot = slot_ref[t]
        face_high = lax.shift_right_logical(face, 7)
        face_low = jnp.bitwise_and(face, 127)
        ranks = onehot(rank_live, RANKS, 128)
        values = jnp.concatenate(
            [
                ranks * face_high.astype(F32),
                ranks * face_low.astype(F32),
                ranks * (lax.shift_right_logical(slot, 4) + 1).astype(F32),
                ranks * jnp.bitwise_and(slot, 15).astype(F32),
            ],
            axis=0,
        ).astype(BF16)
        sent = sent + lax.dot_general(values, hot, NT, preferred_element_type=F32)
        ranked.append((rank, live))
    send_maps[...] = sent
    ids = 16.0 * sent[32:48] + sent[48:64] - 16.0
    ids_out[...] = jnp.transpose(jnp.concatenate([ids, jnp.zeros((112, 128), F32)], axis=0))

    pl.semaphore_wait(barrier, PA + PD - 2)
    go(*ids_first)

    placed = jnp.zeros((64, 128), F32)
    for t in range(RANKS):
        rank, live = ranked[t]
        face = face_ref[t]
        highs = onehot(lax.shift_right_logical(face, 7), 32, 128) * live
        values = jnp.concatenate([highs * (rank + 1.0), highs * owner_ref[t].astype(F32)], axis=0).astype(BF16)
        lows = onehot(jnp.bitwise_and(face, 127), 128, 128).astype(BF16)
        placed = placed + lax.dot_general(values, lows, NT, preferred_element_type=F32)
    face_maps[...] = placed

    sides = (
        (0, 1, (along + 1, depth), along < PA - 1, along > 0),
        (1, 0, (along - 1, depth), along > 0, along < PA - 1),
        (2, 3, (along, depth + 1), depth < PD - 1, depth > 0),
        (3, 2, (along, depth - 1), depth > 0, depth < PD - 1),
    )

    for side, piece, target, sends, receives in sides:
        @pl.when(jnp.logical_not(receives))
        def _():
            halo[:, side] = jnp.zeros((ITERS, ROWS, 128), F32)

    for fetch in fetches[3:]:
        fetch.wait()
    weight[...] = jnp.zeros_like(weight)
    for f in range(4):
        for c in range(3):
            weight[f * ROWS + c * 12 : f * ROWS + c * 12 + 12, c * 20 : c * 20 + 20] = interp[:, f, :]
    weight[160:220, 0:60] = stiff_shear[...]
    weight[224:284, 0:60] = stiff_lame[...]
    whole = weight[:, 0:64]
    high = whole.astype(BF16).astype(F32)
    rest = whole - high
    lift_pair[0:128, 0:128] = jnp.transpose(weight[0:128, :])
    lift_pair[0:128, 128:256] = jnp.transpose(weight[128:256, :])
    weights[:, 0:64] = high
    weights[:, 64:128] = high
    weights[:, 128:192] = rest
    lifter, lifter_rest = halves(lift_pair[0:64, 0:160])
    matrix = weights[:, 0:192].astype(BF16)
    rim_matrix = weights[120:160, 0:192].astype(BF16)
    rim_lifter, rim_rest = halves(lift_pair[0:64, 120:160])

    shear = shear_ref[...]
    lame = lame_ref[...]
    material = lame + 2.0 * shear
    inverse = 1.0 / material

    def lifted(ref):
        high, low = halves(ref[...])
        return product(lifter, high) + product(lifter_rest, high) + product(lifter, low)

    def build_links(b, carry):
        slots = links[b + b // 6]
        hot = onehot(jnp.bitwise_and(slots, 127), 128, BLOCK).astype(BF16)
        hot_links[b, 0:128, :] = hot
        hot_links[b, 128:256, :] = hot
        return carry

    right = load[...].reshape(60, ELEMS)
    left_over[...] = right
    field[60:64, :] = jnp.zeros((4, ELEMS), F32)
    field[0:60, :] = right * (inverse * (1.0 / CENTER))
    solved[...] = jnp.zeros_like(solved)
    flux_sum[...] = jnp.zeros_like(flux_sum)

    def halo_copy(i, side, piece, target):
        return pltpu.make_async_remote_copy(
            src_ref=rims.at[i, piece],
            dst_ref=halo.at[i, side],
            send_sem=halo_send.at[i, side],
            recv_sem=halo_recv.at[i, side],
            device_id=target,
            device_id_type=MESH,
        )

    def step(i, scale_old, scale_new, split, middle, between):
        first = i == 0
        now = field[...]
        high, low = halves(now)
        stacked[0:64, :] = high
        stacked[64:128, :] = low
        stacked[128:192, :] = high
        rim = product(rim_matrix, stacked[:, 0:BLOCK])
        for side, piece, target, sends, receives in sides:
            rims[i, piece] = rim[:, piece * 128 : piece * 128 + 128]
            if first:
                rims[i, piece, 36:37, :] = material[:, piece * 128 : piece * 128 + 128]

            @pl.when(sends)
            def _():
                halo_copy(i, side, piece, target).start()

        trace[...] = product(matrix[0:160], stacked[...])
        if first:
            for f in range(4):
                trace[f * ROWS + 36 : f * ROWS + 37, :] = material
        if first:
            lax.fori_loop(0, 7, build_links, 0)

        for p in range(SPLIT // 2):
            parts = []
            for s in (2 * p, 2 * p + 1):
                t = s if s < 24 else s + 4
                f, j = t // 8, t % 8
                parts.append(trace[f * ROWS : (f + 1) * ROWS, j * 128 : (j + 1) * 128])
            high, low = halves(jnp.concatenate(parts, axis=0))
            table[p * 80 : p * 80 + 80, 0:128] = high
            table[p * 80 : p * 80 + 80, 128:256] = low

        def block(b, carry):
            place = b + b // 6
            chunk = lax.shift_right_logical(links[place], 7)
            chunk = jnp.where(chunk >= 24, chunk - 4, chunk)
            result = product(table[0 : SPLIT * ROWS, :], hot_links[b])
            lanes = jnp.bitwise_and(links[place], 127)
            total = choose(result, chunk, SPLIT, ROWS)
            total = lane_gather(total, trace, chunk, lanes, range(SPLIT, CHUNKS), ROWS)
            f = place // 2
            half = place - 2 * f
            gathered[
                pl.ds(pl.multiple_of(f * ROWS, 8), ROWS), pl.ds(pl.multiple_of(half * BLOCK, BLOCK), BLOCK)
            ] = total
            return carry

        lax.fori_loop(0, split, block, 0)
        middle()
        if split < 7:
            lax.fori_loop(split, 7, block, 0)

        volume = product(matrix[160:288], stacked[...])
        image[...] = shear * volume[0:64] + lame * volume[64:128]
        solved[...] = solved[...] + now[0:60]

        inner = slice(BLOCK, ELEMS)
        outer = slice(0, BLOCK)
        if first:
            for f in range(3):
                alpha[f : f + 1, :] = 0.5 * (material + gathered[f * ROWS + 36 : f * ROWS + 37, :])
            alpha[3:4, inner] = 0.5 * (material[:, inner] + gathered[156:157, inner])
        for f in range(4):
            rows = slice(f * ROWS, (f + 1) * ROWS)
            columns = slice(0, ELEMS) if f < 3 else inner
            value = alpha[f : f + 1, columns] * (trace[rows, columns] - gathered[rows, columns])
            flux[rows, columns] = value
            flux_sum[rows, columns] = flux_sum[rows, columns] + value
        flux[120:160, outer] = jnp.zeros((ROWS, BLOCK), F32)
        left = left_over[...] - (image[...] + lifted(flux))[0:60]
        left_over[...] = left
        if i < ITERS - 1:
            field[0:60, :] = scale_old * now[0:60] + scale_new * (left * inverse)
        between()

        for side, piece, target, sends, receives in sides:
            @pl.when(receives)
            def _():
                halo_copy(i, side, piece, target).wait_recv()
        arrived = jnp.concatenate([halo[i, side] for side in range(4)], axis=1)
        if first:
            alpha[3:4, outer] = 0.5 * (material[:, outer] + arrived[36:37])
        value = alpha[3:4, outer] * (trace[120:160, outer] - arrived)
        flux_sum[120:160, outer] = flux_sum[120:160, outer] + value
        high, low = halves(value)
        late = (product(rim_lifter, high) + product(rim_rest, high) + product(rim_lifter, low))[0:60]
        left_over[:, outer] = left_over[:, outer] - late
        if i < ITERS - 1:
            field[0:60, outer] = field[0:60, outer] - scale_new * (late * inverse[:, outer])

    def nothing():
        pass

    def ids_middle():
        arrive(*ids_first)
        for a in range(PA):
            ids_mid[pl.ds(a, PD, stride=PA), :] = ids_one[a * PD : (a + 1) * PD, :]
        go(*ids_second)

    def answer():
        arrive(*ids_second)
        asked = jnp.transpose(ids_in[...])[0:RANKS].astype(jnp.int32)
        for rank in range(RANKS):
            hot_grid[:, rank * 128 : (rank + 1) * 128] = onehot(asked[rank : rank + 1], BLOCK, 128).astype(BF16)
        owned = jnp.concatenate(
            [normal_ref[...] * friction_ref[...], state_ref[...], shear_load[:, 0, :], shear_load[:, 1, :]], axis=0
        )
        high = owned.astype(BF16).astype(F32)
        both = product(jnp.concatenate([high, owned - high], axis=0).astype(BF16), hot_grid[...])
        for rank in range(RANKS):
            lanes = slice(rank * 128, (rank + 1) * 128)
            params_pack[rank * 48 : (rank + 1) * 48, :] = both[0:48, lanes] + both[48:96, lanes]
        for j in range(3):
            down_out[pl.ds(j, 128, stride=3), :] = jnp.transpose(params_pack[j * 128 : (j + 1) * 128, :])
        go(*down_first)
        for j in range(3):
            turned = jnp.transpose(params_pack[(3 + j) * 128 : (4 + j) * 128, :])
            for d in range(PD):
                over_out[pl.ds(d * 3 + j, PA, stride=48), :] = turned[d * PA : (d + 1) * PA]
        go(*over_first)

    def params_middle():
        arrive(*down_first)
        for d in range(PD):
            for j in range(3):
                down_mid[pl.ds(d * 3 + j, PA, stride=48), :] = down_one[pl.ds(d * 24 + j, PA, stride=3), :]
        go(*down_second)
        arrive(*over_first)
        for a in range(PA):
            for j in range(3):
                over_mid[pl.ds(a * 3 + j, PD, stride=24), :] = over_one[pl.ds(a * 48 + j, PD, stride=3), :]
        go(*over_second)

    pairs = coefficients()
    step(0, *pairs[0], 4, ids_middle, nothing)
    step(1, *pairs[1], 7, nothing, answer)
    step(2, *pairs[2], 7, nothing, nothing)
    step(3, *pairs[3], 0, params_middle, nothing)
    residual_ref[...] = left_over[...].reshape(60, 1, ELEMS)
    results[0].start()

    for p in range(SEND_SPLIT // 2):
        parts = []
        for s in (2 * p, 2 * p + 1):
            f, j = s // 8, s % 8
            parts.append(flux_sum[f * ROWS : (f + 1) * ROWS, j * 128 : (j + 1) * 128])
        high, low = halves(jnp.concatenate(parts, axis=0))
        table_send[p * 80 : p * 80 + 80, 0:128] = high
        table_send[p * 80 : p * 80 + 80, 128:256] = low
    for b in range(4):
        high = jnp.concatenate([send_maps[4 * b + j : 4 * b + j + 1, :] for j in range(4)], axis=1)
        low = jnp.concatenate([send_maps[16 + 4 * b + j : 17 + 4 * b + j, :] for j in range(4)], axis=1)
        hot = onehot(low.astype(jnp.int32), 128, BLOCK).astype(BF16)
        hot_send[0:128, :] = hot
        hot_send[128:256, :] = hot
        result = product(table_send[0 : SEND_SPLIT * ROWS, :], hot_send[...])
        chunk = high.astype(jnp.int32)
        total = choose(result, chunk, SEND_SPLIT, ROWS)
        tractions[b] = lane_gather(total, flux_sum, chunk, low.astype(jnp.int32), range(SEND_SPLIT, 32), ROWS)

    def build_face(b, carry):
        low = jnp.concatenate([face_maps[pl.ds(32 + 4 * b + j, 1), :] for j in range(4)], axis=1)
        hot = onehot(low.astype(jnp.int32), 128, BLOCK).astype(BF16)
        hot_face[b, 0:128, :] = hot
        hot_face[b, 128:256, :] = hot
        return carry

    lax.fori_loop(0, 8, build_face, 0)
    rate_pack[...] = jnp.zeros_like(rate_pack)

    def solve(b):
        owned = jnp.concatenate([params[(4 * b + j) * 48 : (4 * b + j + 1) * 48, :] for j in range(4)], axis=1)
        traction = tractions[b]
        state = owned[12:24]
        strike = owned[24:36] + traction[0:12]
        updip = owned[36:48] + traction[12:24]
        magnitude = jnp.sqrt(strike * strike + updip * updip)
        resist = owned[0:12] * (1.0 + 0.5 * jnp.tanh(traction[24:36]))
        steep = resist * state
        velocity = magnitude / (DAMPING + steep)
        for _ in range(NEWTON - 1):
            scaled = state * velocity
            square = 1.0 + scaled * scaled
            inverse_root = lax.rsqrt(square)
            misfit = magnitude - DAMPING * velocity - resist * inverse_sinh(scaled, square * inverse_root)
            velocity = velocity + misfit / (DAMPING + steep * inverse_root)
        for j in range(4):
            rank = 4 * b + j
            rate_pack[rank * 16 : rank * 16 + 12, :] = velocity[:, j * 128 : (j + 1) * 128]
        return velocity, magnitude, strike, updip

    arrive(*down_second)
    for j in range(3):
        params[j * 128 : (j + 1) * 128, :] = jnp.transpose(down_in[pl.ds(j, 128, stride=3), :])
    arrive(*over_second)
    for j in range(3):
        parts = [over_in[pl.ds(a * 3 + j, PD, stride=24), :] for a in range(PA)]
        params[(3 + j) * 128 : (4 + j) * 128, :] = jnp.transpose(jnp.concatenate(parts, axis=0))
    motion = [solve(b) for b in range(4)]
    for j in range(2):
        rate_out[pl.ds(j, 128, stride=2), :] = jnp.transpose(rate_pack[j * 128 : (j + 1) * 128, :])
    go(*rate_first)

    for b, (velocity, magnitude, strike, updip) in enumerate(motion):
        factor = TIME_STEP * velocity / jnp.maximum(magnitude, 1.0)
        slip = jnp.concatenate([factor * strike, factor * updip], axis=0)
        for j in (0, 2):
            parts = [slip[:, j * 128 : (j + 1) * 128], slip[:, (j + 1) * 128 : (j + 2) * 128]]
            high, low = halves(jnp.concatenate(parts, axis=0))
            at = (4 * b + j) * 24
            table_back[at : at + 48, 0:128] = high
            table_back[at : at + 48, 128:256] = low

    flux[...] = jnp.zeros_like(flux)

    def place_back(b, carry):
        rank = jnp.concatenate([face_maps[pl.ds(4 * b + j, 1), :] for j in range(4)], axis=1)
        result = product(table_back[...], hot_face[b])
        f = b // 2
        half = b - 2 * f
        flux[
            pl.ds(pl.multiple_of(f * ROWS, 8), 24), pl.ds(pl.multiple_of(half * BLOCK, BLOCK), BLOCK)
        ] = choose(result, rank.astype(jnp.int32) - 1, RANKS, 24)
        return carry

    lax.fori_loop(0, 8, place_back, 0)

    arrive(*rate_first)
    for a in range(PA):
        for j in range(2):
            rate_mid[pl.ds(a * 2 + j, PD, stride=16), :] = rate_one[pl.ds(a * 32 + j, PD, stride=2), :]
    go(*rate_second)
    disp_ref[...] = (solved[...] + 0.5 * lifted(flux)[0:60]).reshape(60, 1, ELEMS)
    results[1].start()
    for each in (ids_first, ids_second, down_first, down_second, over_first, over_second, rate_first):
        drain(*each)
    for i in range(ITERS):
        for side, piece, target, sends, receives in sides:
            @pl.when(sends)
            def _():
                halo_copy(i, side, piece, target).wait_send()

    arrive(*rate_second)
    for j in range(2):
        value = jnp.transpose(rate_in[pl.ds(j, 128, stride=2), :])
        high = value.astype(BF16).astype(F32)
        low = value - high
        for r in range(8):
            lanes = slice((8 * j + r) * 128, (8 * j + r + 1) * 128)
            wide[0:16, lanes] = high[r * 16 : (r + 1) * 16]
            wide[16:32, lanes] = low[r * 16 : (r + 1) * 16]
    both = lax.dot_general(wide[...].astype(BF16), hot_grid[...], NT, preferred_element_type=F32)
    rate_ref[...] = both[0:12] + both[16:28]
    results[2].start()
    drain(*rate_second)
    for result in results:
        result.wait()


def hand_over(disp_ref, residual_ref, rate_ref, disp_out, residual_out, rate_out, disp, residual, rate, sems):
    ways = ((disp_ref, disp, disp_out), (residual_ref, residual, residual_out), (rate_ref, rate, rate_out))
    inward = [pltpu.make_async_copy(way[0], way[1], sems.at[0, i]) for i, way in enumerate(ways)]
    outward = [pltpu.make_async_copy(way[1], way[2], sems.at[1, i]) for i, way in enumerate(ways)]
    for copy in inward:
        copy.start()
    for first, second in zip(inward, outward):
        first.wait()
        second.start()
    for copy in outward:
        copy.wait()


def on_device(
    right_side,
    shear_modulus,
    lame_lambda,
    stiff_shear,
    stiff_lame,
    face_interp,
    neighbours,
    fault_count,
    fault_owner,
    fault_slot,
    fault_face,
    normal_stress,
    friction,
    state_factor,
    shear_load,
):
    vmem = pl.BlockSpec(memory_space=pltpu.VMEM)
    hbm = pl.BlockSpec(memory_space=pltpu.HBM)
    scratch = [
        pltpu.VMEM((60, 1, ELEMS), F32),
        pltpu.VMEM((60, 1, ELEMS), F32),
        pltpu.VMEM((12, 512), F32),
        pltpu.SemaphoreType.DMA((3,)),
        pltpu.VMEM((60, 1, ELEMS), F32),
        pltpu.VMEM((1, ELEMS), F32),
        pltpu.VMEM((1, ELEMS), F32),
        pltpu.VMEM((60, 60), F32),
        pltpu.VMEM((60, 60), F32),
        pltpu.VMEM((12, 4, 20), F32),
        pltpu.VMEM((8, 1, BLOCK), jnp.int32),
        pltpu.VMEM((16, 1, 128), jnp.int32),
        pltpu.VMEM((16, 1, 128), jnp.int32),
        pltpu.VMEM((16, 1, 128), jnp.int32),
        pltpu.VMEM((12, 512), F32),
        pltpu.VMEM((12, 512), F32),
        pltpu.VMEM((12, 512), F32),
        pltpu.VMEM((12, 2, 512), F32),
        pltpu.SemaphoreType.DMA((14,)),
        pltpu.VMEM((288, 128), F32),
        pltpu.VMEM((288, 256), F32),
        pltpu.VMEM((128, 256), F32),
        pltpu.VMEM((60, ELEMS), F32),
        pltpu.VMEM((60, ELEMS), F32),
        pltpu.VMEM((64, ELEMS), F32),
        pltpu.VMEM((192, ELEMS), BF16),
        pltpu.VMEM((160, ELEMS), F32),
        pltpu.VMEM((64, ELEMS), F32),
        pltpu.VMEM((160, ELEMS), F32),
        pltpu.VMEM((160, ELEMS), F32),
        pltpu.VMEM((160, ELEMS), F32),
        pltpu.VMEM((8, ELEMS), F32),
        pltpu.VMEM((CHUNKS * ROWS, 256), BF16),
        pltpu.VMEM((7, 256, BLOCK), BF16),
        pltpu.VMEM((2048, 128), BF16),
        pltpu.VMEM((2048, 256), F32),
        pltpu.VMEM((64, 128), F32),
        pltpu.VMEM((64, 128), F32),
        pltpu.VMEM((256, BLOCK), BF16),
        pltpu.VMEM((8, 256, BLOCK), BF16),
        pltpu.VMEM((32 * ROWS, 256), BF16),
        pltpu.VMEM((ITERS, 4, ROWS, 128), F32),
        pltpu.VMEM((ITERS, 4, ROWS, 128), F32),
        pltpu.VMEM((128, 128), F32),
        pltpu.VMEM((128, 128), F32),
        pltpu.VMEM((128, 128), F32),
        pltpu.VMEM((128, 128), F32),
        pltpu.VMEM((BLOCK, 2048), BF16),
        pltpu.VMEM((768, 128), F32),
        pltpu.VMEM((384, 128), F32),
        pltpu.VMEM((384, 128), F32),
        pltpu.VMEM((384, 128), F32),
        pltpu.VMEM((384, 128), F32),
        pltpu.VMEM((384, 128), F32),
        pltpu.VMEM((384, 128), F32),
        pltpu.VMEM((384, 128), F32),
        pltpu.VMEM((384, 128), F32),
        pltpu.VMEM((768, 128), F32),
        pltpu.VMEM((4, ROWS, BLOCK), F32),
        pltpu.VMEM((256, 128), F32),
        pltpu.VMEM((256, 128), F32),
        pltpu.VMEM((256, 128), F32),
        pltpu.VMEM((256, 128), F32),
        pltpu.VMEM((256, 128), F32),
        pltpu.VMEM((32, 2048), F32),
        pltpu.VMEM((384, 256), BF16),
        pltpu.SemaphoreType.DMA((ITERS, 4)),
        pltpu.SemaphoreType.DMA((ITERS, 4)),
    ] + [pltpu.SemaphoreType.DMA((PD,))] * 16
    displacement, residual, rate = pl.pallas_call(
        kernel,
        out_shape=(
            jax.ShapeDtypeStruct((60, 1, ELEMS), F32),
            jax.ShapeDtypeStruct((60, 1, ELEMS), F32),
            jax.ShapeDtypeStruct((12, 512), F32),
        ),
        in_specs=[vmem] + [hbm] * 14,
        out_specs=(hbm, hbm, hbm),
        scratch_shapes=scratch,
        compiler_params=pltpu.CompilerParams(collective_id=0, has_side_effects=True, vmem_limit_bytes=64000 * 1024),
        name="window",
    )(
        fault_count.reshape(1, 1),
        right_side.reshape(60, 1, ELEMS),
        shear_modulus.reshape(1, ELEMS),
        lame_lambda.reshape(1, ELEMS),
        stiff_shear,
        stiff_lame,
        face_interp,
        neighbours.reshape(8, 1, BLOCK),
        fault_owner.reshape(16, 1, 128),
        fault_slot.reshape(16, 1, 128),
        fault_face.reshape(16, 1, 128),
        normal_stress,
        friction,
        state_factor,
        shear_load.transpose(1, 0, 2),
    )
    displacement, residual, rate = pl.pallas_call(
        hand_over,
        out_shape=(
            jax.ShapeDtypeStruct((480, 128), F32),
            jax.ShapeDtypeStruct((480, 128), F32),
            jax.ShapeDtypeStruct((12, 512), F32),
        ),
        in_specs=[hbm] * 3,
        out_specs=(hbm, hbm, hbm),
        scratch_shapes=[
            pltpu.VMEM((480, 128), F32),
            pltpu.VMEM((480, 128), F32),
            pltpu.VMEM((12, 512), F32),
            pltpu.SemaphoreType.DMA((2, 3)),
        ],
        compiler_params=pltpu.CompilerParams(vmem_limit_bytes=64000 * 1024),
        name="hand_over",
    )(displacement.reshape(480, 128), residual.reshape(480, 128), rate)
    return displacement.reshape(right_side.shape), residual.reshape(right_side.shape), rate


def solution(mesh):
    in_specs = (
        P(None, None, "along", "depth", None),
        P("along", "depth", None),
        P("along", "depth", None),
        P(),
        P(),
        P(),
        P("along", "depth", None),
        P("along", "depth"),
        P("along", "depth", None),
        P("along", "depth", None),
        P("along", "depth", None),
        P(None, ("along", "depth")),
        P(None, ("along", "depth")),
        P(None, ("along", "depth")),
        P(None, None, ("along", "depth")),
    )
    out_specs = (
        P(None, None, "along", "depth", None),
        P(None, None, "along", "depth", None),
        P(None, ("along", "depth")),
    )
    return jax.shard_map(
        on_device, mesh=mesh, in_specs=in_specs, out_specs=out_specs, check_vma=False
    )
```

```python
import functools

import jax
import jax.numpy as jnp
from jax import lax
from jax.experimental import pallas as pl
from jax.experimental.pallas import tpu as pltpu
from jax.sharding import PartitionSpec as P

ITERS = 4
NEWTON = 6
DAMPING = 0.5
TIME_STEP = 0.5
LOWER_EDGE = 0.25
UPPER_EDGE = 5.0
CENTER = 0.5 * (UPPER_EDGE + LOWER_EDGE)
SPREAD = 0.5 * (UPPER_EDGE - LOWER_EDGE)

MESH = pl.DeviceIdType.MESH
F32 = jnp.float32
BF16 = jnp.bfloat16
NT = (((1,), (1,)), ((), ()))

PA, PD = 8, 16
DEVS = PA * PD
ELEMS = 1024
ROWS = 40
BLOCK = 512
CHUNKS = 28
SPLIT = 18
SEND_SPLIT = 20
FAR_ROW = (4, 3, 5, 2, 6, 1, 7)
FAR_COLUMN = (6, 10, 7, 9, 2, 14, 5, 11, 8, 3, 13, 1, 15, 4, 12)
RANKS = 16


def coefficients():
    ratio = CENTER / SPREAD
    rho = 1.0 / ratio
    pairs = []
    for _ in range(ITERS):
        rho_next = 1.0 / (2.0 * ratio - rho)
        pairs.append((rho_next * rho, 2.0 * rho_next / SPREAD))
        rho = rho_next
    return pairs


def halves(value):
    high = value.astype(BF16)
    return high, (value - high.astype(F32)).astype(BF16)


def product(left, right):
    return jnp.dot(left, right, preferred_element_type=F32)


def onehot(digit, rows, columns):
    return (lax.broadcasted_iota(jnp.int32, (rows, columns), 0) == digit).astype(F32)


def choose(result, chunk, count, rows):
    width = result.shape[1]
    index = jnp.broadcast_to(chunk, (8, width))
    total = jnp.zeros((rows // 8, 8, width), F32)
    for s in range(count):
        part = result[s * rows : (s + 1) * rows].reshape(rows // 8, 8, width)
        total = jnp.where((index == s)[None], part, total)
    return total.reshape(rows, width)


def lane_gather(total, rows_ref, chunk, lanes, chunks, rows):
    columns = []
    for q in range(4):
        part = slice(q * 128, (q + 1) * 128)
        low = jnp.broadcast_to(lanes[:, part], (8, 128))
        index = jnp.broadcast_to(chunk[:, part], (8, 128))
        groups = [total[8 * g : 8 * g + 8, part] for g in range(rows // 8)]
        for s in chunks:
            t = s if len(chunks) + chunks[0] == 32 or s < 24 else s + 4
            mine = index == s
            for g in range(rows // 8):
                at = t // 8 * ROWS + 8 * g
                source = rows_ref[at : at + 8, t % 8 * 128 : t % 8 * 128 + 128]
                groups[g] = jnp.where(mine, jnp.take_along_axis(source, low, axis=1), groups[g])
        columns.append(jnp.concatenate(groups, axis=0))
    return jnp.concatenate(columns, axis=1)


def inverse_sinh(size, root):
    magnitude = jnp.log(jnp.abs(size) + root)
    return jnp.where(size < 0.0, -magnitude, magnitude)


def kernel(
    count_ref, load_hbm, shear_hbm, lame_hbm, stiff_shear_hbm, stiff_lame_hbm, interp_hbm, links_hbm, owner_hbm,
    slot_hbm, face_hbm, normal_hbm, friction_hbm, state_hbm, shear_load_hbm,
    disp_hbm, residual_hbm, rate_hbm,
    disp_ref, residual_ref, rate_ref, result_sem,
    load, shear_ref, lame_ref, stiff_shear, stiff_lame, interp, links, owner_ref, slot_ref, face_ref,
    normal_ref, friction_ref, state_ref, shear_load, fetch_sem,
    weight, weights, lift_pair, solved, left_over, field, stacked, trace, image, gathered, flux, flux_sum, alpha,
    table, hot_links, hot_owner, prefix, send_maps, face_maps, hot_send, hot_face, table_send, halo, rims,
    ids_out, ids_one, ids_mid, ids_in, hot_grid, params_pack, down_out, down_one, down_mid, down_in, over_out,
    over_one, over_mid, over_in, params,
    tractions, rate_pack, rate_out, rate_one, rate_mid, rate_in, wide, table_back,
    halo_send, halo_recv, ids_a, ids_b, ids_c, ids_d, par_a, par_b, par_c, par_d, par_e, par_f, par_g, par_h,
    rate_a, rate_b, rate_c, rate_d,
):
    along = lax.axis_index("along")
    depth = lax.axis_index("depth")

    operands = (
        (owner_hbm, owner_ref), (slot_hbm, slot_ref), (face_hbm, face_ref), (load_hbm, load), (shear_hbm, shear_ref),
        (lame_hbm, lame_ref), (stiff_shear_hbm, stiff_shear), (stiff_lame_hbm, stiff_lame), (interp_hbm, interp),
        (links_hbm, links), (normal_hbm, normal_ref), (friction_hbm, friction_ref), (state_hbm, state_ref),
        (shear_load_hbm, shear_load),
    )
    fetches = [
        pltpu.make_async_copy(source, target, fetch_sem.at[i]) for i, (source, target) in enumerate(operands)
    ]
    for fetch in fetches[0:3]:
        fetch.start()

    results = [
        pltpu.make_async_copy(source, target, result_sem.at[i])
        for i, (source, target) in enumerate(
            ((residual_ref, residual_hbm), (disp_ref, disp_hbm), (rate_ref, rate_hbm))
        )
    ]

    barrier = pltpu.get_barrier_semaphore()
    for i in FAR_ROW:
        pl.semaphore_signal(barrier, inc=1, device_id=(lax.rem(along + i, PA), depth), device_id_type=MESH)
    for i in FAR_COLUMN:
        pl.semaphore_signal(barrier, inc=1, device_id=(along, lax.rem(depth + i, PD)), device_id_type=MESH)

    for fetch in fetches[3:]:
        fetch.start()

    def row_copy(i, source, landing, size, sems, sending):
        peer = lax.rem(along + i, PA) if sending else lax.rem(along + PA - i, PA)
        place = along if sending else peer
        return pltpu.make_async_remote_copy(
            src_ref=source.at[pl.ds(pl.multiple_of(peer * size, 8), size)],
            dst_ref=landing.at[pl.ds(pl.multiple_of(place * size, 8), size)],
            send_sem=sems[0].at[i],
            recv_sem=sems[1].at[i],
            device_id=(peer, depth),
            device_id_type=MESH,
        )

    def column_copy(i, source, landing, size, sems, sending):
        peer = lax.rem(depth + i, PD) if sending else lax.rem(depth + PD - i, PD)
        place = depth if sending else peer
        return pltpu.make_async_remote_copy(
            src_ref=source.at[pl.ds(pl.multiple_of(peer * size, 8), size)],
            dst_ref=landing.at[pl.ds(pl.multiple_of(place * size, 8), size)],
            send_sem=sems[0].at[i],
            recv_sem=sems[1].at[i],
            device_id=(along, peer),
            device_id_type=MESH,
        )

    def go(kind, source, landing, size, sems):
        mine, order = (along, FAR_ROW) if kind is row_copy else (depth, FAR_COLUMN)
        for i in order:
            kind(i, source, landing, size, sems, True).start()
        own = pl.ds(pl.multiple_of(mine * size, 8), size)
        landing[own, :] = source[own, :]

    def arrive(kind, source, landing, size, sems):
        for i in range(1, PA if kind is row_copy else PD):
            kind(i, source, landing, size, sems, False).wait_recv()

    def drain(kind, source, landing, size, sems):
        for i in range(1, PA if kind is row_copy else PD):
            kind(i, source, landing, size, sems, True).wait_send()

    ids_first = (row_copy, ids_out, ids_one, 16, (ids_a, ids_b))
    ids_second = (column_copy, ids_mid, ids_in, 8, (ids_c, ids_d))
    down_first = (column_copy, down_out, down_one, 24, (par_a, par_b))
    down_second = (row_copy, down_mid, down_in, 48, (par_c, par_d))
    over_first = (row_copy, over_out, over_one, 48, (par_e, par_f))
    over_second = (column_copy, over_mid, over_in, 24, (par_g, par_h))
    rate_first = (row_copy, rate_out, rate_one, 32, (rate_a, rate_b))
    rate_second = (column_copy, rate_mid, rate_in, 16, (rate_c, rate_d))

    for fetch in fetches[0:3]:
        fetch.wait()
    count = count_ref[...]
    lane = lax.broadcasted_iota(jnp.int32, (1, 128), 1)
    for t in range(RANKS):
        live = (lane + t * 128) < count
        owner = jnp.where(live, owner_ref[t], -1)
        hot_owner[t * 128 : (t + 1) * 128, :] = onehot(owner, 128, 128).astype(BF16)
    row = lax.broadcasted_iota(jnp.int32, (128, 256), 0)
    column = lax.broadcasted_iota(jnp.int32, (128, 256), 1)
    earlier = ((row < column) | (column >= 128)).astype(F32).astype(BF16)
    prefix[...] = product(hot_owner[...], earlier)
    base = jnp.zeros((128, 128), F32)
    sent = jnp.zeros((64, 128), F32)
    ranked = []
    for t in range(RANKS):
        rows = slice(t * 128, (t + 1) * 128)
        hot = hot_owner[rows, :]
        rank = jnp.sum(hot.astype(F32) * (prefix[rows, 0:128] + base), axis=0, keepdims=True)
        base = base + prefix[rows, 128:256]
        live = ((lane + t * 128) < count).astype(F32)
        rank_live = jnp.where(live > 0.0, rank, -1.0).astype(jnp.int32)
        face = face_ref[t]
        slot = slot_ref[t]
        face_high = lax.shift_right_logical(face, 7)
        face_low = jnp.bitwise_and(face, 127)
        ranks = onehot(rank_live, RANKS, 128)
        values = jnp.concatenate(
            [
                ranks * face_high.astype(F32),
                ranks * face_low.astype(F32),
                ranks * (lax.shift_right_logical(slot, 4) + 1).astype(F32),
                ranks * jnp.bitwise_and(slot, 15).astype(F32),
            ],
            axis=0,
        ).astype(BF16)
        sent = sent + lax.dot_general(values, hot, NT, preferred_element_type=F32)
        ranked.append((rank, live))
    send_maps[...] = sent
    ids = 16.0 * sent[32:48] + sent[48:64] - 16.0
    ids_out[...] = jnp.transpose(jnp.concatenate([ids, jnp.zeros((112, 128), F32)], axis=0))

    pl.semaphore_wait(barrier, PA + PD - 2)
    go(*ids_first)

    placed = jnp.zeros((64, 128), F32)
    for t in range(RANKS):
        rank, live = ranked[t]
        face = face_ref[t]
        highs = onehot(lax.shift_right_logical(face, 7), 32, 128) * live
        values = jnp.concatenate([highs * (rank + 1.0), highs * owner_ref[t].astype(F32)], axis=0).astype(BF16)
        lows = onehot(jnp.bitwise_and(face, 127), 128, 128).astype(BF16)
        placed = placed + lax.dot_general(values, lows, NT, preferred_element_type=F32)
    face_maps[...] = placed

    sides = (
        (0, 1, (along + 1, depth), along < PA - 1, along > 0),
        (1, 0, (along - 1, depth), along > 0, along < PA - 1),
        (2, 3, (along, depth + 1), depth < PD - 1, depth > 0),
        (3, 2, (along, depth - 1), depth > 0, depth < PD - 1),
    )

    for side, piece, target, sends, receives in sides:
        @pl.when(jnp.logical_not(receives))
        def _():
            halo[:, side] = jnp.zeros((ITERS, ROWS, 128), F32)

    for fetch in fetches[3:]:
        fetch.wait()
    weight[...] = jnp.zeros_like(weight)
    for f in range(4):
        for c in range(3):
            weight[f * ROWS + c * 12 : f * ROWS + c * 12 + 12, c * 20 : c * 20 + 20] = interp[:, f, :]
    weight[160:220, 0:60] = stiff_shear[...]
    weight[224:284, 0:60] = stiff_lame[...]
    whole = weight[:, 0:64]
    high = whole.astype(BF16).astype(F32)
    rest = whole - high
    lift_pair[0:128, 0:128] = jnp.transpose(weight[0:128, :])
    lift_pair[0:128, 128:256] = jnp.transpose(weight[128:256, :])
    weights[:, 0:64] = high
    weights[:, 64:128] = high
    weights[:, 128:192] = rest
    lifter, lifter_rest = halves(lift_pair[0:64, 0:160])
    matrix = weights[:, 0:192].astype(BF16)
    rim_matrix = weights[120:160, 0:192].astype(BF16)
    rim_lifter, rim_rest = halves(lift_pair[0:64, 120:160])

    shear = shear_ref[...]
    lame = lame_ref[...]
    material = lame + 2.0 * shear
    inverse = 1.0 / material

    def lifted(ref):
        high, low = halves(ref[...])
        return product(lifter, high) + product(lifter_rest, high) + product(lifter, low)

    def build_links(b, carry):
        slots = links[b + b // 6]
        hot = onehot(jnp.bitwise_and(slots, 127), 128, BLOCK).astype(BF16)
        hot_links[b, 0:128, :] = hot
        hot_links[b, 128:256, :] = hot
        return carry

    right = load[...].reshape(60, ELEMS)
    left_over[...] = right
    field[60:64, :] = jnp.zeros((4, ELEMS), F32)
    field[0:60, :] = right * (inverse * (1.0 / CENTER))
    solved[...] = jnp.zeros_like(solved)
    flux_sum[...] = jnp.zeros_like(flux_sum)

    def halo_copy(i, side, piece, target):
        return pltpu.make_async_remote_copy(
            src_ref=rims.at[i, piece],
            dst_ref=halo.at[i, side],
            send_sem=halo_send.at[i, side],
            recv_sem=halo_recv.at[i, side],
            device_id=target,
            device_id_type=MESH,
        )

    def step(i, scale_old, scale_new, split, middle, between):
        first = i == 0
        now = field[...]
        high, low = halves(now)
        stacked[0:64, :] = high
        stacked[64:128, :] = low
        stacked[128:192, :] = high
        rim = product(rim_matrix, stacked[:, 0:BLOCK])
        for side, piece, target, sends, receives in sides:
            rims[i, piece] = rim[:, piece * 128 : piece * 128 + 128]
            if first:
                rims[i, piece, 36:37, :] = material[:, piece * 128 : piece * 128 + 128]

            @pl.when(sends)
            def _():
                halo_copy(i, side, piece, target).start()

        trace[...] = product(matrix[0:160], stacked[...])
        if first:
            for f in range(4):
                trace[f * ROWS + 36 : f * ROWS + 37, :] = material
        if first:
            lax.fori_loop(0, 7, build_links, 0)

        for p in range(SPLIT // 2):
            parts = []
            for s in (2 * p, 2 * p + 1):
                t = s if s < 24 else s + 4
                f, j = t // 8, t % 8
                parts.append(trace[f * ROWS : (f + 1) * ROWS, j * 128 : (j + 1) * 128])
            high, low = halves(jnp.concatenate(parts, axis=0))
            table[p * 80 : p * 80 + 80, 0:128] = high
            table[p * 80 : p * 80 + 80, 128:256] = low

        def block(b, carry):
            place = b + b // 6
            chunk = lax.shift_right_logical(links[place], 7)
            chunk = jnp.where(chunk >= 24, chunk - 4, chunk)
            result = product(table[0 : SPLIT * ROWS, :], hot_links[b])
            lanes = jnp.bitwise_and(links[place], 127)
            total = choose(result, chunk, SPLIT, ROWS)
            total = lane_gather(total, trace, chunk, lanes, range(SPLIT, CHUNKS), ROWS)
            f = place // 2
            half = place - 2 * f
            gathered[
                pl.ds(pl.multiple_of(f * ROWS, 8), ROWS), pl.ds(pl.multiple_of(half * BLOCK, BLOCK), BLOCK)
            ] = total
            return carry

        lax.fori_loop(0, split, block, 0)
        middle()
        if split < 7:
            lax.fori_loop(split, 7, block, 0)

        volume = product(matrix[160:288], stacked[...])
        image[...] = shear * volume[0:64] + lame * volume[64:128]
        solved[...] = solved[...] + now[0:60]

        inner = slice(BLOCK, ELEMS)
        outer = slice(0, BLOCK)
        if first:
            for f in range(3):
                alpha[f : f + 1, :] = 0.5 * (material + gathered[f * ROWS + 36 : f * ROWS + 37, :])
            alpha[3:4, inner] = 0.5 * (material[:, inner] + gathered[156:157, inner])
        for f in range(4):
            rows = slice(f * ROWS, (f + 1) * ROWS)
            columns = slice(0, ELEMS) if f < 3 else inner
            value = alpha[f : f + 1, columns] * (trace[rows, columns] - gathered[rows, columns])
            flux[rows, columns] = value
            flux_sum[rows, columns] = flux_sum[rows, columns] + value
        flux[120:160, outer] = jnp.zeros((ROWS, BLOCK), F32)
        left = left_over[...] - (image[...] + lifted(flux))[0:60]
        left_over[...] = left
        if i < ITERS - 1:
            field[0:60, :] = scale_old * now[0:60] + scale_new * (left * inverse)
        between()

        for side, piece, target, sends, receives in sides:
            @pl.when(receives)
            def _():
                halo_copy(i, side, piece, target).wait_recv()
        arrived = jnp.concatenate([halo[i, side] for side in range(4)], axis=1)
        if first:
            alpha[3:4, outer] = 0.5 * (material[:, outer] + arrived[36:37])
        value = alpha[3:4, outer] * (trace[120:160, outer] - arrived)
        flux_sum[120:160, outer] = flux_sum[120:160, outer] + value
        high, low = halves(value)
        late = (product(rim_lifter, high) + product(rim_rest, high) + product(rim_lifter, low))[0:60]
        left_over[:, outer] = left_over[:, outer] - late
        if i < ITERS - 1:
            field[0:60, outer] = field[0:60, outer] - scale_new * (late * inverse[:, outer])

    def nothing():
        pass

    def ids_middle():
        arrive(*ids_first)
        for a in range(PA):
            ids_mid[pl.ds(a, PD, stride=PA), :] = ids_one[a * PD : (a + 1) * PD, :]
        go(*ids_second)

    def answer():
        arrive(*ids_second)
        asked = jnp.transpose(ids_in[...])[0:RANKS].astype(jnp.int32)
        for rank in range(RANKS):
            hot_grid[:, rank * 128 : (rank + 1) * 128] = onehot(asked[rank : rank + 1], BLOCK, 128).astype(BF16)
        owned = jnp.concatenate(
            [normal_ref[...] * friction_ref[...], state_ref[...], shear_load[:, 0, :], shear_load[:, 1, :]], axis=0
        )
        high = owned.astype(BF16).astype(F32)
        both = product(jnp.concatenate([high, owned - high], axis=0).astype(BF16), hot_grid[...])
        for rank in range(RANKS):
            lanes = slice(rank * 128, (rank + 1) * 128)
            params_pack[rank * 48 : (rank + 1) * 48, :] = both[0:48, lanes] + both[48:96, lanes]
        for j in range(3):
            down_out[pl.ds(j, 128, stride=3), :] = jnp.transpose(params_pack[j * 128 : (j + 1) * 128, :])
        go(*down_first)
        for j in range(3):
            turned = jnp.transpose(params_pack[(3 + j) * 128 : (4 + j) * 128, :])
            for d in range(PD):
                over_out[pl.ds(d * 3 + j, PA, stride=48), :] = turned[d * PA : (d + 1) * PA]
        go(*over_first)

    def params_middle():
        arrive(*down_first)
        for d in range(PD):
            for j in range(3):
                down_mid[pl.ds(d * 3 + j, PA, stride=48), :] = down_one[pl.ds(d * 24 + j, PA, stride=3), :]
        go(*down_second)
        arrive(*over_first)
        for a in range(PA):
            for j in range(3):
                over_mid[pl.ds(a * 3 + j, PD, stride=24), :] = over_one[pl.ds(a * 48 + j, PD, stride=3), :]
        go(*over_second)

    pairs = coefficients()
    step(0, *pairs[0], 4, ids_middle, nothing)
    step(1, *pairs[1], 7, nothing, answer)
    step(2, *pairs[2], 7, nothing, nothing)
    step(3, *pairs[3], 0, params_middle, nothing)
    residual_ref[...] = left_over[...].reshape(60, 1, ELEMS)
    results[0].start()

    for p in range(SEND_SPLIT // 2):
        parts = []
        for s in (2 * p, 2 * p + 1):
            f, j = s // 8, s % 8
            parts.append(flux_sum[f * ROWS : (f + 1) * ROWS, j * 128 : (j + 1) * 128])
        high, low = halves(jnp.concatenate(parts, axis=0))
        table_send[p * 80 : p * 80 + 80, 0:128] = high
        table_send[p * 80 : p * 80 + 80, 128:256] = low
    for b in range(4):
        high = jnp.concatenate([send_maps[4 * b + j : 4 * b + j + 1, :] for j in range(4)], axis=1)
        low = jnp.concatenate([send_maps[16 + 4 * b + j : 17 + 4 * b + j, :] for j in range(4)], axis=1)
        hot = onehot(low.astype(jnp.int32), 128, BLOCK).astype(BF16)
        hot_send[0:128, :] = hot
        hot_send[128:256, :] = hot
        result = product(table_send[0 : SEND_SPLIT * ROWS, :], hot_send[...])
        chunk = high.astype(jnp.int32)
        total = choose(result, chunk, SEND_SPLIT, ROWS)
        tractions[b] = lane_gather(total, flux_sum, chunk, low.astype(jnp.int32), range(SEND_SPLIT, 32), ROWS)

    rate_pack[...] = jnp.zeros_like(rate_pack)

    def solve(b):
        owned = jnp.concatenate([params[(4 * b + j) * 48 : (4 * b + j + 1) * 48, :] for j in range(4)], axis=1)
        traction = tractions[b]
        state = owned[12:24]
        strike = owned[24:36] + traction[0:12]
        updip = owned[36:48] + traction[12:24]
        magnitude = jnp.sqrt(strike * strike + updip * updip)
        resist = owned[0:12] * (1.0 + 0.5 * jnp.tanh(traction[24:36]))
        steep = resist * state
        velocity = magnitude / (DAMPING + steep)
        for _ in range(NEWTON - 1):
            scaled = state * velocity
            square = 1.0 + scaled * scaled
            inverse_root = lax.rsqrt(square)
            misfit = magnitude - DAMPING * velocity - resist * inverse_sinh(scaled, square * inverse_root)
            velocity = velocity + misfit / (DAMPING + steep * inverse_root)
        for j in range(4):
            rank = 4 * b + j
            rate_pack[rank * 16 : rank * 16 + 12, :] = velocity[:, j * 128 : (j + 1) * 128]
        return velocity, magnitude, strike, updip

    arrive(*down_second)
    for j in range(3):
        params[j * 128 : (j + 1) * 128, :] = jnp.transpose(down_in[pl.ds(j, 128, stride=3), :])
    arrive(*over_second)
    for j in range(3):
        parts = [over_in[pl.ds(a * 3 + j, PD, stride=24), :] for a in range(PA)]
        params[(3 + j) * 128 : (4 + j) * 128, :] = jnp.transpose(jnp.concatenate(parts, axis=0))
    motion = [solve(b) for b in range(4)]
    for j in range(2):
        rate_out[pl.ds(j, 128, stride=2), :] = jnp.transpose(rate_pack[j * 128 : (j + 1) * 128, :])
    go(*rate_first)

    for b, (velocity, magnitude, strike, updip) in enumerate(motion):
        factor = TIME_STEP * velocity / jnp.maximum(magnitude, 1.0)
        slip = jnp.concatenate([factor * strike, factor * updip], axis=0)
        for j in (0, 2):
            parts = [slip[:, j * 128 : (j + 1) * 128], slip[:, (j + 1) * 128 : (j + 2) * 128]]
            high, low = halves(jnp.concatenate(parts, axis=0))
            at = (4 * b + j) * 24
            table_back[at : at + 48, 0:128] = high
            table_back[at : at + 48, 128:256] = low

    def build_face(b, carry):
        low = jnp.concatenate([face_maps[pl.ds(32 + 4 * b + j, 1), :] for j in range(4)], axis=1)
        hot = onehot(low.astype(jnp.int32), 128, BLOCK).astype(BF16)
        hot_face[b, 0:128, :] = hot
        hot_face[b, 128:256, :] = hot
        return carry

    lax.fori_loop(0, 8, build_face, 0)
    flux[...] = jnp.zeros_like(flux)

    def place_back(b, carry):
        rank = jnp.concatenate([face_maps[pl.ds(4 * b + j, 1), :] for j in range(4)], axis=1)
        result = product(table_back[...], hot_face[b])
        f = b // 2
        half = b - 2 * f
        flux[
            pl.ds(pl.multiple_of(f * ROWS, 8), 24), pl.ds(pl.multiple_of(half * BLOCK, BLOCK), BLOCK)
        ] = choose(result, rank.astype(jnp.int32) - 1, RANKS, 24)
        return carry

    lax.fori_loop(0, 8, place_back, 0)

    arrive(*rate_first)
    for a in range(PA):
        for j in range(2):
            rate_mid[pl.ds(a * 2 + j, PD, stride=16), :] = rate_one[pl.ds(a * 32 + j, PD, stride=2), :]
    go(*rate_second)
    disp_ref[...] = (solved[...] + 0.5 * lifted(flux)[0:60]).reshape(60, 1, ELEMS)
    results[1].start()
    for each in (ids_first, ids_second, down_first, down_second, over_first, over_second, rate_first):
        drain(*each)
    for i in range(ITERS):
        for side, piece, target, sends, receives in sides:
            @pl.when(sends)
            def _():
                halo_copy(i, side, piece, target).wait_send()

    arrive(*rate_second)
    for j in range(2):
        value = jnp.transpose(rate_in[pl.ds(j, 128, stride=2), :])
        high = value.astype(BF16).astype(F32)
        low = value - high
        for r in range(8):
            lanes = slice((8 * j + r) * 128, (8 * j + r + 1) * 128)
            wide[0:16, lanes] = high[r * 16 : (r + 1) * 16]
            wide[16:32, lanes] = low[r * 16 : (r + 1) * 16]
    both = lax.dot_general(wide[...].astype(BF16), hot_grid[...], NT, preferred_element_type=F32)
    rate_ref[...] = both[0:12] + both[16:28]
    results[2].start()
    drain(*rate_second)
    for result in results:
        result.wait()


def hand_over(disp_ref, residual_ref, rate_ref, disp_out, residual_out, rate_out, disp, residual, rate, sems):
    ways = ((disp_ref, disp, disp_out), (residual_ref, residual, residual_out), (rate_ref, rate, rate_out))
    inward = [pltpu.make_async_copy(way[0], way[1], sems.at[0, i]) for i, way in enumerate(ways)]
    outward = [pltpu.make_async_copy(way[1], way[2], sems.at[1, i]) for i, way in enumerate(ways)]
    for copy in inward:
        copy.start()
    for first, second in zip(inward, outward):
        first.wait()
        second.start()
    for copy in outward:
        copy.wait()


def on_device(
    right_side,
    shear_modulus,
    lame_lambda,
    stiff_shear,
    stiff_lame,
    face_interp,
    neighbours,
    fault_count,
    fault_owner,
    fault_slot,
    fault_face,
    normal_stress,
    friction,
    state_factor,
    shear_load,
):
    vmem = pl.BlockSpec(memory_space=pltpu.VMEM)
    hbm = pl.BlockSpec(memory_space=pltpu.HBM)
    scratch = [
        pltpu.VMEM((60, 1, ELEMS), F32),
        pltpu.VMEM((60, 1, ELEMS), F32),
        pltpu.VMEM((12, 512), F32),
        pltpu.SemaphoreType.DMA((3,)),
        pltpu.VMEM((60, 1, ELEMS), F32),
        pltpu.VMEM((1, ELEMS), F32),
        pltpu.VMEM((1, ELEMS), F32),
        pltpu.VMEM((60, 60), F32),
        pltpu.VMEM((60, 60), F32),
        pltpu.VMEM((12, 4, 20), F32),
        pltpu.VMEM((8, 1, BLOCK), jnp.int32),
        pltpu.VMEM((16, 1, 128), jnp.int32),
        pltpu.VMEM((16, 1, 128), jnp.int32),
        pltpu.VMEM((16, 1, 128), jnp.int32),
        pltpu.VMEM((12, 512), F32),
        pltpu.VMEM((12, 512), F32),
        pltpu.VMEM((12, 512), F32),
        pltpu.VMEM((12, 2, 512), F32),
        pltpu.SemaphoreType.DMA((14,)),
        pltpu.VMEM((288, 128), F32),
        pltpu.VMEM((288, 256), F32),
        pltpu.VMEM((128, 256), F32),
        pltpu.VMEM((60, ELEMS), F32),
        pltpu.VMEM((60, ELEMS), F32),
        pltpu.VMEM((64, ELEMS), F32),
        pltpu.VMEM((192, ELEMS), BF16),
        pltpu.VMEM((160, ELEMS), F32),
        pltpu.VMEM((64, ELEMS), F32),
        pltpu.VMEM((160, ELEMS), F32),
        pltpu.VMEM((160, ELEMS), F32),
        pltpu.VMEM((160, ELEMS), F32),
        pltpu.VMEM((8, ELEMS), F32),
        pltpu.VMEM((CHUNKS * ROWS, 256), BF16),
        pltpu.VMEM((7, 256, BLOCK), BF16),
        pltpu.VMEM((2048, 128), BF16),
        pltpu.VMEM((2048, 256), F32),
        pltpu.VMEM((64, 128), F32),
        pltpu.VMEM((64, 128), F32),
        pltpu.VMEM((256, BLOCK), BF16),
        pltpu.VMEM((8, 256, BLOCK), BF16),
        pltpu.VMEM((32 * ROWS, 256), BF16),
        pltpu.VMEM((ITERS, 4, ROWS, 128), F32),
        pltpu.VMEM((ITERS, 4, ROWS, 128), F32),
        pltpu.VMEM((128, 128), F32),
        pltpu.VMEM((128, 128), F32),
        pltpu.VMEM((128, 128), F32),
        pltpu.VMEM((128, 128), F32),
        pltpu.VMEM((BLOCK, 2048), BF16),
        pltpu.VMEM((768, 128), F32),
        pltpu.VMEM((384, 128), F32),
        pltpu.VMEM((384, 128), F32),
        pltpu.VMEM((384, 128), F32),
        pltpu.VMEM((384, 128), F32),
        pltpu.VMEM((384, 128), F32),
        pltpu.VMEM((384, 128), F32),
        pltpu.VMEM((384, 128), F32),
        pltpu.VMEM((384, 128), F32),
        pltpu.VMEM((768, 128), F32),
        pltpu.VMEM((4, ROWS, BLOCK), F32),
        pltpu.VMEM((256, 128), F32),
        pltpu.VMEM((256, 128), F32),
        pltpu.VMEM((256, 128), F32),
        pltpu.VMEM((256, 128), F32),
        pltpu.VMEM((256, 128), F32),
        pltpu.VMEM((32, 2048), F32),
        pltpu.VMEM((384, 256), BF16),
        pltpu.SemaphoreType.DMA((ITERS, 4)),
        pltpu.SemaphoreType.DMA((ITERS, 4)),
    ] + [pltpu.SemaphoreType.DMA((PD,))] * 16
    displacement, residual, rate = pl.pallas_call(
        kernel,
        out_shape=(
            jax.ShapeDtypeStruct((60, 1, ELEMS), F32),
            jax.ShapeDtypeStruct((60, 1, ELEMS), F32),
            jax.ShapeDtypeStruct((12, 512), F32),
        ),
        in_specs=[vmem] + [hbm] * 14,
        out_specs=(hbm, hbm, hbm),
        scratch_shapes=scratch,
        compiler_params=pltpu.CompilerParams(collective_id=0, has_side_effects=True, vmem_limit_bytes=64000 * 1024),
        name="window",
    )(
        fault_count.reshape(1, 1),
        right_side.reshape(60, 1, ELEMS),
        shear_modulus.reshape(1, ELEMS),
        lame_lambda.reshape(1, ELEMS),
        stiff_shear,
        stiff_lame,
        face_interp,
        neighbours.reshape(8, 1, BLOCK),
        fault_owner.reshape(16, 1, 128),
        fault_slot.reshape(16, 1, 128),
        fault_face.reshape(16, 1, 128),
        normal_stress,
        friction,
        state_factor,
        shear_load.transpose(1, 0, 2),
    )
    displacement, residual, rate = pl.pallas_call(
        hand_over,
        out_shape=(
            jax.ShapeDtypeStruct((480, 128), F32),
            jax.ShapeDtypeStruct((480, 128), F32),
            jax.ShapeDtypeStruct((12, 512), F32),
        ),
        in_specs=[hbm] * 3,
        out_specs=(hbm, hbm, hbm),
        scratch_shapes=[
            pltpu.VMEM((480, 128), F32),
            pltpu.VMEM((480, 128), F32),
            pltpu.VMEM((12, 512), F32),
            pltpu.SemaphoreType.DMA((2, 3)),
        ],
        compiler_params=pltpu.CompilerParams(vmem_limit_bytes=64000 * 1024),
        name="hand_over",
    )(displacement.reshape(480, 128), residual.reshape(480, 128), rate)
    return displacement.reshape(right_side.shape), residual.reshape(right_side.shape), rate


def solution(mesh):
    in_specs = (
        P(None, None, "along", "depth", None),
        P("along", "depth", None),
        P("along", "depth", None),
        P(),
        P(),
        P(),
        P("along", "depth", None),
        P("along", "depth"),
        P("along", "depth", None),
        P("along", "depth", None),
        P("along", "depth", None),
        P(None, ("along", "depth")),
        P(None, ("along", "depth")),
        P(None, ("along", "depth")),
        P(None, None, ("along", "depth")),
    )
    out_specs = (
        P(None, None, "along", "depth", None),
        P(None, None, "along", "depth", None),
        P(None, ("along", "depth")),
    )
    return jax.shard_map(
        on_device, mesh=mesh, in_specs=in_specs, out_specs=out_specs, check_vma=False
    )
```

```python
import functools

import jax
import jax.numpy as jnp
from jax import lax
from jax.experimental import pallas as pl
from jax.experimental.pallas import tpu as pltpu
from jax.sharding import PartitionSpec as P

ITERS = 4
NEWTON = 6
DAMPING = 0.5
TIME_STEP = 0.5
LOWER_EDGE = 0.25
UPPER_EDGE = 5.0
CENTER = 0.5 * (UPPER_EDGE + LOWER_EDGE)
SPREAD = 0.5 * (UPPER_EDGE - LOWER_EDGE)

MESH = pl.DeviceIdType.MESH
F32 = jnp.float32
BF16 = jnp.bfloat16
NT = (((1,), (1,)), ((), ()))

PA, PD = 8, 16
DEVS = PA * PD
ELEMS = 1024
ROWS = 40
BLOCK = 512
CHUNKS = 28
SPLIT = 16
SEND_SPLIT = 20
FAR_ROW = (4, 3, 5, 2, 6, 1, 7)
FAR_COLUMN = (6, 10, 7, 9, 2, 14, 5, 11, 8, 3, 13, 1, 15, 4, 12)
RANKS = 16


def coefficients():
    ratio = CENTER / SPREAD
    rho = 1.0 / ratio
    pairs = []
    for _ in range(ITERS):
        rho_next = 1.0 / (2.0 * ratio - rho)
        pairs.append((rho_next * rho, 2.0 * rho_next / SPREAD))
        rho = rho_next
    return pairs


def halves(value):
    high = value.astype(BF16)
    return high, (value - high.astype(F32)).astype(BF16)


def product(left, right):
    return jnp.dot(left, right, preferred_element_type=F32)


def onehot(digit, rows, columns):
    return (lax.broadcasted_iota(jnp.int32, (rows, columns), 0) == digit).astype(F32)


def choose(result, chunk, count, rows):
    width = result.shape[1]
    index = jnp.broadcast_to(chunk, (8, width))
    total = jnp.zeros((rows // 8, 8, width), F32)
    for s in range(count):
        part = result[s * rows : (s + 1) * rows].reshape(rows // 8, 8, width)
        total = jnp.where((index == s)[None], part, total)
    return total.reshape(rows, width)


def lane_gather(total, rows_ref, chunk, lanes, chunks, rows):
    columns = []
    for q in range(4):
        part = slice(q * 128, (q + 1) * 128)
        low = jnp.broadcast_to(lanes[:, part], (8, 128))
        index = jnp.broadcast_to(chunk[:, part], (8, 128))
        groups = [total[8 * g : 8 * g + 8, part] for g in range(rows // 8)]
        for s in chunks:
            t = s if len(chunks) + chunks[0] == 32 or s < 24 else s + 4
            mine = index == s
            for g in range(rows // 8):
                at = t // 8 * ROWS + 8 * g
                source = rows_ref[at : at + 8, t % 8 * 128 : t % 8 * 128 + 128]
                groups[g] = jnp.where(mine, jnp.take_along_axis(source, low, axis=1), groups[g])
        columns.append(jnp.concatenate(groups, axis=0))
    return jnp.concatenate(columns, axis=1)


def inverse_sinh(size, root):
    magnitude = jnp.log(jnp.abs(size) + root)
    return jnp.where(size < 0.0, -magnitude, magnitude)


def kernel(
    count_ref, load_hbm, shear_hbm, lame_hbm, stiff_shear_hbm, stiff_lame_hbm, interp_hbm, links_hbm, owner_hbm,
    slot_hbm, face_hbm, normal_hbm, friction_hbm, state_hbm, shear_load_hbm,
    disp_hbm, residual_hbm, rate_hbm,
    disp_ref, residual_ref, rate_ref, result_sem,
    load, shear_ref, lame_ref, stiff_shear, stiff_lame, interp, links, owner_ref, slot_ref, face_ref,
    normal_ref, friction_ref, state_ref, shear_load, fetch_sem,
    weight, weights, lift_pair, solved, left_over, field, stacked, trace, image, gathered, flux, flux_sum, alpha,
    table, hot_links, hot_owner, prefix, send_maps, face_maps, hot_send, hot_face, table_send, halo, rims,
    ids_out, ids_one, ids_mid, ids_in, hot_grid, params_pack, down_out, down_one, down_mid, down_in, over_out,
    over_one, over_mid, over_in, params,
    tractions, rate_pack, rate_out, rate_one, rate_mid, rate_in, wide, table_back,
    halo_send, halo_recv, ids_a, ids_b, ids_c, ids_d, par_a, par_b, par_c, par_d, par_e, par_f, par_g, par_h,
    rate_a, rate_b, rate_c, rate_d,
):
    along = lax.axis_index("along")
    depth = lax.axis_index("depth")

    operands = (
        (owner_hbm, owner_ref), (slot_hbm, slot_ref), (face_hbm, face_ref), (load_hbm, load), (shear_hbm, shear_ref),
        (lame_hbm, lame_ref), (stiff_shear_hbm, stiff_shear), (stiff_lame_hbm, stiff_lame), (interp_hbm, interp),
        (links_hbm, links), (normal_hbm, normal_ref), (friction_hbm, friction_ref), (state_hbm, state_ref),
        (shear_load_hbm, shear_load),
    )
    fetches = [
        pltpu.make_async_copy(source, target, fetch_sem.at[i]) for i, (source, target) in enumerate(operands)
    ]
    for fetch in fetches[0:3]:
        fetch.start()

    results = [
        pltpu.make_async_copy(source, target, result_sem.at[i])
        for i, (source, target) in enumerate(
            ((residual_ref, residual_hbm), (disp_ref, disp_hbm), (rate_ref, rate_hbm))
        )
    ]

    barrier = pltpu.get_barrier_semaphore()
    for i in FAR_ROW:
        pl.semaphore_signal(barrier, inc=1, device_id=(lax.rem(along + i, PA), depth), device_id_type=MESH)
    for i in FAR_COLUMN:
        pl.semaphore_signal(barrier, inc=1, device_id=(along, lax.rem(depth + i, PD)), device_id_type=MESH)

    for fetch in fetches[3:]:
        fetch.start()

    def row_copy(i, source, landing, size, sems, sending):
        peer = lax.rem(along + i, PA) if sending else lax.rem(along + PA - i, PA)
        place = along if sending else peer
        return pltpu.make_async_remote_copy(
            src_ref=source.at[pl.ds(pl.multiple_of(peer * size, 8), size)],
            dst_ref=landing.at[pl.ds(pl.multiple_of(place * size, 8), size)],
            send_sem=sems[0].at[i],
            recv_sem=sems[1].at[i],
            device_id=(peer, depth),
            device_id_type=MESH,
        )

    def column_copy(i, source, landing, size, sems, sending):
        peer = lax.rem(depth + i, PD) if sending else lax.rem(depth + PD - i, PD)
        place = depth if sending else peer
        return pltpu.make_async_remote_copy(
            src_ref=source.at[pl.ds(pl.multiple_of(peer * size, 8), size)],
            dst_ref=landing.at[pl.ds(pl.multiple_of(place * size, 8), size)],
            send_sem=sems[0].at[i],
            recv_sem=sems[1].at[i],
            device_id=(along, peer),
            device_id_type=MESH,
        )

    def go(kind, source, landing, size, sems):
        mine, order = (along, FAR_ROW) if kind is row_copy else (depth, FAR_COLUMN)
        for i in order:
            kind(i, source, landing, size, sems, True).start()
        own = pl.ds(pl.multiple_of(mine * size, 8), size)
        landing[own, :] = source[own, :]

    def arrive(kind, source, landing, size, sems):
        for i in range(1, PA if kind is row_copy else PD):
            kind(i, source, landing, size, sems, False).wait_recv()

    def drain(kind, source, landing, size, sems):
        for i in range(1, PA if kind is row_copy else PD):
            kind(i, source, landing, size, sems, True).wait_send()

    ids_first = (row_copy, ids_out, ids_one, 16, (ids_a, ids_b))
    ids_second = (column_copy, ids_mid, ids_in, 8, (ids_c, ids_d))
    down_first = (column_copy, down_out, down_one, 24, (par_a, par_b))
    down_second = (row_copy, down_mid, down_in, 48, (par_c, par_d))
    over_first = (row_copy, over_out, over_one, 48, (par_e, par_f))
    over_second = (column_copy, over_mid, over_in, 24, (par_g, par_h))
    rate_first = (row_copy, rate_out, rate_one, 32, (rate_a, rate_b))
    rate_second = (column_copy, rate_mid, rate_in, 16, (rate_c, rate_d))

    for fetch in fetches[0:3]:
        fetch.wait()
    count = count_ref[...]
    lane = lax.broadcasted_iota(jnp.int32, (1, 128), 1)
    for t in range(RANKS):
        live = (lane + t * 128) < count
        owner = jnp.where(live, owner_ref[t], -1)
        hot_owner[t * 128 : (t + 1) * 128, :] = onehot(owner, 128, 128).astype(BF16)
    row = lax.broadcasted_iota(jnp.int32, (128, 256), 0)
    column = lax.broadcasted_iota(jnp.int32, (128, 256), 1)
    earlier = ((row < column) | (column >= 128)).astype(F32).astype(BF16)
    prefix[...] = product(hot_owner[...], earlier)
    base = jnp.zeros((128, 128), F32)
    sent = jnp.zeros((64, 128), F32)
    ranked = []
    for t in range(RANKS):
        rows = slice(t * 128, (t + 1) * 128)
        hot = hot_owner[rows, :]
        rank = jnp.sum(hot.astype(F32) * (prefix[rows, 0:128] + base), axis=0, keepdims=True)
        base = base + prefix[rows, 128:256]
        live = ((lane + t * 128) < count).astype(F32)
        rank_live = jnp.where(live > 0.0, rank, -1.0).astype(jnp.int32)
        face = face_ref[t]
        slot = slot_ref[t]
        face_high = lax.shift_right_logical(face, 7)
        face_low = jnp.bitwise_and(face, 127)
        ranks = onehot(rank_live, RANKS, 128)
        values = jnp.concatenate(
            [
                ranks * face_high.astype(F32),
                ranks * face_low.astype(F32),
                ranks * (lax.shift_right_logical(slot, 4) + 1).astype(F32),
                ranks * jnp.bitwise_and(slot, 15).astype(F32),
            ],
            axis=0,
        ).astype(BF16)
        sent = sent + lax.dot_general(values, hot, NT, preferred_element_type=F32)
        ranked.append((rank, live))
    send_maps[...] = sent
    ids = 16.0 * sent[32:48] + sent[48:64] - 16.0
    ids_out[...] = jnp.transpose(jnp.concatenate([ids, jnp.zeros((112, 128), F32)], axis=0))

    pl.semaphore_wait(barrier, PA + PD - 2)
    go(*ids_first)

    placed = jnp.zeros((64, 128), F32)
    for t in range(RANKS):
        rank, live = ranked[t]
        face = face_ref[t]
        highs = onehot(lax.shift_right_logical(face, 7), 32, 128) * live
        values = jnp.concatenate([highs * (rank + 1.0), highs * owner_ref[t].astype(F32)], axis=0).astype(BF16)
        lows = onehot(jnp.bitwise_and(face, 127), 128, 128).astype(BF16)
        placed = placed + lax.dot_general(values, lows, NT, preferred_element_type=F32)
    face_maps[...] = placed

    sides = (
        (0, 1, (along + 1, depth), along < PA - 1, along > 0),
        (1, 0, (along - 1, depth), along > 0, along < PA - 1),
        (2, 3, (along, depth + 1), depth < PD - 1, depth > 0),
        (3, 2, (along, depth - 1), depth > 0, depth < PD - 1),
    )

    for side, piece, target, sends, receives in sides:
        @pl.when(jnp.logical_not(receives))
        def _():
            halo[:, side] = jnp.zeros((ITERS, ROWS, 128), F32)

    for fetch in fetches[3:]:
        fetch.wait()
    weight[...] = jnp.zeros_like(weight)
    for f in range(4):
        for c in range(3):
            weight[f * ROWS + c * 12 : f * ROWS + c * 12 + 12, c * 20 : c * 20 + 20] = interp[:, f, :]
    weight[160:220, 0:60] = stiff_shear[...]
    weight[224:284, 0:60] = stiff_lame[...]
    whole = weight[:, 0:64]
    high = whole.astype(BF16).astype(F32)
    rest = whole - high
    lift_pair[0:128, 0:128] = jnp.transpose(weight[0:128, :])
    lift_pair[0:128, 128:256] = jnp.transpose(weight[128:256, :])
    weights[:, 0:64] = high
    weights[:, 64:128] = high
    weights[:, 128:192] = rest
    lifter, lifter_rest = halves(lift_pair[0:64, 0:160])
    matrix = weights[:, 0:192].astype(BF16)
    rim_matrix = weights[120:160, 0:192].astype(BF16)
    rim_lifter, rim_rest = halves(lift_pair[0:64, 120:160])

    shear = shear_ref[...]
    lame = lame_ref[...]
    material = lame + 2.0 * shear
    inverse = 1.0 / material

    def lifted(ref):
        high, low = halves(ref[...])
        return product(lifter, high) + product(lifter_rest, high) + product(lifter, low)

    def build_links(b, carry):
        slots = links[b + b // 6]
        hot = onehot(jnp.bitwise_and(slots, 127), 128, BLOCK).astype(BF16)
        hot_links[b, 0:128, :] = hot
        hot_links[b, 128:256, :] = hot
        return carry

    right = load[...].reshape(60, ELEMS)
    left_over[...] = right
    field[60:64, :] = jnp.zeros((4, ELEMS), F32)
    field[0:60, :] = right * (inverse * (1.0 / CENTER))
    solved[...] = jnp.zeros_like(solved)
    flux_sum[...] = jnp.zeros_like(flux_sum)

    def halo_copy(i, side, piece, target):
        return pltpu.make_async_remote_copy(
            src_ref=rims.at[i, piece],
            dst_ref=halo.at[i, side],
            send_sem=halo_send.at[i, side],
            recv_sem=halo_recv.at[i, side],
            device_id=target,
            device_id_type=MESH,
        )

    def step(i, scale_old, scale_new, split, middle, between):
        first = i == 0
        now = field[...]
        high, low = halves(now)
        stacked[0:64, :] = high
        stacked[64:128, :] = low
        stacked[128:192, :] = high
        rim = product(rim_matrix, stacked[:, 0:BLOCK])
        for side, piece, target, sends, receives in sides:
            rims[i, piece] = rim[:, piece * 128 : piece * 128 + 128]
            if first:
                rims[i, piece, 36:37, :] = material[:, piece * 128 : piece * 128 + 128]

            @pl.when(sends)
            def _():
                halo_copy(i, side, piece, target).start()

        trace[...] = product(matrix[0:160], stacked[...])
        if first:
            for f in range(4):
                trace[f * ROWS + 36 : f * ROWS + 37, :] = material
        if first:
            lax.fori_loop(0, 7, build_links, 0)

        for p in range(SPLIT // 2):
            parts = []
            for s in (2 * p, 2 * p + 1):
                t = s if s < 24 else s + 4
                f, j = t // 8, t % 8
                parts.append(trace[f * ROWS : (f + 1) * ROWS, j * 128 : (j + 1) * 128])
            high, low = halves(jnp.concatenate(parts, axis=0))
            table[p * 80 : p * 80 + 80, 0:128] = high
            table[p * 80 : p * 80 + 80, 128:256] = low

        def block(b, carry):
            place = b + b // 6
            chunk = lax.shift_right_logical(links[place], 7)
            chunk = jnp.where(chunk >= 24, chunk - 4, chunk)
            result = product(table[0 : SPLIT * ROWS, :], hot_links[b])
            lanes = jnp.bitwise_and(links[place], 127)
            total = choose(result, chunk, SPLIT, ROWS)
            total = lane_gather(total, trace, chunk, lanes, range(SPLIT, CHUNKS), ROWS)
            f = place // 2
            half = place - 2 * f
            gathered[
                pl.ds(pl.multiple_of(f * ROWS, 8), ROWS), pl.ds(pl.multiple_of(half * BLOCK, BLOCK), BLOCK)
            ] = total
            return carry

        lax.fori_loop(0, split, block, 0)
        middle()
        if split < 7:
            lax.fori_loop(split, 7, block, 0)

        volume = product(matrix[160:288], stacked[...])
        image[...] = shear * volume[0:64] + lame * volume[64:128]
        solved[...] = solved[...] + now[0:60]

        inner = slice(BLOCK, ELEMS)
        outer = slice(0, BLOCK)
        if first:
            for f in range(3):
                alpha[f : f + 1, :] = 0.5 * (material + gathered[f * ROWS + 36 : f * ROWS + 37, :])
            alpha[3:4, inner] = 0.5 * (material[:, inner] + gathered[156:157, inner])
        for f in range(4):
            rows = slice(f * ROWS, (f + 1) * ROWS)
            columns = slice(0, ELEMS) if f < 3 else inner
            value = alpha[f : f + 1, columns] * (trace[rows, columns] - gathered[rows, columns])
            flux[rows, columns] = value
            flux_sum[rows, columns] = flux_sum[rows, columns] + value
        flux[120:160, outer] = jnp.zeros((ROWS, BLOCK), F32)
        left = left_over[...] - (image[...] + lifted(flux))[0:60]
        left_over[...] = left
        if i < ITERS - 1:
            field[0:60, :] = scale_old * now[0:60] + scale_new * (left * inverse)
        between()

        for side, piece, target, sends, receives in sides:
            @pl.when(receives)
            def _():
                halo_copy(i, side, piece, target).wait_recv()
        arrived = jnp.concatenate([halo[i, side] for side in range(4)], axis=1)
        if first:
            alpha[3:4, outer] = 0.5 * (material[:, outer] + arrived[36:37])
        value = alpha[3:4, outer] * (trace[120:160, outer] - arrived)
        flux_sum[120:160, outer] = flux_sum[120:160, outer] + value
        high, low = halves(value)
        late = (product(rim_lifter, high) + product(rim_rest, high) + product(rim_lifter, low))[0:60]
        left_over[:, outer] = left_over[:, outer] - late
        if i < ITERS - 1:
            field[0:60, outer] = field[0:60, outer] - scale_new * (late * inverse[:, outer])

    def nothing():
        pass

    def ids_middle():
        arrive(*ids_first)
        for a in range(PA):
            ids_mid[pl.ds(a, PD, stride=PA), :] = ids_one[a * PD : (a + 1) * PD, :]
        go(*ids_second)

    def answer():
        arrive(*ids_second)
        asked = jnp.transpose(ids_in[...])[0:RANKS].astype(jnp.int32)
        for rank in range(RANKS):
            hot_grid[:, rank * 128 : (rank + 1) * 128] = onehot(asked[rank : rank + 1], BLOCK, 128).astype(BF16)
        owned = jnp.concatenate(
            [normal_ref[...] * friction_ref[...], state_ref[...], shear_load[:, 0, :], shear_load[:, 1, :]], axis=0
        )
        high = owned.astype(BF16).astype(F32)
        both = product(jnp.concatenate([high, owned - high], axis=0).astype(BF16), hot_grid[...])
        for rank in range(RANKS):
            lanes = slice(rank * 128, (rank + 1) * 128)
            params_pack[rank * 48 : (rank + 1) * 48, :] = both[0:48, lanes] + both[48:96, lanes]
        for j in range(3):
            down_out[pl.ds(j, 128, stride=3), :] = jnp.transpose(params_pack[j * 128 : (j + 1) * 128, :])
        go(*down_first)
        for j in range(3):
            turned = jnp.transpose(params_pack[(3 + j) * 128 : (4 + j) * 128, :])
            for d in range(PD):
                over_out[pl.ds(d * 3 + j, PA, stride=48), :] = turned[d * PA : (d + 1) * PA]
        go(*over_first)

    def params_middle():
        arrive(*down_first)
        for d in range(PD):
            for j in range(3):
                down_mid[pl.ds(d * 3 + j, PA, stride=48), :] = down_one[pl.ds(d * 24 + j, PA, stride=3), :]
        go(*down_second)
        arrive(*over_first)
        for a in range(PA):
            for j in range(3):
                over_mid[pl.ds(a * 3 + j, PD, stride=24), :] = over_one[pl.ds(a * 48 + j, PD, stride=3), :]
        go(*over_second)

    pairs = coefficients()
    step(0, *pairs[0], 4, ids_middle, nothing)
    step(1, *pairs[1], 7, nothing, answer)
    step(2, *pairs[2], 7, nothing, nothing)
    step(3, *pairs[3], 0, params_middle, nothing)
    residual_ref[...] = left_over[...].reshape(60, 1, ELEMS)
    results[0].start()

    for p in range(SEND_SPLIT // 2):
        parts = []
        for s in (2 * p, 2 * p + 1):
            f, j = s // 8, s % 8
            parts.append(flux_sum[f * ROWS : (f + 1) * ROWS, j * 128 : (j + 1) * 128])
        high, low = halves(jnp.concatenate(parts, axis=0))
        table_send[p * 80 : p * 80 + 80, 0:128] = high
        table_send[p * 80 : p * 80 + 80, 128:256] = low
    for b in range(4):
        high = jnp.concatenate([send_maps[4 * b + j : 4 * b + j + 1, :] for j in range(4)], axis=1)
        low = jnp.concatenate([send_maps[16 + 4 * b + j : 17 + 4 * b + j, :] for j in range(4)], axis=1)
        hot = onehot(low.astype(jnp.int32), 128, BLOCK).astype(BF16)
        hot_send[0:128, :] = hot
        hot_send[128:256, :] = hot
        result = product(table_send[0 : SEND_SPLIT * ROWS, :], hot_send[...])
        chunk = high.astype(jnp.int32)
        total = choose(result, chunk, SEND_SPLIT, ROWS)
        tractions[b] = lane_gather(total, flux_sum, chunk, low.astype(jnp.int32), range(SEND_SPLIT, 32), ROWS)

    rate_pack[...] = jnp.zeros_like(rate_pack)

    def solve(b):
        owned = jnp.concatenate([params[(4 * b + j) * 48 : (4 * b + j + 1) * 48, :] for j in range(4)], axis=1)
        traction = tractions[b]
        state = owned[12:24]
        strike = owned[24:36] + traction[0:12]
        updip = owned[36:48] + traction[12:24]
        magnitude = jnp.sqrt(strike * strike + updip * updip)
        resist = owned[0:12] * (1.0 + 0.5 * jnp.tanh(traction[24:36]))
        steep = resist * state
        velocity = magnitude / (DAMPING + steep)
        for _ in range(NEWTON - 1):
            scaled = state * velocity
            square = 1.0 + scaled * scaled
            inverse_root = lax.rsqrt(square)
            misfit = magnitude - DAMPING * velocity - resist * inverse_sinh(scaled, square * inverse_root)
            velocity = velocity + misfit / (DAMPING + steep * inverse_root)
        for j in range(4):
            rank = 4 * b + j
            rate_pack[rank * 16 : rank * 16 + 12, :] = velocity[:, j * 128 : (j + 1) * 128]
        return velocity, magnitude, strike, updip

    arrive(*down_second)
    for j in range(3):
        params[j * 128 : (j + 1) * 128, :] = jnp.transpose(down_in[pl.ds(j, 128, stride=3), :])
    arrive(*over_second)
    for j in range(3):
        parts = [over_in[pl.ds(a * 3 + j, PD, stride=24), :] for a in range(PA)]
        params[(3 + j) * 128 : (4 + j) * 128, :] = jnp.transpose(jnp.concatenate(parts, axis=0))
    motion = [solve(b) for b in range(4)]
    for j in range(2):
        rate_out[pl.ds(j, 128, stride=2), :] = jnp.transpose(rate_pack[j * 128 : (j + 1) * 128, :])
    go(*rate_first)

    for b, (velocity, magnitude, strike, updip) in enumerate(motion):
        factor = TIME_STEP * velocity / jnp.maximum(magnitude, 1.0)
        slip = jnp.concatenate([factor * strike, factor * updip], axis=0)
        for j in (0, 2):
            parts = [slip[:, j * 128 : (j + 1) * 128], slip[:, (j + 1) * 128 : (j + 2) * 128]]
            high, low = halves(jnp.concatenate(parts, axis=0))
            at = (4 * b + j) * 24
            table_back[at : at + 48, 0:128] = high
            table_back[at : at + 48, 128:256] = low

    def build_face(b, carry):
        low = jnp.concatenate([face_maps[pl.ds(32 + 4 * b + j, 1), :] for j in range(4)], axis=1)
        hot = onehot(low.astype(jnp.int32), 128, BLOCK).astype(BF16)
        hot_face[b, 0:128, :] = hot
        hot_face[b, 128:256, :] = hot
        return carry

    lax.fori_loop(0, 8, build_face, 0)
    flux[...] = jnp.zeros_like(flux)

    def place_back(b, carry):
        rank = jnp.concatenate([face_maps[pl.ds(4 * b + j, 1), :] for j in range(4)], axis=1)
        result = product(table_back[...], hot_face[b])
        f = b // 2
        half = b - 2 * f
        flux[
            pl.ds(pl.multiple_of(f * ROWS, 8), 24), pl.ds(pl.multiple_of(half * BLOCK, BLOCK), BLOCK)
        ] = choose(result, rank.astype(jnp.int32) - 1, RANKS, 24)
        return carry

    lax.fori_loop(0, 8, place_back, 0)

    arrive(*rate_first)
    for a in range(PA):
        for j in range(2):
            rate_mid[pl.ds(a * 2 + j, PD, stride=16), :] = rate_one[pl.ds(a * 32 + j, PD, stride=2), :]
    go(*rate_second)
    disp_ref[...] = (solved[...] + 0.5 * lifted(flux)[0:60]).reshape(60, 1, ELEMS)
    results[1].start()
    for each in (ids_first, ids_second, down_first, down_second, over_first, over_second, rate_first):
        drain(*each)
    for i in range(ITERS):
        for side, piece, target, sends, receives in sides:
            @pl.when(sends)
            def _():
                halo_copy(i, side, piece, target).wait_send()

    arrive(*rate_second)
    for j in range(2):
        value = jnp.transpose(rate_in[pl.ds(j, 128, stride=2), :])
        high = value.astype(BF16).astype(F32)
        low = value - high
        for r in range(8):
            lanes = slice((8 * j + r) * 128, (8 * j + r + 1) * 128)
            wide[0:16, lanes] = high[r * 16 : (r + 1) * 16]
            wide[16:32, lanes] = low[r * 16 : (r + 1) * 16]
    both = lax.dot_general(wide[...].astype(BF16), hot_grid[...], NT, preferred_element_type=F32)
    rate_ref[...] = both[0:12] + both[16:28]
    results[2].start()
    drain(*rate_second)
    for result in results:
        result.wait()


def hand_over(disp_ref, residual_ref, rate_ref, disp_out, residual_out, rate_out, disp, residual, rate, sems):
    ways = ((disp_ref, disp, disp_out), (residual_ref, residual, residual_out), (rate_ref, rate, rate_out))
    inward = [pltpu.make_async_copy(way[0], way[1], sems.at[0, i]) for i, way in enumerate(ways)]
    outward = [pltpu.make_async_copy(way[1], way[2], sems.at[1, i]) for i, way in enumerate(ways)]
    for copy in inward:
        copy.start()
    for first, second in zip(inward, outward):
        first.wait()
        second.start()
    for copy in outward:
        copy.wait()


def on_device(
    right_side,
    shear_modulus,
    lame_lambda,
    stiff_shear,
    stiff_lame,
    face_interp,
    neighbours,
    fault_count,
    fault_owner,
    fault_slot,
    fault_face,
    normal_stress,
    friction,
    state_factor,
    shear_load,
):
    vmem = pl.BlockSpec(memory_space=pltpu.VMEM)
    hbm = pl.BlockSpec(memory_space=pltpu.HBM)
    scratch = [
        pltpu.VMEM((60, 1, ELEMS), F32),
        pltpu.VMEM((60, 1, ELEMS), F32),
        pltpu.VMEM((12, 512), F32),
        pltpu.SemaphoreType.DMA((3,)),
        pltpu.VMEM((60, 1, ELEMS), F32),
        pltpu.VMEM((1, ELEMS), F32),
        pltpu.VMEM((1, ELEMS), F32),
        pltpu.VMEM((60, 60), F32),
        pltpu.VMEM((60, 60), F32),
        pltpu.VMEM((12, 4, 20), F32),
        pltpu.VMEM((8, 1, BLOCK), jnp.int32),
        pltpu.VMEM((16, 1, 128), jnp.int32),
        pltpu.VMEM((16, 1, 128), jnp.int32),
        pltpu.VMEM((16, 1, 128), jnp.int32),
        pltpu.VMEM((12, 512), F32),
        pltpu.VMEM((12, 512), F32),
        pltpu.VMEM((12, 512), F32),
        pltpu.VMEM((12, 2, 512), F32),
        pltpu.SemaphoreType.DMA((14,)),
        pltpu.VMEM((288, 128), F32),
        pltpu.VMEM((288, 256), F32),
        pltpu.VMEM((128, 256), F32),
        pltpu.VMEM((60, ELEMS), F32),
        pltpu.VMEM((60, ELEMS), F32),
        pltpu.VMEM((64, ELEMS), F32),
        pltpu.VMEM((192, ELEMS), BF16),
        pltpu.VMEM((160, ELEMS), F32),
        pltpu.VMEM((64, ELEMS), F32),
        pltpu.VMEM((160, ELEMS), F32),
        pltpu.VMEM((160, ELEMS), F32),
        pltpu.VMEM((160, ELEMS), F32),
        pltpu.VMEM((8, ELEMS), F32),
        pltpu.VMEM((CHUNKS * ROWS, 256), BF16),
        pltpu.VMEM((7, 256, BLOCK), BF16),
        pltpu.VMEM((2048, 128), BF16),
        pltpu.VMEM((2048, 256), F32),
        pltpu.VMEM((64, 128), F32),
        pltpu.VMEM((64, 128), F32),
        pltpu.VMEM((256, BLOCK), BF16),
        pltpu.VMEM((8, 256, BLOCK), BF16),
        pltpu.VMEM((32 * ROWS, 256), BF16),
        pltpu.VMEM((ITERS, 4, ROWS, 128), F32),
        pltpu.VMEM((ITERS, 4, ROWS, 128), F32),
        pltpu.VMEM((128, 128), F32),
        pltpu.VMEM((128, 128), F32),
        pltpu.VMEM((128, 128), F32),
        pltpu.VMEM((128, 128), F32),
        pltpu.VMEM((BLOCK, 2048), BF16),
        pltpu.VMEM((768, 128), F32),
        pltpu.VMEM((384, 128), F32),
        pltpu.VMEM((384, 128), F32),
        pltpu.VMEM((384, 128), F32),
        pltpu.VMEM((384, 128), F32),
        pltpu.VMEM((384, 128), F32),
        pltpu.VMEM((384, 128), F32),
        pltpu.VMEM((384, 128), F32),
        pltpu.VMEM((384, 128), F32),
        pltpu.VMEM((768, 128), F32),
        pltpu.VMEM((4, ROWS, BLOCK), F32),
        pltpu.VMEM((256, 128), F32),
        pltpu.VMEM((256, 128), F32),
        pltpu.VMEM((256, 128), F32),
        pltpu.VMEM((256, 128), F32),
        pltpu.VMEM((256, 128), F32),
        pltpu.VMEM((32, 2048), F32),
        pltpu.VMEM((384, 256), BF16),
        pltpu.SemaphoreType.DMA((ITERS, 4)),
        pltpu.SemaphoreType.DMA((ITERS, 4)),
    ] + [pltpu.SemaphoreType.DMA((PD,))] * 16
    displacement, residual, rate = pl.pallas_call(
        kernel,
        out_shape=(
            jax.ShapeDtypeStruct((60, 1, ELEMS), F32),
            jax.ShapeDtypeStruct((60, 1, ELEMS), F32),
            jax.ShapeDtypeStruct((12, 512), F32),
        ),
        in_specs=[vmem] + [hbm] * 14,
        out_specs=(hbm, hbm, hbm),
        scratch_shapes=scratch,
        compiler_params=pltpu.CompilerParams(collective_id=0, has_side_effects=True, vmem_limit_bytes=64000 * 1024),
        name="window",
    )(
        fault_count.reshape(1, 1),
        right_side.reshape(60, 1, ELEMS),
        shear_modulus.reshape(1, ELEMS),
        lame_lambda.reshape(1, ELEMS),
        stiff_shear,
        stiff_lame,
        face_interp,
        neighbours.reshape(8, 1, BLOCK),
        fault_owner.reshape(16, 1, 128),
        fault_slot.reshape(16, 1, 128),
        fault_face.reshape(16, 1, 128),
        normal_stress,
        friction,
        state_factor,
        shear_load.transpose(1, 0, 2),
    )
    displacement, residual, rate = pl.pallas_call(
        hand_over,
        out_shape=(
            jax.ShapeDtypeStruct((480, 128), F32),
            jax.ShapeDtypeStruct((480, 128), F32),
            jax.ShapeDtypeStruct((12, 512), F32),
        ),
        in_specs=[hbm] * 3,
        out_specs=(hbm, hbm, hbm),
        scratch_shapes=[
            pltpu.VMEM((480, 128), F32),
            pltpu.VMEM((480, 128), F32),
            pltpu.VMEM((12, 512), F32),
            pltpu.SemaphoreType.DMA((2, 3)),
        ],
        compiler_params=pltpu.CompilerParams(vmem_limit_bytes=64000 * 1024),
        name="hand_over",
    )(displacement.reshape(480, 128), residual.reshape(480, 128), rate)
    return displacement.reshape(right_side.shape), residual.reshape(right_side.shape), rate


def solution(mesh):
    in_specs = (
        P(None, None, "along", "depth", None),
        P("along", "depth", None),
        P("along", "depth", None),
        P(),
        P(),
        P(),
        P("along", "depth", None),
        P("along", "depth"),
        P("along", "depth", None),
        P("along", "depth", None),
        P("along", "depth", None),
        P(None, ("along", "depth")),
        P(None, ("along", "depth")),
        P(None, ("along", "depth")),
        P(None, None, ("along", "depth")),
    )
    out_specs = (
        P(None, None, "along", "depth", None),
        P(None, None, "along", "depth", None),
        P(None, ("along", "depth")),
    )
    return jax.shard_map(
        on_device, mesh=mesh, in_specs=in_specs, out_specs=out_specs, check_vma=False
    )
```
